32 devices in a mesh: section: 2 (over y), dp: 16 (over z, x, core).
Axes of the slice: x: 2, y: 2, z: 4, core: 2. Of those that a mesh axis runs over, the one named last changes fastest.
Arguments:
- boundary: bfloat16 [2, 2, 2048, 960], P('section', None, 'dp'), may hold values from -6 to 6
- doc_lens: int32 [2, 16, 4], P(None, 'dp'), may hold values from 0 to 128, as said below
- w_query: bfloat16 [2, 921600], P('section', 'dp'), may hold values from -0.1875 to 0.1875
- w_key: bfloat16 [2, 307200], P('section', 'dp'), may hold values from -0.1875 to 0.1875
- w_value: bfloat16 [2, 307200], P('section', 'dp'), may hold values from -0.1875 to 0.1875
- w_out: bfloat16 [2, 921600], P('section', 'dp'), may hold values from -0.75 to 0.75
- gains: bfloat16 [2, 1920], P('section', 'dp'), may hold values from 0.5 to 1.5
- w_gate: bfloat16 [2, 2457600], P('section', 'dp'), may hold values from -0.1875 to 0.1875
- w_up: bfloat16 [2, 2457600], P('section', 'dp'), may hold values from -0.1875 to 0.1875
- w_down: bfloat16 [2, 2457600], P('section', 'dp'), may hold values from -0.125 to 0.125
Outputs:
- boundary_out: float32 [2, 2, 2048, 960], P('section', None, 'dp')
- grad_query: float32 [2, 921600], P('section', 'dp')
- grad_key: float32 [2, 307200], P('section', 'dp')
- grad_value: float32 [2, 307200], P('section', 'dp')
- grad_out: float32 [2, 921600], P('section', 'dp')
- grad_gains: float32 [2, 1920], P('section', 'dp')
- grad_gate: float32 [2, 2457600], P('section', 'dp')
- grad_up: float32 [2, 2457600], P('section', 'dp')
- grad_down: float32 [2, 2457600], P('section', 'dp')
The draws below stay inside these ranges and needn't reach their ends.
Inputs may be any that keep to these rules, and one draw needn't show every extreme that they name: `doc_lens`: in each micro-batch and group of 128 slots the 4 lengths sum to at most 128; documents fill the slots from the first in order and the rest is padding. In every micro-batch one group holds a single document of 128.
All inputs are finite; a program needn't handle non-finite values.
Results may differ from the reference program's by a relative error of at most 0.02.
Values may be sent and summed in bfloat16 or wider, within the bound.
A program may use at most 256 MiB of HBM per device.

```python
import jax
import jax.numpy as jnp
from jax import lax

D = 960
HEADS = 15
KV_HEADS = 5
HEAD = 64
FF = 2560
CAP = 128
MB = 2
NDOC = 4
TOKENS = 2048
N_SECTION = 2


def draw_doc_lens(key, part):
    key = jax.random.fold_in(key, 17)
    group_total = TOKENS // CAP
    key_total, key_cut, key_full = jax.random.split(key, 3)
    totals = jax.random.randint(key_total, (MB, group_total, 1), CAP // 4, CAP + 1, dtype=jnp.int32)
    cut_points = jax.random.randint(key_cut, (MB, group_total, NDOC - 1), 0, CAP + 1, dtype=jnp.int32)
    cut_points = jnp.sort(jnp.minimum(cut_points, totals), axis=-1)
    edge_points = jnp.concatenate([jnp.zeros((MB, group_total, 1), jnp.int32), cut_points, totals], axis=-1)
    lengths = edge_points[..., 1:] - edge_points[..., :-1]
    full_group = jax.random.randint(key_full, (MB, 1), 0, group_total, dtype=jnp.int32)
    chosen = jnp.arange(group_total, dtype=jnp.int32)[None, :] == full_group
    single_doc = jnp.concatenate([jnp.full((1, 1, 1), CAP, jnp.int32), jnp.zeros((1, 1, NDOC - 1), jnp.int32)], axis=-1)
    return jnp.where(chosen[..., None], single_doc, lengths).astype(jnp.int32)


def steps_of(key, dims, cuts, low, largest):
    factor_of, own = 1.0, jax.random.fold_in(key, 6)
    for axis_at, blocks in cuts:
        steps = jnp.exp(jax.random.uniform(jax.random.fold_in(own, axis_at), (blocks,), jnp.float32, low / len(cuts), largest / len(cuts)))
        factor_of = factor_of * jnp.repeat(steps, dims[axis_at] // blocks).reshape([-1 if axis == axis_at else 1 for axis in range(len(dims))])
    return factor_of


def bell_draw(rng, shape, deviation, most, cuts=(), kind=jnp.bfloat16):
    array = deviation * jax.random.normal(rng, shape, jnp.float32)
    if cuts:
        array = array * steps_of(rng, shape, cuts, -0.22, 0.18)
    return jnp.clip(array, -most, most).astype(kind)


def setup_inputs(seed: int = 0) -> dict:
    keys = jax.random.split(jax.random.key(seed), 11)
    boundary = bell_draw(keys[0], (N_SECTION, MB, TOKENS, D), 1.0, 6.0, ((0, 2), (2, 16)))
    doc_lens = draw_doc_lens(jax.random.fold_in(keys[10], 71), 0)
    w_query = bell_draw(keys[2], (N_SECTION, D * D), D ** -0.5, 0.1875, ((0, 2), (1, 16)))
    w_key = bell_draw(keys[3], (N_SECTION, D * KV_HEADS * HEAD), D ** -0.5, 0.1875, ((0, 2), (1, 16)))
    w_value = bell_draw(keys[4], (N_SECTION, D * KV_HEADS * HEAD), D ** -0.5, 0.1875, ((0, 2), (1, 16)))
    w_out = bell_draw(keys[5], (N_SECTION, D * D), (D // 16) ** -0.5, 0.75, ((0, 2), (1, 16)))
    gains = jnp.clip(1.0 + 0.1 * jax.random.normal(keys[6], (N_SECTION, 2 * D), jnp.float32), 0.5, 1.5).astype(jnp.bfloat16)
    w_gate = bell_draw(keys[7], (N_SECTION, D * FF), D ** -0.5, 0.1875, ((0, 2), (1, 16)))
    w_up = bell_draw(keys[8], (N_SECTION, D * FF), D ** -0.5, 0.1875, ((0, 2), (1, 16)))
    w_down = bell_draw(keys[9], (N_SECTION, FF * D), FF ** -0.5, 0.125, ((0, 2), (1, 16)))
    return {"boundary": boundary, "doc_lens": doc_lens, "w_query": w_query, "w_key": w_key, "w_value": w_value, "w_out": w_out, "gains": gains, "w_gate": w_gate, "w_up": w_up, "w_down": w_down}


EPSILON = 1e-05
ROPE_BASE = 100000.0
PRECISE = lax.Precision.HIGHEST

@jax.custom_vjp
def low(v):
    return lax.optimization_barrier(v.astype(jnp.bfloat16)).astype(jnp.float32)

@jax.custom_vjp
def low_back(v):
    return v

def low_keep(v):
    return (low(v), None)

def low_pass(kept, grad):
    return (grad,)

def back_keep(v):
    return (v, None)

def back_low(kept, grad):
    return (low(grad),)
low.defvjp(low_keep, low_pass)
low_back.defvjp(back_keep, back_low)

def matmul(left, right):
    return jnp.dot(left, right, precision=PRECISE)

def doc_layout(lengths, slot_count):
    doc_ends = jnp.cumsum(lengths, dtype=jnp.int32)
    doc_starts = doc_ends - lengths
    doc_count = lengths.shape[0]
    slot_ids = jnp.arange(slot_count, dtype=jnp.int32)
    segment = lax.optimization_barrier(jnp.sum((slot_ids[:, None] >= doc_ends[None, :]).astype(jnp.int32), axis=1, dtype=jnp.int32))
    start_table = jnp.concatenate([doc_starts, doc_ends[doc_count - 1:]])
    picked = segment[:, None] == jnp.arange(doc_count + 1, dtype=jnp.int32)[None, :]
    first_slot = lax.optimization_barrier(jnp.sum(jnp.where(picked, start_table[None, :], 0), axis=1, dtype=jnp.int32))
    return (segment, slot_ids - first_slot, segment < doc_count)

def rope_tables(position):
    half_width = HEAD // 2
    inverse_freq = ROPE_BASE ** (-(jnp.arange(half_width, dtype=jnp.float32) * (2.0 / HEAD)))
    angles = position.astype(jnp.float32)[:, None] * inverse_freq[None, :]
    cos_table = jnp.cos(angles)
    sine_table = jnp.sin(angles)
    return (jnp.concatenate([cos_table, cos_table], axis=1), jnp.concatenate([sine_table, sine_table], axis=1))

def rotate(values, cos_table, sine_table):
    half_width = values.shape[-1] // 2
    turned = jnp.concatenate([-values[..., half_width:], values[..., :half_width]], axis=-1)
    return values * cos_table[:, None, :] + turned * sine_table[:, None, :]

def unpack(flat_weights, section_number):
    kv_width = KV_HEADS * HEAD
    return (flat_weights[0][section_number].reshape(D, D), flat_weights[1][section_number].reshape(D, kv_width), flat_weights[2][section_number].reshape(D, kv_width), flat_weights[3][section_number].reshape(D, D), flat_weights[4][section_number], flat_weights[5][section_number].reshape(D, FF), flat_weights[6][section_number].reshape(D, FF), flat_weights[7][section_number].reshape(FF, D))

def block_layer(residual, matrices, allowed, cos_table, sine_table):
    w_query, w_key, w_value, w_out, gain_pair, w_gate, w_up, w_down = matrices
    row_count = residual.shape[0]
    group_size = HEADS // KV_HEADS
    score_scale = HEAD ** (-0.5)
    first_inverse_scale = lax.rsqrt(lax.optimization_barrier(jnp.mean(residual * residual, axis=1, keepdims=True)) + EPSILON)
    normed = low(residual * first_inverse_scale * gain_pair[:D])
    queries = low(rotate(low_back(matmul(normed, w_query)).reshape(row_count, HEADS, HEAD), cos_table, sine_table))
    keys_turned = low(rotate(low_back(matmul(normed, w_key)).reshape(row_count, KV_HEADS, HEAD), cos_table, sine_table))
    values_low = low(low_back(matmul(normed, w_value))).reshape(row_count, KV_HEADS, HEAD)
    scores = jnp.einsum('qkgd,tkd->kgqt', queries.reshape(row_count, KV_HEADS, group_size, HEAD), keys_turned, precision=PRECISE) * score_scale
    scores = jnp.where(allowed[None, None], low_back(scores), -1e+30)
    probability = low(jax.nn.softmax(scores, axis=-1))
    mixed_low = jnp.einsum('kgqt,tkd->qkgd', probability, values_low, precision=PRECISE).reshape(row_count, D)
    mixed_low = low(low_back(mixed_low))
    midway_hidden = residual + low_back(matmul(mixed_low, w_out))
    second_inverse_scale = lax.rsqrt(lax.optimization_barrier(jnp.mean(midway_hidden * midway_hidden, axis=1, keepdims=True)) + EPSILON)
    normed_two = low(midway_hidden * second_inverse_scale * gain_pair[D:])
    gate_pre = low_back(matmul(normed_two, w_gate))
    up_pre = low_back(matmul(normed_two, w_up))
    activation = low(jax.nn.silu(gate_pre) * up_pre)
    return midway_hidden + low_back(matmul(activation, w_down))

def reference(boundary, doc_lens, w_query, w_key, w_value, w_out, gains, w_gate, w_up, w_down):
    group_total = TOKENS // CAP
    group_count = MB * group_total
    flat_weights = tuple((member.astype(jnp.float32) for member in (w_query, w_key, w_value, w_out, gains, w_gate, w_up, w_down)))
    inputs = boundary[0].astype(jnp.float32).reshape(group_count, CAP, D)
    group_lengths = doc_lens.reshape(group_count, NDOC)
    slot_ids = jnp.arange(CAP, dtype=jnp.int32)
    causal = slot_ids[None, :] <= slot_ids[:, None]

    def forward(inputs, *flat_weights):
        section_mats = [unpack(flat_weights, section_number) for section_number in range(N_SECTION)]

        def one_group(operands):
            hidden_rows, lengths = operands
            segment, position, live_mask = doc_layout(lengths, CAP)
            allowed = causal & (segment[:, None] == segment[None, :])
            cos_table, sine_table = rope_tables(position)
            for section_number in range(N_SECTION):
                if section_number > 0:
                    hidden_rows = low(low_back(hidden_rows))
                hidden_rows = block_layer(hidden_rows, section_mats[section_number], allowed, cos_table, sine_table)
            return hidden_rows
        return lax.map(jax.checkpoint(one_group), (inputs, group_lengths))
    outputs, pullback = jax.vjp(forward, inputs, *flat_weights)
    live_mask = jax.vmap(lambda lengths: doc_layout(lengths, CAP)[2])(group_lengths)
    cotangent = boundary[N_SECTION - 1].astype(jnp.float32).reshape(group_count, CAP, D) * live_mask[..., None].astype(jnp.float32)
    gradients = pullback(cotangent)
    boundary_grads = jnp.stack([gradients[0].reshape(MB, TOKENS, D), outputs.reshape(MB, TOKENS, D)])
    return (boundary_grads, gradients[1], gradients[2], gradients[3], gradients[4], gradients[5], gradients[6], gradients[7], gradients[8])
```

```python
import functools

import jax
import jax.numpy as jnp
from jax import lax
from jax.experimental import pallas as pl
from jax.experimental.pallas import tpu as pltpu
from jax.sharding import PartitionSpec as P

HEAD = 64


EPSILON = 1e-05
ROPE_BASE = 100000.0


def passed_along(x, axis, by):
    devices = lax.axis_size(axis)
    pairs = [(i, i + by) for i in range(devices) if 0 <= i + by < devices]
    return lax.ppermute(x, axis, pairs)


def as_sent(x):
    return jax.tree.map(lambda a: a.astype(jnp.bfloat16) if a.dtype == jnp.float32 else a, x)


def doc_layout(lengths, slot_count):
    doc_ends = jnp.cumsum(lengths, dtype=jnp.int32)
    doc_starts = doc_ends - lengths
    doc_count = lengths.shape[0]
    slot_ids = jnp.arange(slot_count, dtype=jnp.int32)
    segment = jnp.sum(
        (slot_ids[:, None] >= doc_ends[None, :]).astype(jnp.int32), axis=1, dtype=jnp.int32
    )
    start_table = jnp.concatenate([doc_starts, doc_ends[doc_count - 1 :]])
    picked = segment[:, None] == jnp.arange(doc_count + 1, dtype=jnp.int32)[None, :]
    first_slot = jnp.sum(jnp.where(picked, start_table[None, :], 0), axis=1, dtype=jnp.int32)
    return (segment, slot_ids - first_slot, segment < doc_count)


def rope_tables(position):
    half_width = HEAD // 2
    inverse_freq = ROPE_BASE ** (-(jnp.arange(half_width, dtype=jnp.float32) * (2.0 / HEAD)))
    angles = position.astype(jnp.float32)[:, None] * inverse_freq[None, :]
    cos_table = jnp.cos(angles)
    sine_table = jnp.sin(angles)
    return (
        jnp.concatenate([cos_table, cos_table], axis=1),
        jnp.concatenate([sine_table, sine_table], axis=1),
    )


def rotate(values, cos_table, sine_table):
    half_width = values.shape[-1] // 2
    turned = jnp.concatenate([-values[..., half_width:], values[..., :half_width]], axis=-1)
    return values * cos_table[:, None, :] + turned * sine_table[:, None, :]


def unrotate(values, cos_table, sine_table):
    half_width = values.shape[-1] // 2
    sined = values * sine_table[:, None, :]
    turned = jnp.concatenate([sined[..., half_width:], -sined[..., :half_width]], axis=-1)
    return values * cos_table[:, None, :] + turned


def unpack(gathered, model_width):
    kv_width = gathered[1].size // model_width
    hidden_width = gathered[5].size // model_width
    return (
        gathered[0].reshape(model_width, model_width),
        gathered[1].reshape(model_width, kv_width),
        gathered[2].reshape(model_width, kv_width),
        gathered[3].reshape(model_width, model_width),
        gathered[4].reshape(2 * model_width),
        gathered[5].reshape(model_width, hidden_width),
        gathered[6].reshape(model_width, hidden_width),
        gathered[7].reshape(hidden_width, model_width),
    )


def add_sources(received):
    return tuple((jnp.sum(member, axis=0, keepdims=True) for member in received))


def forward_layer(layer_input_rows, matrices, allowed, cos_table, sine_table):
    w_query, w_key, w_value, w_out, gain_pair, w_gate, w_up, w_down = matrices
    row_count, model_width = layer_input_rows.shape
    kv_count = w_key.shape[1] // HEAD
    group_size = w_query.shape[1] // w_key.shape[1]
    score_scale = HEAD ** (-0.5)
    gain_one = gain_pair[:model_width].astype(jnp.float32)
    gain_two = gain_pair[model_width:].astype(jnp.float32)
    residual = layer_input_rows.astype(jnp.float32)
    first_inverse_scale = lax.rsqrt(jnp.mean(residual * residual, axis=1, keepdims=True) + EPSILON)
    normed = (residual * first_inverse_scale * gain_one).astype(jnp.bfloat16)
    queries = rotate(
        jnp.dot(normed, w_query, preferred_element_type=jnp.float32).reshape(row_count, -1, HEAD),
        cos_table,
        sine_table,
    ).astype(jnp.bfloat16)
    keys_turned = rotate(
        jnp.dot(normed, w_key, preferred_element_type=jnp.float32).reshape(
            row_count, kv_count, HEAD
        ),
        cos_table,
        sine_table,
    ).astype(jnp.bfloat16)
    values_low = jnp.dot(normed, w_value, preferred_element_type=jnp.float32).astype(jnp.bfloat16)
    heads_query = queries.reshape(row_count, kv_count, group_size, HEAD).transpose(1, 0, 2, 3)
    heads_key = keys_turned.transpose(1, 0, 2)
    heads_value = values_low.reshape(row_count, kv_count, HEAD).transpose(1, 0, 2)

    def one_head(operands):
        head_query, head_key, head_value = operands
        scores = (
            jnp.einsum("qgd,td->gqt", head_query, head_key, preferred_element_type=jnp.float32)
            * score_scale
        )
        scores = jnp.where(allowed[None], scores, -1e30)
        row_top = jnp.max(scores, axis=2, keepdims=True)
        exponent = jnp.exp(scores - row_top)
        row_total = jnp.sum(exponent, axis=2, keepdims=True)
        probability = (exponent / row_total).astype(jnp.bfloat16)
        attended = jnp.einsum(
            "gqt,td->qgd", probability, head_value, preferred_element_type=jnp.float32
        )
        return (attended, (row_top + jnp.log(row_total))[..., 0])

    attended, log_total = lax.map(one_head, (heads_query, heads_key, heads_value))
    mixed_low = attended.transpose(1, 0, 2, 3).reshape(row_count, model_width).astype(jnp.bfloat16)
    midway_hidden = residual + jnp.dot(mixed_low, w_out, preferred_element_type=jnp.float32)
    second_inverse_scale = lax.rsqrt(
        jnp.mean(midway_hidden * midway_hidden, axis=1, keepdims=True) + EPSILON
    )
    normed_two = (midway_hidden * second_inverse_scale * gain_two).astype(jnp.bfloat16)
    gate_pre = jnp.dot(normed_two, w_gate, preferred_element_type=jnp.float32)
    up_pre = jnp.dot(normed_two, w_up, preferred_element_type=jnp.float32)
    activation = (jax.nn.silu(gate_pre) * up_pre).astype(jnp.bfloat16)
    layer_out = midway_hidden + jnp.dot(activation, w_down, preferred_element_type=jnp.float32)
    kept_values = (
        layer_input_rows,
        normed,
        queries,
        keys_turned,
        values_low,
        log_total,
        mixed_low,
        midway_hidden,
        first_inverse_scale,
        second_inverse_scale,
        normed_two,
        gate_pre,
        up_pre,
        activation,
    )
    return (layer_out, kept_values)


def backward_layer(kept_values, matrices, allowed, cos_table, sine_table, grad_output, piece_count):
    (
        layer_input_rows,
        normed,
        queries,
        keys_turned,
        values_low,
        log_total,
        mixed_low,
        midway_hidden,
        first_inverse_scale,
        second_inverse_scale,
        normed_two,
        gate_pre,
        up_pre,
        activation,
    ) = kept_values
    w_query, w_key, w_value, w_out, gain_pair, w_gate, w_up, w_down = matrices
    row_count, model_width = layer_input_rows.shape
    kv_count = w_key.shape[1] // HEAD
    group_size = w_query.shape[1] // w_key.shape[1]
    score_scale = HEAD ** (-0.5)
    gain_one = gain_pair[:model_width].astype(jnp.float32)
    gain_two = gain_pair[model_width:].astype(jnp.float32)
    grad_low = grad_output.astype(jnp.bfloat16)
    grad_wdown = jnp.einsum("nf,nd->fd", activation, grad_low, preferred_element_type=jnp.float32)
    grad_act = jnp.einsum("nd,fd->nf", grad_low, w_down, preferred_element_type=jnp.float32)
    sigmoid_gate = jax.nn.sigmoid(gate_pre)
    grad_gate_pre = (
        grad_act * up_pre * sigmoid_gate * (1.0 + gate_pre * (1.0 - sigmoid_gate))
    ).astype(jnp.bfloat16)
    grad_up_pre = (grad_act * gate_pre * sigmoid_gate).astype(jnp.bfloat16)
    grad_wgate = jnp.einsum(
        "nd,nf->df", normed_two, grad_gate_pre, preferred_element_type=jnp.float32
    )
    grad_wup = jnp.einsum("nd,nf->df", normed_two, grad_up_pre, preferred_element_type=jnp.float32)
    second_norm_gradient = jnp.einsum(
        "nf,df->nd", grad_gate_pre, w_gate, preferred_element_type=jnp.float32
    ) + jnp.einsum("nf,df->nd", grad_up_pre, w_up, preferred_element_type=jnp.float32)
    second_centered_input = midway_hidden * second_inverse_scale
    second_normalized_rows = second_norm_gradient * gain_two
    second_gain_gradient = jnp.sum(second_norm_gradient * second_centered_input, axis=0)
    grad_middle = grad_output + second_inverse_scale * (
        second_normalized_rows
        - second_centered_input
        * jnp.mean(second_normalized_rows * second_centered_input, axis=1, keepdims=True)
    )
    grad_branch = grad_middle.astype(jnp.bfloat16)
    grad_wout = jnp.einsum("nd,ne->de", mixed_low, grad_branch, preferred_element_type=jnp.float32)
    grad_mixed = jnp.einsum(
        "ne,de->nd", grad_branch, w_out, preferred_element_type=jnp.float32
    ).astype(jnp.bfloat16)
    heads_query = queries.reshape(row_count, kv_count, group_size, HEAD).transpose(1, 0, 2, 3)
    heads_key = keys_turned.transpose(1, 0, 2)
    heads_value = values_low.reshape(row_count, kv_count, HEAD).transpose(1, 0, 2)
    heads_grad = grad_mixed.reshape(row_count, kv_count, group_size, HEAD).transpose(1, 0, 2, 3)

    def one_back(operands):
        head_query, head_key, head_value, head_lse, head_grad = operands
        scores = (
            jnp.einsum("qgd,td->gqt", head_query, head_key, preferred_element_type=jnp.float32)
            * score_scale
        )
        scores = jnp.where(allowed[None], scores, -1e30)
        probability = jnp.exp(scores - head_lse[..., None])
        grad_vhead = jnp.einsum(
            "gqt,qgd->td",
            probability.astype(jnp.bfloat16),
            head_grad,
            preferred_element_type=jnp.float32,
        )
        grad_prob = jnp.einsum(
            "qgd,td->gqt", head_grad, head_value, preferred_element_type=jnp.float32
        )
        grad_scores = (
            probability * (grad_prob - jnp.sum(probability * grad_prob, axis=2, keepdims=True))
        ).astype(jnp.bfloat16)
        grad_qhead = (
            jnp.einsum("gqt,td->qgd", grad_scores, head_key, preferred_element_type=jnp.float32)
            * score_scale
        )
        grad_khead = (
            jnp.einsum("gqt,qgd->td", grad_scores, head_query, preferred_element_type=jnp.float32)
            * score_scale
        )
        return (grad_qhead, grad_khead, grad_vhead)

    grad_qheads, grad_kheads, grad_vheads = lax.map(
        one_back, (heads_query, heads_key, heads_value, log_total, heads_grad)
    )
    grad_queries = (
        unrotate(
            grad_qheads.transpose(1, 0, 2, 3).reshape(row_count, -1, HEAD), cos_table, sine_table
        )
        .reshape(row_count, -1)
        .astype(jnp.bfloat16)
    )
    grad_keys = (
        unrotate(grad_kheads.transpose(1, 0, 2), cos_table, sine_table)
        .reshape(row_count, -1)
        .astype(jnp.bfloat16)
    )
    grad_values = grad_vheads.transpose(1, 0, 2).reshape(row_count, -1).astype(jnp.bfloat16)
    grad_wquery = jnp.einsum("nd,ne->de", normed, grad_queries, preferred_element_type=jnp.float32)
    grad_wkey = jnp.einsum("nd,ne->de", normed, grad_keys, preferred_element_type=jnp.float32)
    grad_wvalue = jnp.einsum("nd,ne->de", normed, grad_values, preferred_element_type=jnp.float32)
    first_norm_gradient = (
        jnp.einsum("ne,de->nd", grad_queries, w_query, preferred_element_type=jnp.float32)
        + jnp.einsum("ne,de->nd", grad_keys, w_key, preferred_element_type=jnp.float32)
        + jnp.einsum("ne,de->nd", grad_values, w_value, preferred_element_type=jnp.float32)
    )
    first_centered_input = layer_input_rows.astype(jnp.float32) * first_inverse_scale
    first_normalized_rows = first_norm_gradient * gain_one
    first_gain_gradient = jnp.sum(first_norm_gradient * first_centered_input, axis=0)
    grad_input = grad_middle + first_inverse_scale * (
        first_normalized_rows
        - first_centered_input
        * jnp.mean(first_normalized_rows * first_centered_input, axis=1, keepdims=True)
    )
    grad_terms = (
        grad_wquery,
        grad_wkey,
        grad_wvalue,
        grad_wout,
        jnp.concatenate([first_gain_gradient, second_gain_gradient]),
        grad_wgate,
        grad_wup,
        grad_wdown,
    )
    return (grad_input, tuple((member.reshape(piece_count, -1) for member in grad_terms)))


def on_device(boundary, doc_lens, w_query, w_key, w_value, w_out, gains, w_gate, w_up, w_down):
    sections = lax.axis_size("section")
    section_index = lax.axis_index("section")
    dp_count = lax.axis_size("dp")
    micro_count = boundary.shape[1]
    row_count = boundary.shape[2]
    model_width = boundary.shape[3]
    round_total = micro_count + sections - 1
    shards = (w_query, w_key, w_value, w_out, gains, w_gate, w_up, w_down)
    layouts = [
        doc_layout(doc_lens[micro_number, 0], row_count) for micro_number in range(micro_count)
    ]
    segments = jnp.stack([layout_item[0] for layout_item in layouts])
    positions = jnp.stack([layout_item[1] for layout_item in layouts])
    live_rows = jnp.stack([layout_item[2] for layout_item in layouts]).astype(jnp.float32)
    slot_ids = jnp.arange(row_count, dtype=jnp.int32)
    causal = slot_ids[None, :] <= slot_ids[:, None]

    def layout_for(micro_slot):
        segment = lax.dynamic_index_in_dim(segments, micro_slot, 0, keepdims=False)
        position = lax.dynamic_index_in_dim(positions, micro_slot, 0, keepdims=False)
        allowed = causal & (segment[:, None] == segment[None, :])
        cos_table, sine_table = rope_tables(position)
        return (allowed, cos_table, sine_table)

    matrices = unpack(
        (
            lax.all_gather(shards[0], "dp", axis=0, tiled=True),
            lax.all_gather(shards[1], "dp", axis=0, tiled=True),
            lax.all_gather(shards[2], "dp", axis=0, tiled=True),
            lax.all_gather(shards[3], "dp", axis=0, tiled=True),
            lax.all_gather(shards[4], "dp", axis=0, tiled=True),
            lax.all_gather(shards[5], "dp", axis=0, tiled=True),
            lax.all_gather(shards[6], "dp", axis=0, tiled=True),
            lax.all_gather(shards[7], "dp", axis=0, tiled=True),
        ),
        model_width,
    )
    own_inputs = boundary[0]
    results = jnp.zeros((micro_count, row_count, model_width), jnp.float32)
    outgoing = jnp.zeros((row_count, model_width), jnp.bfloat16)
    kept_rounds = []
    for round_index in range(round_total):
        if round_index > 0:
            incoming = passed_along(outgoing, "section", 1)
        else:
            incoming = jnp.zeros((row_count, model_width), jnp.bfloat16)
        micro_index = round_index - section_index
        is_valid = (micro_index >= 0) & (micro_index < micro_count)
        micro_slot = jnp.clip(micro_index, 0, micro_count - 1)
        layer_input_rows = jnp.where(
            section_index == 0,
            lax.dynamic_index_in_dim(own_inputs, micro_slot, 0, keepdims=False),
            incoming,
        )
        allowed, cos_table, sine_table = layout_for(micro_slot)
        layer_out, kept_values = forward_layer(
            layer_input_rows, matrices, allowed, cos_table, sine_table
        )
        kept_rounds.append(kept_values)
        finished = is_valid & (section_index == sections - 1)
        results = jnp.where(
            finished, lax.dynamic_update_index_in_dim(results, layer_out, micro_slot, 0), results
        )
        outgoing = layer_out.astype(jnp.bfloat16)
    stacked = jax.tree.map(lambda *members: jnp.stack(members), *kept_rounds)
    matrices_back = unpack(
        (
            lax.all_gather(shards[0], "dp", axis=0, tiled=True),
            lax.all_gather(shards[1], "dp", axis=0, tiled=True),
            lax.all_gather(shards[2], "dp", axis=0, tiled=True),
            lax.all_gather(shards[3], "dp", axis=0, tiled=True),
            lax.all_gather(shards[4], "dp", axis=0, tiled=True),
            lax.all_gather(shards[5], "dp", axis=0, tiled=True),
            lax.all_gather(shards[6], "dp", axis=0, tiled=True),
            lax.all_gather(shards[7], "dp", axis=0, tiled=True),
        ),
        model_width,
    )
    cotangent = boundary[sections - 1]
    totals = tuple(
        (jnp.zeros((dp_count, shard_piece.shape[1]), jnp.float32) for shard_piece in shards)
    )
    shares = tuple((jnp.zeros(shard_piece.shape, jnp.float32) for shard_piece in shards))
    back_outgoing = jnp.zeros((row_count, model_width), jnp.bfloat16)
    for round_index in range(round_total):
        if round_index > 0:
            arriving = passed_along(back_outgoing, "section", -1)
        else:
            arriving = jnp.zeros((row_count, model_width), jnp.bfloat16)
        micro_index = micro_count - 1 - round_index + (sections - 1 - section_index)
        is_valid = (micro_index >= 0) & (micro_index < micro_count)
        micro_slot = jnp.clip(micro_index, 0, micro_count - 1)
        kept_slot = jnp.clip(micro_index + section_index, 0, round_total - 1)
        kept_values = jax.tree.map(
            lambda member: lax.dynamic_index_in_dim(member, kept_slot, 0, keepdims=False), stacked
        )
        live_now = lax.dynamic_index_in_dim(live_rows, micro_slot, 0, keepdims=False)
        own_grad = (
            lax.dynamic_index_in_dim(cotangent, micro_slot, 0, keepdims=False).astype(jnp.float32)
            * live_now[:, None]
        )
        grad_output = jnp.where(
            section_index == sections - 1, own_grad, arriving.astype(jnp.float32)
        )
        grad_output = grad_output * is_valid.astype(jnp.float32)
        allowed, cos_table, sine_table = layout_for(micro_slot)
        grad_input, grad_terms = backward_layer(
            kept_values, matrices_back, allowed, cos_table, sine_table, grad_output, dp_count
        )
        totals = tuple(
            (left_term + right_term for left_term, right_term in zip(totals, grad_terms))
        )
        results = jnp.where(
            is_valid & (section_index == 0),
            lax.dynamic_update_index_in_dim(results, grad_input, micro_slot, 0),
            results,
        )
        back_outgoing = grad_input.astype(jnp.bfloat16)
    shares = add_sources(
        jax.tree.map(
            lambda part, own: part.astype(own.dtype),
            lax.all_to_all(as_sent(totals), "dp", split_axis=0, concat_axis=0, tiled=True),
            totals,
        )
    )
    return (
        results[None],
        shares[0],
        shares[1],
        shares[2],
        shares[3],
        shares[4],
        shares[5],
        shares[6],
        shares[7],
    )


def ring_place(chips):
    depth = chips // 2

    def place_of(chip):
        side = chip % 2
        level = chip // 2
        return level * (1 - side) + (chips - 1 - level) * side

    def chip_at(place):
        side = place // depth
        level = place * (1 - side) + (chips - 1 - place) * side
        return level * 2 + side

    return place_of, chip_at


def ring_setup(chips):
    place_of, chip_at = ring_place(chips)
    member = lax.axis_index("dp")
    core = member % 2
    place = place_of(member // 2)
    turn = 1 - 2 * core

    def at(offset, on_core):
        return chip_at((place + offset + 2 * chips) % chips) * 2 + on_core

    following = at(turn, core)
    preceding = at(-turn, core)
    sibling = member + turn
    barrier = pltpu.get_barrier_semaphore()
    for other in (following, preceding, sibling):
        pl.semaphore_signal(
            barrier, inc=1, device_id={"dp": other}, device_id_type=pl.DeviceIdType.MESH
        )
    pl.semaphore_wait(barrier, 3)
    return member, core, turn, at, following, sibling


def gather_kernel(chips, heights, *refs):
    count = len(heights)
    pieces = refs[:count]
    wholes = refs[count : 2 * count]
    keep_sem, ring_send, ring_recv, side_send, side_recv = refs[2 * count :]
    member, core, turn, at, following, sibling = ring_setup(chips)

    def rows(index, owner):
        height = heights[index]
        return wholes[index].at[pl.ds(pl.multiple_of(owner * height, 16), height), :]

    def ring_copy(index, source, owner, step):
        return pltpu.make_async_remote_copy(
            src_ref=source,
            dst_ref=rows(index, owner),
            send_sem=ring_send.at[step, index],
            recv_sem=ring_recv.at[step, index],
            device_id={"dp": following},
            device_id_type=pl.DeviceIdType.MESH,
        )

    def side_copy(index, source, owner, step):
        return pltpu.make_async_remote_copy(
            src_ref=source,
            dst_ref=rows(index, owner),
            send_sem=side_send.at[step, index],
            recv_sem=side_recv.at[step, index],
            device_id={"dp": sibling},
            device_id_type=pl.DeviceIdType.MESH,
        )

    for index in range(count):
        ring_copy(index, pieces[index], member, 0).start()
    for index in range(count):
        side_copy(index, pieces[index], member, 0).start()
        pltpu.make_async_copy(pieces[index], rows(index, member), keep_sem.at[index]).start()
    for step in range(1, chips):
        owner = at(-turn * step, core)
        for index in range(count):
            ring_copy(index, rows(index, owner), owner, step - 1).wait_recv()
            if step < chips - 1:
                ring_copy(index, rows(index, owner), owner, step).start()
            side_copy(index, rows(index, owner), owner, step).start()
    for index in range(count):
        pltpu.make_async_copy(pieces[index], rows(index, member), keep_sem.at[index]).wait()
    for step in range(chips):
        owner = at(-turn * step, core)
        theirs = at(turn * step, 1 - core)
        for index in range(count):
            if step < chips - 1:
                ring_copy(index, rows(index, owner), owner, step).wait_send()
            side_copy(index, rows(index, owner), owner, step).wait_send()
            side_copy(index, rows(index, theirs), theirs, step).wait_recv()


def gather_all(pieces, members):
    chips = members // 2
    heights = tuple(piece.shape[0] for piece in pieces)
    count = len(pieces)
    return pl.pallas_call(
        functools.partial(gather_kernel, chips, heights),
        out_shape=tuple(
            jax.ShapeDtypeStruct((members * piece.shape[0], piece.shape[1]), piece.dtype)
            for piece in pieces
        ),
        in_specs=[pl.BlockSpec(memory_space=pl.ANY)] * count,
        out_specs=tuple([pl.BlockSpec(memory_space=pl.ANY)] * count),
        scratch_shapes=[pltpu.SemaphoreType.DMA((count,))]
        + [pltpu.SemaphoreType.DMA((chips, count))] * 4,
        compiler_params=pltpu.CompilerParams(collective_id=0, has_side_effects=True),
        name="gather_ring",
    )(*pieces)


def scatter_kernel(chips, heights, *refs):
    count = len(heights)
    terms = refs[:count]
    totals = refs[count : 2 * count]
    owns = refs[2 * count : 3 * count]
    sides = refs[3 * count : 4 * count]
    rings = refs[4 * count : 5 * count]
    load_sem, ring_send, ring_recv, side_send, side_recv = refs[5 * count :]
    member, core, turn, at, following, sibling = ring_setup(chips)

    def rows(index, owner):
        height = heights[index]
        return terms[index].at[pl.ds(pl.multiple_of(owner * height, 16), height), :]

    def load(index, step):
        owner = at(-turn * (step + 1), core)
        return pltpu.make_async_copy(
            rows(index, owner), owns[index].at[step], load_sem.at[step, index]
        )

    def side_copy(index, step):
        owner = at(turn * (step + 1), 1 - core)
        return pltpu.make_async_remote_copy(
            src_ref=rows(index, owner),
            dst_ref=sides[index].at[step],
            send_sem=side_send.at[step, index],
            recv_sem=side_recv.at[step, index],
            device_id={"dp": sibling},
            device_id_type=pl.DeviceIdType.MESH,
        )

    def ring_copy(index, step):
        return pltpu.make_async_remote_copy(
            src_ref=owns[index].at[step],
            dst_ref=rings[index].at[step],
            send_sem=ring_send.at[step, index],
            recv_sem=ring_recv.at[step, index],
            device_id={"dp": following},
            device_id_type=pl.DeviceIdType.MESH,
        )

    for step in range(chips):
        for index in range(count):
            side_copy(index, step).start()
            load(index, step).start()
    for step in range(chips):
        for index in range(count):
            load(index, step).wait()
            side_copy(index, step).wait_recv()
            if step > 0:
                ring_copy(index, step - 1).wait_recv()

            def add(block):
                part = pl.ds(pl.multiple_of(block * 16, 16), 16)
                total = owns[index][step, part, :].astype(jnp.float32) + sides[index][
                    step, part, :
                ].astype(jnp.float32)
                if step > 0:
                    total = total + rings[index][step - 1, part, :].astype(jnp.float32)
                if step < chips - 1:
                    owns[index][step, part, :] = total.astype(jnp.bfloat16)
                else:
                    totals[index][part, :] = total

            pl.loop(0, heights[index] // 16)(add)
            if step < chips - 1:
                ring_copy(index, step).start()
    for step in range(chips):
        for index in range(count):
            side_copy(index, step).wait_send()
            if step < chips - 1:
                ring_copy(index, step).wait_send()


def scatter_all(terms, members):
    chips = members // 2
    heights = tuple(term.shape[0] // members for term in terms)
    widths = tuple(term.shape[1] for term in terms)
    count = len(terms)
    stacks = lambda depth: [
        pltpu.VMEM((depth, height, width), jnp.bfloat16) for height, width in zip(heights, widths)
    ]
    return pl.pallas_call(
        functools.partial(scatter_kernel, chips, heights),
        out_shape=tuple(
            jax.ShapeDtypeStruct((height, width), jnp.float32)
            for height, width in zip(heights, widths)
        ),
        in_specs=[pl.BlockSpec(memory_space=pl.ANY)] * count,
        out_specs=tuple([pl.BlockSpec(memory_space=pltpu.VMEM)] * count),
        scratch_shapes=stacks(chips)
        + stacks(chips)
        + stacks(chips - 1)
        + [pltpu.SemaphoreType.DMA((chips, count))] * 5,
        compiler_params=pltpu.CompilerParams(
            collective_id=1, has_side_effects=True, vmem_limit_bytes=56 * 2**20
        ),
        name="scatter_ring",
    )(*terms)


def dot(left, right):
    return jnp.dot(left, right, preferred_element_type=jnp.float32)


def dot_nt(left, right):
    return lax.dot_general(
        left, right, (((1,), (1,)), ((), ())), preferred_element_type=jnp.float32
    )


def dot_tn(left, right):
    return lax.dot_general(
        left, right, (((0,), (0,)), ((), ())), preferred_element_type=jnp.float32
    )


def turn_heads(values, tables, sign):
    width = values.shape[1]
    cos_table, early_sine, late_sine = tables
    half = HEAD // 2
    return values * cos_table[...] + sign * (
        pltpu.roll(values, width - half, 1) * early_sine[...]
        + pltpu.roll(values, half, 1) * late_sine[...]
    )


def head_rows(source, micro, rows, first, group):
    return jnp.concatenate(
        [
            source[micro * rows : (micro + 1) * rows, (first + g) * HEAD : (first + g + 1) * HEAD]
            for g in range(group)
        ],
        axis=0,
    )


def forward_kernel(
    model,
    layout,
    stream,
    gains,
    bias,
    cos_table,
    early_sine,
    late_sine,
    spread,
    w_qkv,
    w_out,
    w_gate,
    w_up,
    w_down,
    layer_out,
    normed,
    turned,
    values,
    mixed_wide,
    middle,
    normed_two,
    gate_pre,
    up_pre,
    activation,
    mixed,
):
    heads, kv_heads, micro_count, rows = layout
    group = heads // kv_heads

    @pl.when(pl.program_id(0) == 0)
    def _():
        residual = stream[...]
        scale = lax.rsqrt(jnp.sum(residual * residual, axis=1, keepdims=True) / model + EPSILON)
        normed[...] = (residual * scale * gains[0:1, :]).astype(jnp.bfloat16)
        products = dot(normed[...], w_qkv[...])
        split = (heads + kv_heads) * HEAD
        turned[...] = turn_heads(
            products[:, :split], (cos_table, early_sine, late_sine), 1.0
        ).astype(jnp.bfloat16)
        values[...] = products[:, split:].astype(jnp.bfloat16)
        for micro in range(micro_count):
            part = slice(micro * rows, (micro + 1) * rows)
            for kv in range(kv_heads):
                query = head_rows(turned, micro, rows, kv * group, group)
                key = turned[part, (heads + kv) * HEAD : (heads + kv + 1) * HEAD]
                value = values[part, kv * HEAD : (kv + 1) * HEAD]
                scores = dot_nt(query, key) * HEAD ** (-0.5)
                scores = scores + jnp.concatenate([bias[micro]] * group, axis=0)
                exponent = jnp.exp(scores - jnp.max(scores, axis=1, keepdims=True))
                total = jnp.sum(exponent, axis=1, keepdims=True)
                probability = (exponent / total).astype(jnp.bfloat16)
                attended = dot(probability, value).astype(jnp.bfloat16)
                for g in range(group):
                    head = kv * group + g
                    mixed[part, head * HEAD : (head + 1) * HEAD] = attended[
                        g * rows : (g + 1) * rows, :
                    ]
        mixed_wide[...] = dot(mixed[...], spread[...]).astype(jnp.bfloat16)
        halfway = residual + dot(mixed_wide[...], w_out[...])
        middle[...] = halfway
        scale_two = lax.rsqrt(jnp.sum(halfway * halfway, axis=1, keepdims=True) / model + EPSILON)
        normed_two[...] = (halfway * scale_two * gains[1:2, :]).astype(jnp.bfloat16)
        layer_out[...] = halfway

    gate = dot(normed_two[...], w_gate[...])
    up = dot(normed_two[...], w_up[...])
    gate_pre[...] = gate
    up_pre[...] = up
    active = (gate * jax.nn.sigmoid(gate) * up).astype(jnp.bfloat16)
    activation[...] = active
    layer_out[...] += dot(active, w_down[...])


def full(array):
    return pl.BlockSpec(array.shape, lambda i: (0,) * len(array.shape))


def shape_of(rows, width, dtype):
    return jax.ShapeDtypeStruct((rows, width), dtype)


def tile_width(hidden):
    for width in (512, 256, 128):
        if hidden % width == 0:
            return width
    return hidden


def forward_fast(model, layout, stream, gains, bias, tables, spread, matrices):
    w_qkv, w_out, w_gate, w_up, w_down = matrices
    heads, kv_heads, micro_count, rows = layout
    tokens, wide = stream.shape
    hidden = w_gate.shape[1]
    tile = tile_width(hidden)
    split = (heads + kv_heads) * HEAD
    low, high = jnp.bfloat16, jnp.float32
    out_shape = (
        shape_of(tokens, wide, high),
        shape_of(tokens, wide, low),
        shape_of(tokens, split, low),
        shape_of(tokens, w_qkv.shape[1] - split, low),
        shape_of(tokens, wide, low),
        shape_of(tokens, wide, high),
        shape_of(tokens, wide, low),
        shape_of(tokens, hidden, high),
        shape_of(tokens, hidden, high),
        shape_of(tokens, hidden, low),
    )
    columns = lambda height: pl.BlockSpec((height, tile), lambda i: (0, i))
    ins = (stream, gains, bias, *tables, spread, w_qkv, w_out)
    return pl.pallas_call(
        functools.partial(forward_kernel, model, layout),
        grid=(hidden // tile,),
        out_shape=out_shape,
        in_specs=[full(member) for member in ins]
        + [columns(wide), columns(wide), pl.BlockSpec((tile, wide), lambda i: (i, 0))],
        out_specs=tuple([full(member) for member in out_shape[:7]] + [columns(tokens)] * 3),
        scratch_shapes=[pltpu.VMEM((tokens, heads * HEAD), low)],
        compiler_params=pltpu.CompilerParams(vmem_limit_bytes=56 * 2**20),
        cost_estimate=pl.CostEstimate(
            flops=20 * 2**28, bytes_accessed=30 * 2**20, transcendentals=2**20
        ),
        name="forward_layer",
    )(*ins, w_gate, w_up, w_down)


def backward_kernel(
    model,
    layout,
    cotangent,
    stream,
    gains,
    bias,
    cos_table,
    early_sine,
    late_sine,
    spread,
    turned,
    values,
    middle,
    w_qkv,
    w_out,
    gate_pre,
    up_pre,
    w_gate,
    w_up,
    w_down,
    grad_input,
    grad_low,
    grad_gains,
    grad_branch,
    grad_qkv,
    grad_gate,
    grad_up,
    norm_grad,
    grad_mixed,
    grad_turned,
    grad_values,
):
    heads, kv_heads, micro_count, rows = layout
    group = heads // kv_heads
    step = pl.program_id(0)

    @pl.when(step == 0)
    def _():
        grad_low[...] = cotangent[...].astype(jnp.bfloat16)
        norm_grad[...] = jnp.zeros_like(norm_grad)

    gate = gate_pre[...]
    grad_act = dot_nt(grad_low[...], w_down[...])
    sigmoid = jax.nn.sigmoid(gate)
    grad_gate[...] = (
        grad_act * up_pre[...] * sigmoid * (1.0 + gate * (1.0 - sigmoid))
    ).astype(jnp.bfloat16)
    grad_up[...] = (grad_act * gate * sigmoid).astype(jnp.bfloat16)
    norm_grad[...] += dot_nt(grad_gate[...], w_gate[...]) + dot_nt(grad_up[...], w_up[...])

    @pl.when(step == pl.num_programs(0) - 1)
    def _():
        halfway = middle[...]
        scale_two = lax.rsqrt(jnp.sum(halfway * halfway, axis=1, keepdims=True) / model + EPSILON)
        centered = halfway * scale_two
        gradient = norm_grad[...]
        grad_gains[1:2, :] = jnp.sum(gradient * centered, axis=0, keepdims=True)
        scaled = gradient * gains[1:2, :]
        grad_middle = cotangent[...] + scale_two * (
            scaled - centered * (jnp.sum(scaled * centered, axis=1, keepdims=True) / model)
        )
        grad_input[...] = grad_middle
        grad_branch[...] = grad_middle.astype(jnp.bfloat16)
        grad_wide = dot_nt(grad_branch[...], w_out[...]).astype(jnp.bfloat16)
        grad_mixed[...] = dot_nt(grad_wide, spread[...]).astype(jnp.bfloat16)
        grad_values[...] = jnp.zeros_like(grad_values)
        for micro in range(micro_count):
            part = slice(micro * rows, (micro + 1) * rows)
            for kv in range(kv_heads):
                query = head_rows(turned, micro, rows, kv * group, group)
                key = turned[part, (heads + kv) * HEAD : (heads + kv + 1) * HEAD]
                value = values[part, kv * HEAD : (kv + 1) * HEAD]
                grad_head = head_rows(grad_mixed, micro, rows, kv * group, group)
                scores = dot_nt(query, key) * HEAD ** (-0.5)
                scores = scores + jnp.concatenate([bias[micro]] * group, axis=0)
                exponent = jnp.exp(scores - jnp.max(scores, axis=1, keepdims=True))
                total = jnp.sum(exponent, axis=1, keepdims=True)
                probability = exponent / total
                grad_value = dot_tn(probability.astype(jnp.bfloat16), grad_head)
                grad_prob = dot_nt(grad_head, value)
                inner = jnp.sum(probability * grad_prob, axis=1, keepdims=True)
                grad_scores = (probability * (grad_prob - inner)).astype(jnp.bfloat16)
                grad_query = dot(grad_scores, key) * HEAD ** (-0.5)
                grad_key = dot_tn(grad_scores, query) * HEAD ** (-0.5)
                for g in range(group):
                    head = kv * group + g
                    grad_turned[part, head * HEAD : (head + 1) * HEAD] = grad_query[
                        g * rows : (g + 1) * rows, :
                    ]
                grad_turned[part, (heads + kv) * HEAD : (heads + kv + 1) * HEAD] = grad_key
                grad_values[part, kv * HEAD : (kv + 1) * HEAD] = grad_value
        split = (heads + kv_heads) * HEAD
        grad_qkv[:, :split] = turn_heads(
            grad_turned[...], (cos_table, early_sine, late_sine), -1.0
        ).astype(jnp.bfloat16)
        grad_qkv[:, split:] = grad_values[...].astype(jnp.bfloat16)
        first_gradient = dot_nt(grad_qkv[...], w_qkv[...])
        residual = stream[...]
        scale = lax.rsqrt(jnp.sum(residual * residual, axis=1, keepdims=True) / model + EPSILON)
        first_centered = residual * scale
        grad_gains[0:1, :] = jnp.sum(first_gradient * first_centered, axis=0, keepdims=True)
        first_scaled = first_gradient * gains[0:1, :]
        grad_input[...] += scale * (
            first_scaled
            - first_centered
            * (jnp.sum(first_scaled * first_centered, axis=1, keepdims=True) / model)
        )


def backward_fast(model, layout, cotangent, kept, gains, bias, tables, spread, matrices):
    w_qkv, w_out, w_gate, w_up, w_down = matrices
    stream, _, turned, values, _, middle, _, gate_pre, up_pre, _ = kept
    heads, kv_heads, micro_count, rows = layout
    tokens, wide = stream.shape
    hidden = w_gate.shape[1]
    tile = tile_width(hidden)
    split = (heads + kv_heads) * HEAD
    low, high = jnp.bfloat16, jnp.float32
    out_shape = (
        shape_of(tokens, wide, high),
        shape_of(tokens, wide, low),
        shape_of(2, wide, high),
        shape_of(tokens, wide, low),
        shape_of(tokens, w_qkv.shape[1], low),
        shape_of(tokens, hidden, low),
        shape_of(tokens, hidden, low),
    )
    columns = lambda height: pl.BlockSpec((height, tile), lambda i: (0, i))
    ins = (cotangent, stream, gains, bias, *tables, spread, turned, values, middle, w_qkv, w_out)
    return pl.pallas_call(
        functools.partial(backward_kernel, model, layout),
        grid=(hidden // tile,),
        out_shape=out_shape,
        in_specs=[full(member) for member in ins]
        + [columns(tokens)] * 2
        + [columns(wide), columns(wide), pl.BlockSpec((tile, wide), lambda i: (i, 0))],
        out_specs=tuple([full(member) for member in out_shape[:5]] + [columns(tokens)] * 2),
        scratch_shapes=[
            pltpu.VMEM((tokens, wide), high),
            pltpu.VMEM((tokens, heads * HEAD), low),
            pltpu.VMEM((tokens, split), high),
            pltpu.VMEM((tokens, w_qkv.shape[1] - split), high),
        ],
        compiler_params=pltpu.CompilerParams(vmem_limit_bytes=56 * 2**20),
        cost_estimate=pl.CostEstimate(
            flops=24 * 2**28, bytes_accessed=36 * 2**20, transcendentals=2**20
        ),
        name="backward_layer",
    )(*ins, gate_pre, up_pre, w_gate, w_up, w_down)


def widen(array, members, room):
    width = array.shape[-1] // members
    cut = array.reshape(array.shape[:-1] + (members, width))
    cut = jnp.pad(cut, [(0, 0)] * (cut.ndim - 1) + [(0, room - width)])
    return cut.reshape(array.shape[:-1] + (members * room,))


def narrow(array, members, width):
    room = array.shape[-1] // members
    cut = array.reshape(array.shape[:-1] + (members, room))[..., :width]
    return cut.reshape(array.shape[:-1] + (members * width,))


def lifted(array, height, width):
    return jnp.pad(array, [(0, height - array.shape[0]), (0, width - array.shape[1])])


def rows_room(model, members):
    return -(-(model // members + 1) // 16) * 16


def on_device_fast(boundary, doc_lens, w_query, w_key, w_value, w_out, gains, w_gate, w_up, w_down):
    section = lax.axis_index("section")
    members = lax.axis_size("dp")
    _, micro_count, rows, model = boundary.shape
    tokens = micro_count * rows
    piece = model // members
    room = rows_room(model, members)
    wide = room * members
    kv_width = w_key.size // piece
    hidden = w_gate.size // piece
    heads, kv_heads = model // HEAD, kv_width // HEAD
    layout = (heads, kv_heads, micro_count, rows)
    split = model + kv_width
    qkv_wide = split + -(-kv_width // 128) * 128
    hidden_piece = hidden // members
    gain_piece = gains.size

    feature = jnp.arange(model, dtype=jnp.int32)
    spread = (
        (feature // piece * room + feature % piece)[:, None]
        == jnp.arange(wide, dtype=jnp.int32)[None, :]
    ).astype(jnp.bfloat16)

    def spread_out(array):
        return jnp.dot(array, spread, preferred_element_type=jnp.float32).astype(array.dtype)

    qkv_piece = jnp.concatenate(
        [
            w_query.reshape(piece, model),
            w_key.reshape(piece, kv_width),
            w_value.reshape(piece, kv_width),
        ],
        axis=1,
    )
    out_piece = lifted(spread_out(w_out.reshape(piece, model)), room, wide)
    gain_row = lifted(gains.reshape(1, gain_piece), 1, wide)
    out_piece = lax.dynamic_update_slice(out_piece, gain_row, (piece, 0))
    gathered = gather_all(
        (
            lifted(qkv_piece, room, qkv_wide),
            out_piece,
            lifted(w_gate.reshape(piece, hidden), room, hidden),
            lifted(w_up.reshape(piece, hidden), room, hidden),
            spread_out(w_down.reshape(hidden_piece, model)),
        ),
        members,
    )
    gain_rows = gathered[1].reshape(members, room, wide)[:, piece, :gain_piece]
    gain_pair = widen(gain_rows.reshape(2, model), members, room).astype(jnp.float32)

    layouts = [doc_layout(doc_lens[micro, 0], rows) for micro in range(micro_count)]
    segments = jnp.stack([item[0] for item in layouts])
    positions = jnp.concatenate([item[1] for item in layouts])
    live = jnp.concatenate([item[2] for item in layouts]).astype(jnp.float32)
    slot_ids = jnp.arange(rows, dtype=jnp.int32)
    allowed = (slot_ids[None, :] <= slot_ids[:, None])[None] & (
        segments[:, :, None] == segments[:, None, :]
    )
    bias = jnp.where(allowed, 0.0, -1e30).astype(jnp.float32)
    cos_table, sine_table = rope_tables(positions)
    first_half = (jnp.arange(HEAD, dtype=jnp.int32) < HEAD // 2)[None, :]
    repeat = split // HEAD
    tables = tuple(
        jnp.tile(table, (1, repeat))
        for table in (
            cos_table,
            jnp.where(first_half, -sine_table, 0.0),
            jnp.where(first_half, 0.0, sine_table),
        )
    )

    own = spread_out(boundary.reshape(tokens, model))
    stream_zero = own.astype(jnp.float32)
    shared = (gain_pair, bias, tables, spread, gathered)
    kept_zero = forward_fast(model, layout, stream_zero, *shared)
    relayed = passed_along(kept_zero[0].astype(jnp.bfloat16), "section", 1)
    stream_one = relayed.astype(jnp.float32)
    kept_one = forward_fast(model, layout, stream_one, *shared)

    cotangent = jnp.where(section == 1, stream_zero * live[:, None], 0.0)
    back_one = backward_fast(model, layout, cotangent, (stream_one,) + tuple(kept_one[1:]), *shared)
    returned = passed_along(back_one[0].astype(jnp.bfloat16), "section", -1).astype(jnp.float32)
    back_zero = backward_fast(
        model, layout, returned, (stream_zero,) + tuple(kept_zero[1:]), *shared
    )

    pick = lambda early, late: jnp.where(section == 0, early, late)
    results = narrow(pick(back_zero[0], kept_one[0]), members, piece)
    normed, mixed, normed_two, activation = (
        pick(kept_zero[at], kept_one[at]) for at in (1, 4, 6, 9)
    )
    _, grad_low, grad_gains, grad_branch, grad_qkv, grad_gate, grad_up = (
        pick(early, late) for early, late in zip(back_zero, back_one)
    )
    product = lambda left, right: jnp.einsum(
        "nd,ne->de", left, right, preferred_element_type=jnp.float32
    ).astype(jnp.bfloat16)
    gain_terms = narrow(grad_gains, members, piece).reshape(members, 1, gain_piece)
    out_terms = lax.dynamic_update_slice(
        product(mixed, grad_branch).reshape(members, room, wide),
        gain_terms.astype(jnp.bfloat16),
        (0, piece, 0),
    ).reshape(wide, wide)
    share_qkv, share_out, share_gate, share_up, share_down = scatter_all(
        (
            product(normed, grad_qkv),
            out_terms,
            product(normed_two, grad_gate),
            product(normed_two, grad_up),
            product(activation, grad_low),
        ),
        members,
    )
    flat = lambda array: array.reshape(1, -1)
    return (
        results.reshape(1, micro_count, rows, model),
        flat(share_qkv[:piece, :model]),
        flat(share_qkv[:piece, model:split]),
        flat(share_qkv[:piece, split : split + kv_width]),
        flat(narrow(share_out[:piece], members, piece)),
        flat(share_out[piece : piece + 1, :gain_piece]),
        flat(share_gate[:piece]),
        flat(share_up[:piece]),
        flat(narrow(share_down, members, piece)),
    )


def rows_fit(mesh, model, hidden):
    members = mesh.shape["dp"]
    return (
        mesh.shape["section"] == 2
        and members >= 6
        and members % 4 == 0
        and model % members == 0
        and hidden % members == 0
        and (hidden // members) % 16 == 0
        and (rows_room(model, members) * members) % 128 == 0
    )


def solution(mesh):
    placed = (
        P("section", None, "dp", None),
        P(None, "dp", None),
        P("section", "dp"),
        P("section", "dp"),
        P("section", "dp"),
        P("section", "dp"),
        P("section", "dp"),
        P("section", "dp"),
        P("section", "dp"),
        P("section", "dp"),
    )

    def chosen(*operands):
        model = operands[0].shape[3]
        hidden = operands[7].size * mesh.shape["dp"] // model
        return (on_device_fast if rows_fit(mesh, model, hidden) else on_device)(*operands)

    return jax.shard_map(
        chosen,
        mesh=mesh,
        in_specs=placed,
        out_specs=(
            P("section", None, "dp", None),
            P("section", "dp"),
            P("section", "dp"),
            P("section", "dp"),
            P("section", "dp"),
            P("section", "dp"),
            P("section", "dp"),
            P("section", "dp"),
            P("section", "dp"),
        ),
        check_vma=False,
    )
```

```python
import functools

import jax
import jax.numpy as jnp
from jax import lax
from jax.experimental import pallas as pl
from jax.experimental.pallas import tpu as pltpu
from jax.sharding import PartitionSpec as P

HEAD = 64


EPSILON = 1e-05
ROPE_BASE = 100000.0


def passed_along(x, axis, by):
    devices = lax.axis_size(axis)
    pairs = [(i, i + by) for i in range(devices) if 0 <= i + by < devices]
    return lax.ppermute(x, axis, pairs)


def as_sent(x):
    return jax.tree.map(lambda a: a.astype(jnp.bfloat16) if a.dtype == jnp.float32 else a, x)


def doc_layout(lengths, slot_count):
    doc_ends = jnp.cumsum(lengths, dtype=jnp.int32)
    doc_starts = doc_ends - lengths
    doc_count = lengths.shape[0]
    slot_ids = jnp.arange(slot_count, dtype=jnp.int32)
    segment = jnp.sum(
        (slot_ids[:, None] >= doc_ends[None, :]).astype(jnp.int32), axis=1, dtype=jnp.int32
    )
    start_table = jnp.concatenate([doc_starts, doc_ends[doc_count - 1 :]])
    picked = segment[:, None] == jnp.arange(doc_count + 1, dtype=jnp.int32)[None, :]
    first_slot = jnp.sum(jnp.where(picked, start_table[None, :], 0), axis=1, dtype=jnp.int32)
    return (segment, slot_ids - first_slot, segment < doc_count)


def rope_tables(position):
    half_width = HEAD // 2
    inverse_freq = ROPE_BASE ** (-(jnp.arange(half_width, dtype=jnp.float32) * (2.0 / HEAD)))
    angles = position.astype(jnp.float32)[:, None] * inverse_freq[None, :]
    cos_table = jnp.cos(angles)
    sine_table = jnp.sin(angles)
    return (
        jnp.concatenate([cos_table, cos_table], axis=1),
        jnp.concatenate([sine_table, sine_table], axis=1),
    )


def rotate(values, cos_table, sine_table):
    half_width = values.shape[-1] // 2
    turned = jnp.concatenate([-values[..., half_width:], values[..., :half_width]], axis=-1)
    return values * cos_table[:, None, :] + turned * sine_table[:, None, :]


def unrotate(values, cos_table, sine_table):
    half_width = values.shape[-1] // 2
    sined = values * sine_table[:, None, :]
    turned = jnp.concatenate([sined[..., half_width:], -sined[..., :half_width]], axis=-1)
    return values * cos_table[:, None, :] + turned


def unpack(gathered, model_width):
    kv_width = gathered[1].size // model_width
    hidden_width = gathered[5].size // model_width
    return (
        gathered[0].reshape(model_width, model_width),
        gathered[1].reshape(model_width, kv_width),
        gathered[2].reshape(model_width, kv_width),
        gathered[3].reshape(model_width, model_width),
        gathered[4].reshape(2 * model_width),
        gathered[5].reshape(model_width, hidden_width),
        gathered[6].reshape(model_width, hidden_width),
        gathered[7].reshape(hidden_width, model_width),
    )


def add_sources(received):
    return tuple((jnp.sum(member, axis=0, keepdims=True) for member in received))


def forward_layer(layer_input_rows, matrices, allowed, cos_table, sine_table):
    w_query, w_key, w_value, w_out, gain_pair, w_gate, w_up, w_down = matrices
    row_count, model_width = layer_input_rows.shape
    kv_count = w_key.shape[1] // HEAD
    group_size = w_query.shape[1] // w_key.shape[1]
    score_scale = HEAD ** (-0.5)
    gain_one = gain_pair[:model_width].astype(jnp.float32)
    gain_two = gain_pair[model_width:].astype(jnp.float32)
    residual = layer_input_rows.astype(jnp.float32)
    first_inverse_scale = lax.rsqrt(jnp.mean(residual * residual, axis=1, keepdims=True) + EPSILON)
    normed = (residual * first_inverse_scale * gain_one).astype(jnp.bfloat16)
    queries = rotate(
        jnp.dot(normed, w_query, preferred_element_type=jnp.float32).reshape(row_count, -1, HEAD),
        cos_table,
        sine_table,
    ).astype(jnp.bfloat16)
    keys_turned = rotate(
        jnp.dot(normed, w_key, preferred_element_type=jnp.float32).reshape(
            row_count, kv_count, HEAD
        ),
        cos_table,
        sine_table,
    ).astype(jnp.bfloat16)
    values_low = jnp.dot(normed, w_value, preferred_element_type=jnp.float32).astype(jnp.bfloat16)
    heads_query = queries.reshape(row_count, kv_count, group_size, HEAD).transpose(1, 0, 2, 3)
    heads_key = keys_turned.transpose(1, 0, 2)
    heads_value = values_low.reshape(row_count, kv_count, HEAD).transpose(1, 0, 2)

    def one_head(operands):
        head_query, head_key, head_value = operands
        scores = (
            jnp.einsum("qgd,td->gqt", head_query, head_key, preferred_element_type=jnp.float32)
            * score_scale
        )
        scores = jnp.where(allowed[None], scores, -1e30)
        row_top = jnp.max(scores, axis=2, keepdims=True)
        exponent = jnp.exp(scores - row_top)
        row_total = jnp.sum(exponent, axis=2, keepdims=True)
        probability = (exponent / row_total).astype(jnp.bfloat16)
        attended = jnp.einsum(
            "gqt,td->qgd", probability, head_value, preferred_element_type=jnp.float32
        )
        return (attended, (row_top + jnp.log(row_total))[..., 0])

    attended, log_total = lax.map(one_head, (heads_query, heads_key, heads_value))
    mixed_low = attended.transpose(1, 0, 2, 3).reshape(row_count, model_width).astype(jnp.bfloat16)
    midway_hidden = residual + jnp.dot(mixed_low, w_out, preferred_element_type=jnp.float32)
    second_inverse_scale = lax.rsqrt(
        jnp.mean(midway_hidden * midway_hidden, axis=1, keepdims=True) + EPSILON
    )
    normed_two = (midway_hidden * second_inverse_scale * gain_two).astype(jnp.bfloat16)
    gate_pre = jnp.dot(normed_two, w_gate, preferred_element_type=jnp.float32)
    up_pre = jnp.dot(normed_two, w_up, preferred_element_type=jnp.float32)
    activation = (jax.nn.silu(gate_pre) * up_pre).astype(jnp.bfloat16)
    layer_out = midway_hidden + jnp.dot(activation, w_down, preferred_element_type=jnp.float32)
    kept_values = (
        layer_input_rows,
        normed,
        queries,
        keys_turned,
        values_low,
        log_total,
        mixed_low,
        midway_hidden,
        first_inverse_scale,
        second_inverse_scale,
        normed_two,
        gate_pre,
        up_pre,
        activation,
    )
    return (layer_out, kept_values)


def backward_layer(kept_values, matrices, allowed, cos_table, sine_table, grad_output, piece_count):
    (
        layer_input_rows,
        normed,
        queries,
        keys_turned,
        values_low,
        log_total,
        mixed_low,
        midway_hidden,
        first_inverse_scale,
        second_inverse_scale,
        normed_two,
        gate_pre,
        up_pre,
        activation,
    ) = kept_values
    w_query, w_key, w_value, w_out, gain_pair, w_gate, w_up, w_down = matrices
    row_count, model_width = layer_input_rows.shape
    kv_count = w_key.shape[1] // HEAD
    group_size = w_query.shape[1] // w_key.shape[1]
    score_scale = HEAD ** (-0.5)
    gain_one = gain_pair[:model_width].astype(jnp.float32)
    gain_two = gain_pair[model_width:].astype(jnp.float32)
    grad_low = grad_output.astype(jnp.bfloat16)
    grad_wdown = jnp.einsum("nf,nd->fd", activation, grad_low, preferred_element_type=jnp.float32)
    grad_act = jnp.einsum("nd,fd->nf", grad_low, w_down, preferred_element_type=jnp.float32)
    sigmoid_gate = jax.nn.sigmoid(gate_pre)
    grad_gate_pre = (
        grad_act * up_pre * sigmoid_gate * (1.0 + gate_pre * (1.0 - sigmoid_gate))
    ).astype(jnp.bfloat16)
    grad_up_pre = (grad_act * gate_pre * sigmoid_gate).astype(jnp.bfloat16)
    grad_wgate = jnp.einsum(
        "nd,nf->df", normed_two, grad_gate_pre, preferred_element_type=jnp.float32
    )
    grad_wup = jnp.einsum("nd,nf->df", normed_two, grad_up_pre, preferred_element_type=jnp.float32)
    second_norm_gradient = jnp.einsum(
        "nf,df->nd", grad_gate_pre, w_gate, preferred_element_type=jnp.float32
    ) + jnp.einsum("nf,df->nd", grad_up_pre, w_up, preferred_element_type=jnp.float32)
    second_centered_input = midway_hidden * second_inverse_scale
    second_normalized_rows = second_norm_gradient * gain_two
    second_gain_gradient = jnp.sum(second_norm_gradient * second_centered_input, axis=0)
    grad_middle = grad_output + second_inverse_scale * (
        second_normalized_rows
        - second_centered_input
        * jnp.mean(second_normalized_rows * second_centered_input, axis=1, keepdims=True)
    )
    grad_branch = grad_middle.astype(jnp.bfloat16)
    grad_wout = jnp.einsum("nd,ne->de", mixed_low, grad_branch, preferred_element_type=jnp.float32)
    grad_mixed = jnp.einsum(
        "ne,de->nd", grad_branch, w_out, preferred_element_type=jnp.float32
    ).astype(jnp.bfloat16)
    heads_query = queries.reshape(row_count, kv_count, group_size, HEAD).transpose(1, 0, 2, 3)
    heads_key = keys_turned.transpose(1, 0, 2)
    heads_value = values_low.reshape(row_count, kv_count, HEAD).transpose(1, 0, 2)
    heads_grad = grad_mixed.reshape(row_count, kv_count, group_size, HEAD).transpose(1, 0, 2, 3)

    def one_back(operands):
        head_query, head_key, head_value, head_lse, head_grad = operands
        scores = (
            jnp.einsum("qgd,td->gqt", head_query, head_key, preferred_element_type=jnp.float32)
            * score_scale
        )
        scores = jnp.where(allowed[None], scores, -1e30)
        probability = jnp.exp(scores - head_lse[..., None])
        grad_vhead = jnp.einsum(
            "gqt,qgd->td",
            probability.astype(jnp.bfloat16),
            head_grad,
            preferred_element_type=jnp.float32,
        )
        grad_prob = jnp.einsum(
            "qgd,td->gqt", head_grad, head_value, preferred_element_type=jnp.float32
        )
        grad_scores = (
            probability * (grad_prob - jnp.sum(probability * grad_prob, axis=2, keepdims=True))
        ).astype(jnp.bfloat16)
        grad_qhead = (
            jnp.einsum("gqt,td->qgd", grad_scores, head_key, preferred_element_type=jnp.float32)
            * score_scale
        )
        grad_khead = (
            jnp.einsum("gqt,qgd->td", grad_scores, head_query, preferred_element_type=jnp.float32)
            * score_scale
        )
        return (grad_qhead, grad_khead, grad_vhead)

    grad_qheads, grad_kheads, grad_vheads = lax.map(
        one_back, (heads_query, heads_key, heads_value, log_total, heads_grad)
    )
    grad_queries = (
        unrotate(
            grad_qheads.transpose(1, 0, 2, 3).reshape(row_count, -1, HEAD), cos_table, sine_table
        )
        .reshape(row_count, -1)
        .astype(jnp.bfloat16)
    )
    grad_keys = (
        unrotate(grad_kheads.transpose(1, 0, 2), cos_table, sine_table)
        .reshape(row_count, -1)
        .astype(jnp.bfloat16)
    )
    grad_values = grad_vheads.transpose(1, 0, 2).reshape(row_count, -1).astype(jnp.bfloat16)
    grad_wquery = jnp.einsum("nd,ne->de", normed, grad_queries, preferred_element_type=jnp.float32)
    grad_wkey = jnp.einsum("nd,ne->de", normed, grad_keys, preferred_element_type=jnp.float32)
    grad_wvalue = jnp.einsum("nd,ne->de", normed, grad_values, preferred_element_type=jnp.float32)
    first_norm_gradient = (
        jnp.einsum("ne,de->nd", grad_queries, w_query, preferred_element_type=jnp.float32)
        + jnp.einsum("ne,de->nd", grad_keys, w_key, preferred_element_type=jnp.float32)
        + jnp.einsum("ne,de->nd", grad_values, w_value, preferred_element_type=jnp.float32)
    )
    first_centered_input = layer_input_rows.astype(jnp.float32) * first_inverse_scale
    first_normalized_rows = first_norm_gradient * gain_one
    first_gain_gradient = jnp.sum(first_norm_gradient * first_centered_input, axis=0)
    grad_input = grad_middle + first_inverse_scale * (
        first_normalized_rows
        - first_centered_input
        * jnp.mean(first_normalized_rows * first_centered_input, axis=1, keepdims=True)
    )
    grad_terms = (
        grad_wquery,
        grad_wkey,
        grad_wvalue,
        grad_wout,
        jnp.concatenate([first_gain_gradient, second_gain_gradient]),
        grad_wgate,
        grad_wup,
        grad_wdown,
    )
    return (grad_input, tuple((member.reshape(piece_count, -1) for member in grad_terms)))


def on_device(boundary, doc_lens, w_query, w_key, w_value, w_out, gains, w_gate, w_up, w_down):
    sections = lax.axis_size("section")
    section_index = lax.axis_index("section")
    dp_count = lax.axis_size("dp")
    micro_count = boundary.shape[1]
    row_count = boundary.shape[2]
    model_width = boundary.shape[3]
    round_total = micro_count + sections - 1
    shards = (w_query, w_key, w_value, w_out, gains, w_gate, w_up, w_down)
    layouts = [
        doc_layout(doc_lens[micro_number, 0], row_count) for micro_number in range(micro_count)
    ]
    segments = jnp.stack([layout_item[0] for layout_item in layouts])
    positions = jnp.stack([layout_item[1] for layout_item in layouts])
    live_rows = jnp.stack([layout_item[2] for layout_item in layouts]).astype(jnp.float32)
    slot_ids = jnp.arange(row_count, dtype=jnp.int32)
    causal = slot_ids[None, :] <= slot_ids[:, None]

    def layout_for(micro_slot):
        segment = lax.dynamic_index_in_dim(segments, micro_slot, 0, keepdims=False)
        position = lax.dynamic_index_in_dim(positions, micro_slot, 0, keepdims=False)
        allowed = causal & (segment[:, None] == segment[None, :])
        cos_table, sine_table = rope_tables(position)
        return (allowed, cos_table, sine_table)

    matrices = unpack(
        (
            lax.all_gather(shards[0], "dp", axis=0, tiled=True),
            lax.all_gather(shards[1], "dp", axis=0, tiled=True),
            lax.all_gather(shards[2], "dp", axis=0, tiled=True),
            lax.all_gather(shards[3], "dp", axis=0, tiled=True),
            lax.all_gather(shards[4], "dp", axis=0, tiled=True),
            lax.all_gather(shards[5], "dp", axis=0, tiled=True),
            lax.all_gather(shards[6], "dp", axis=0, tiled=True),
            lax.all_gather(shards[7], "dp", axis=0, tiled=True),
        ),
        model_width,
    )
    own_inputs = boundary[0]
    results = jnp.zeros((micro_count, row_count, model_width), jnp.float32)
    outgoing = jnp.zeros((row_count, model_width), jnp.bfloat16)
    kept_rounds = []
    for round_index in range(round_total):
        if round_index > 0:
            incoming = passed_along(outgoing, "section", 1)
        else:
            incoming = jnp.zeros((row_count, model_width), jnp.bfloat16)
        micro_index = round_index - section_index
        is_valid = (micro_index >= 0) & (micro_index < micro_count)
        micro_slot = jnp.clip(micro_index, 0, micro_count - 1)
        layer_input_rows = jnp.where(
            section_index == 0,
            lax.dynamic_index_in_dim(own_inputs, micro_slot, 0, keepdims=False),
            incoming,
        )
        allowed, cos_table, sine_table = layout_for(micro_slot)
        layer_out, kept_values = forward_layer(
            layer_input_rows, matrices, allowed, cos_table, sine_table
        )
        kept_rounds.append(kept_values)
        finished = is_valid & (section_index == sections - 1)
        results = jnp.where(
            finished, lax.dynamic_update_index_in_dim(results, layer_out, micro_slot, 0), results
        )
        outgoing = layer_out.astype(jnp.bfloat16)
    stacked = jax.tree.map(lambda *members: jnp.stack(members), *kept_rounds)
    matrices_back = unpack(
        (
            lax.all_gather(shards[0], "dp", axis=0, tiled=True),
            lax.all_gather(shards[1], "dp", axis=0, tiled=True),
            lax.all_gather(shards[2], "dp", axis=0, tiled=True),
            lax.all_gather(shards[3], "dp", axis=0, tiled=True),
            lax.all_gather(shards[4], "dp", axis=0, tiled=True),
            lax.all_gather(shards[5], "dp", axis=0, tiled=True),
            lax.all_gather(shards[6], "dp", axis=0, tiled=True),
            lax.all_gather(shards[7], "dp", axis=0, tiled=True),
        ),
        model_width,
    )
    cotangent = boundary[sections - 1]
    totals = tuple(
        (jnp.zeros((dp_count, shard_piece.shape[1]), jnp.float32) for shard_piece in shards)
    )
    shares = tuple((jnp.zeros(shard_piece.shape, jnp.float32) for shard_piece in shards))
    back_outgoing = jnp.zeros((row_count, model_width), jnp.bfloat16)
    for round_index in range(round_total):
        if round_index > 0:
            arriving = passed_along(back_outgoing, "section", -1)
        else:
            arriving = jnp.zeros((row_count, model_width), jnp.bfloat16)
        micro_index = micro_count - 1 - round_index + (sections - 1 - section_index)
        is_valid = (micro_index >= 0) & (micro_index < micro_count)
        micro_slot = jnp.clip(micro_index, 0, micro_count - 1)
        kept_slot = jnp.clip(micro_index + section_index, 0, round_total - 1)
        kept_values = jax.tree.map(
            lambda member: lax.dynamic_index_in_dim(member, kept_slot, 0, keepdims=False), stacked
        )
        live_now = lax.dynamic_index_in_dim(live_rows, micro_slot, 0, keepdims=False)
        own_grad = (
            lax.dynamic_index_in_dim(cotangent, micro_slot, 0, keepdims=False).astype(jnp.float32)
            * live_now[:, None]
        )
        grad_output = jnp.where(
            section_index == sections - 1, own_grad, arriving.astype(jnp.float32)
        )
        grad_output = grad_output * is_valid.astype(jnp.float32)
        allowed, cos_table, sine_table = layout_for(micro_slot)
        grad_input, grad_terms = backward_layer(
            kept_values, matrices_back, allowed, cos_table, sine_table, grad_output, dp_count
        )
        totals = tuple(
            (left_term + right_term for left_term, right_term in zip(totals, grad_terms))
        )
        results = jnp.where(
            is_valid & (section_index == 0),
            lax.dynamic_update_index_in_dim(results, grad_input, micro_slot, 0),
            results,
        )
        back_outgoing = grad_input.astype(jnp.bfloat16)
    shares = add_sources(
        jax.tree.map(
            lambda part, own: part.astype(own.dtype),
            lax.all_to_all(as_sent(totals), "dp", split_axis=0, concat_axis=0, tiled=True),
            totals,
        )
    )
    return (
        results[None],
        shares[0],
        shares[1],
        shares[2],
        shares[3],
        shares[4],
        shares[5],
        shares[6],
        shares[7],
    )


def ring_place(chips):
    depth = chips // 2

    def place_of(chip):
        side = chip % 2
        level = chip // 2
        return level * (1 - side) + (chips - 1 - level) * side

    def chip_at(place):
        side = place // depth
        level = place * (1 - side) + (chips - 1 - place) * side
        return level * 2 + side

    return place_of, chip_at


def ring_setup(chips):
    place_of, chip_at = ring_place(chips)
    member = lax.axis_index("dp")
    core = member % 2
    place = place_of(member // 2)
    turn = 1 - 2 * core

    def at(offset, on_core):
        return chip_at((place + offset + 2 * chips) % chips) * 2 + on_core

    following = at(turn, core)
    preceding = at(-turn, core)
    sibling = member + turn
    barrier = pltpu.get_barrier_semaphore()
    for other in (following, preceding, sibling):
        pl.semaphore_signal(
            barrier, inc=1, device_id={"dp": other}, device_id_type=pl.DeviceIdType.MESH
        )
    pl.semaphore_wait(barrier, 3)
    return member, core, turn, at, following, sibling


def unit_of(width):
    return 1 if width % 128 == 0 else 2


def flat_part(line, width):
    span = unit_of(width) * width
    return pl.ds(pl.multiple_of(line * span, 128), span)


def rows_from(flat, stage, count, width, lane):
    unit = unit_of(width)

    def body(line):
        taken = flat[0:1, flat_part(line, width)].astype(jnp.float32)
        for u in range(unit):
            stage[pl.ds(line * unit + u, 1), lane : lane + width] = taken[
                :, u * width : (u + 1) * width
            ]

    pl.loop(0, count // unit)(body)


def rows_into(flat, stage, count, width, lane):
    unit = unit_of(width)

    def body(line):
        taken = [stage[pl.ds(line * unit + u, 1), lane : lane + width] for u in range(unit)]
        flat[0:1, flat_part(line, width)] = jnp.concatenate(taken, axis=1)

    pl.loop(0, count // unit)(body)


SEND_ORDER = (2, 3, 4, 0, 1)


def gather_kernel(
    chips,
    sizes,
    w_query,
    w_key,
    w_value,
    w_out,
    w_gate,
    w_up,
    w_down,
    gain_row,
    spread,
    *refs,
):
    piece, hidden_piece, model, kv_width, hidden = sizes
    wholes = refs[:5]
    pieces = refs[5:10]
    stage, keep_sem, ring_send, ring_recv, side_send, side_recv = refs[10:]
    heights = [whole.shape[0] // (2 * chips) for whole in wholes]
    room, wide = pieces[1].shape
    member, core, turn, at, following, sibling = ring_setup(chips)

    def rows(index, owner):
        height = heights[index]
        return wholes[index].at[pl.ds(pl.multiple_of(owner * height, 16), height), :]

    def ring_copy(index, source, owner, step):
        return pltpu.make_async_remote_copy(
            src_ref=source,
            dst_ref=rows(index, owner),
            send_sem=ring_send.at[step, index],
            recv_sem=ring_recv.at[step, index],
            device_id={"dp": following},
            device_id_type=pl.DeviceIdType.MESH,
        )

    def side_copy(index, source, owner, step):
        return pltpu.make_async_remote_copy(
            src_ref=source,
            dst_ref=rows(index, owner),
            send_sem=side_send.at[step, index],
            recv_sem=side_recv.at[step, index],
            device_id={"dp": sibling},
            device_id_type=pl.DeviceIdType.MESH,
        )

    def keep_copy(index):
        return pltpu.make_async_copy(pieces[index], rows(index, member), keep_sem.at[index])

    def build(index):
        if index == 0:
            stage[:room, : pieces[0].shape[1]] = jnp.zeros(pieces[0].shape, jnp.float32)
            rows_from(w_query, stage, piece, model, 0)
            rows_from(w_key, stage, piece, kv_width, model)
            rows_from(w_value, stage, piece, kv_width, model + kv_width)
            pieces[0][...] = stage[:room, : pieces[0].shape[1]].astype(jnp.bfloat16)
        elif index == 1:
            stage[:room, :model] = jnp.zeros((room, model), jnp.float32)
            rows_from(w_out, stage, piece, model, 0)
            spaced = dot(stage[:room, :model].astype(jnp.bfloat16), spread[...])
            line = lax.broadcasted_iota(jnp.int32, (room, wide), 0)
            spaced = spaced + jnp.where(line == piece, gain_row[...], 0.0)
            pieces[1][...] = spaced.astype(jnp.bfloat16)
        elif index == 4:
            rows_from(w_down, stage, hidden_piece, model, 0)
            pieces[4][...] = dot(
                stage[:hidden_piece, :model].astype(jnp.bfloat16), spread[...]
            ).astype(jnp.bfloat16)
        else:
            stage[:room, :hidden] = jnp.zeros((room, hidden), jnp.float32)
            rows_from(w_gate if index == 2 else w_up, stage, piece, hidden, 0)
            pieces[index][...] = stage[:room, :hidden].astype(jnp.bfloat16)

    for index in SEND_ORDER:
        build(index)
        ring_copy(index, pieces[index], member, 0).start()
        side_copy(index, pieces[index], member, 0).start()
        keep_copy(index).start()
    for step in range(1, chips):
        owner = at(-turn * step, core)
        for index in SEND_ORDER:
            ring_copy(index, rows(index, owner), owner, step - 1).wait_recv()
            if step < chips - 1:
                ring_copy(index, rows(index, owner), owner, step).start()
            side_copy(index, rows(index, owner), owner, step).start()
    for index in SEND_ORDER:
        keep_copy(index).wait()
    for step in range(chips):
        owner = at(-turn * step, core)
        theirs = at(turn * step, 1 - core)
        for index in SEND_ORDER:
            if step < chips - 1:
                ring_copy(index, rows(index, owner), owner, step).wait_send()
            side_copy(index, rows(index, owner), owner, step).wait_send()
            side_copy(index, rows(index, theirs), theirs, step).wait_recv()


def gather_all(operands, sizes, members, shapes):
    chips = members // 2
    piece, hidden_piece, model, kv_width, hidden = sizes
    vmem = pl.BlockSpec(memory_space=pltpu.VMEM)
    return pl.pallas_call(
        functools.partial(gather_kernel, chips, sizes),
        out_shape=tuple(
            jax.ShapeDtypeStruct((members * height, width), jnp.bfloat16)
            for height, width in shapes
        ),
        in_specs=[vmem] * len(operands),
        out_specs=tuple([pl.BlockSpec(memory_space=pl.ANY)] * 5),
        scratch_shapes=[pltpu.VMEM(shape, jnp.bfloat16) for shape in shapes]
        + [pltpu.VMEM((max(shapes[0][0], hidden_piece), max(hidden, shapes[0][1])), jnp.float32)]
        + [pltpu.SemaphoreType.DMA((5,))]
        + [pltpu.SemaphoreType.DMA((chips, 5))] * 4,
        compiler_params=pltpu.CompilerParams(
            collective_id=0, has_side_effects=True, vmem_limit_bytes=56 * 2**20
        ),
        name="gather_ring",
    )(*operands)


def scatter_kernel(chips, sizes, *refs):
    piece, hidden_piece, model, kv_width, hidden = sizes
    lefts = refs[:5]
    rights = refs[5:10]
    gain_terms, spread = refs[10:12]
    out_query, out_key, out_value, out_out, out_gains, out_gate, out_up, out_down = refs[12:20]
    owns, outs, sides, rings = refs[20:25], refs[25:30], refs[30:35], refs[35:40]
    stage, ring_send, ring_recv, side_send, side_recv = refs[40:]
    heights = [own.shape[1] for own in owns]
    widths = [own.shape[2] for own in owns]
    room = heights[1]
    member, core, turn, at, following, sibling = ring_setup(chips)

    def term(index, owner):
        height = heights[index]
        part = lefts[index][pl.ds(pl.multiple_of(owner * height, 16), height), :]
        value = dot(part, rights[index][...])
        if index == 1:
            line = lax.broadcasted_iota(jnp.int32, value.shape, 0)
            value = value + jnp.where(line == piece, gain_terms[owner], 0.0)
        return value.astype(jnp.bfloat16)

    def side_copy(index, step):
        return pltpu.make_async_remote_copy(
            src_ref=outs[index].at[step % 2],
            dst_ref=sides[index].at[step],
            send_sem=side_send.at[step, index],
            recv_sem=side_recv.at[step, index],
            device_id={"dp": sibling},
            device_id_type=pl.DeviceIdType.MESH,
        )

    def ring_copy(index, step):
        return pltpu.make_async_remote_copy(
            src_ref=owns[index].at[step],
            dst_ref=rings[index].at[step],
            send_sem=ring_send.at[step, index],
            recv_sem=ring_recv.at[step, index],
            device_id={"dp": following},
            device_id_type=pl.DeviceIdType.MESH,
        )

    def finish(index):
        if index == 0:
            rows_into(out_query, stage, piece, model, 0)
            rows_into(out_key, stage, piece, kv_width, model)
            rows_into(out_value, stage, piece, kv_width, model + kv_width)
        elif index == 2:
            rows_into(out_gate, stage, piece, hidden, 0)
        elif index == 3:
            rows_into(out_up, stage, piece, hidden, 0)
        else:
            height = heights[index]
            total = stage[:height, : widths[index]]
            if index == 1:
                out_gains[...] = total[piece : piece + 1, : out_gains.shape[1]]
            upper = total.astype(jnp.bfloat16)
            lower = (total - upper.astype(jnp.float32)).astype(jnp.bfloat16)
            stage[:height, :model] = dot_nt(upper, spread[...]) + dot_nt(lower, spread[...])
            if index == 1:
                rows_into(out_out, stage, piece, model, 0)
            else:
                rows_into(out_down, stage, hidden_piece, model, 0)

    for step in range(chips):
        theirs = at(turn * (step + 1), 1 - core)
        mine = at(-turn * (step + 1), core)
        for index in SEND_ORDER:
            if step > 1:
                side_copy(index, step - 2).wait_send()
            outs[index][step % 2] = term(index, theirs)
            side_copy(index, step).start()
            owns[index][step] = term(index, mine)
        for index in SEND_ORDER:
            side_copy(index, step).wait_recv()
            if step > 0:
                ring_copy(index, step - 1).wait_recv()

            def add(block):
                part = pl.ds(pl.multiple_of(block * 16, 16), 16)
                total = owns[index][step, part, :].astype(jnp.float32) + sides[index][
                    step, part, :
                ].astype(jnp.float32)
                if step > 0:
                    total = total + rings[index][step - 1, part, :].astype(jnp.float32)
                if step < chips - 1:
                    owns[index][step, part, :] = total.astype(jnp.bfloat16)
                else:
                    stage[part, : widths[index]] = total

            pl.loop(0, heights[index] // 16)(add)
            if step < chips - 1:
                ring_copy(index, step).start()
            else:
                finish(index)
    for step in range(chips):
        for index in SEND_ORDER:
            if step >= chips - 2:
                side_copy(index, step).wait_send()
            if step < chips - 1:
                ring_copy(index, step).wait_send()


def scatter_all(lefts, rights, gain_terms, spread, sizes, members):
    chips = members // 2
    piece, hidden_piece, model, kv_width, hidden = sizes
    shapes = [
        (left.shape[0] // members, right.shape[1]) for left, right in zip(lefts, rights)
    ]
    stacks = lambda depth: [pltpu.VMEM((depth, *shape), jnp.bfloat16) for shape in shapes]
    lengths = (
        piece * model,
        piece * kv_width,
        piece * kv_width,
        piece * model,
        -(-2 * piece // 128) * 128,
        piece * hidden,
        piece * hidden,
        hidden_piece * model,
    )
    vmem = pl.BlockSpec(memory_space=pltpu.VMEM)
    return pl.pallas_call(
        functools.partial(scatter_kernel, chips, sizes),
        out_shape=tuple(jax.ShapeDtypeStruct((1, length), jnp.float32) for length in lengths),
        in_specs=[vmem] * 12,
        out_specs=tuple([vmem] * 8),
        scratch_shapes=stacks(chips)
        + stacks(2)
        + stacks(chips)
        + stacks(chips - 1)
        + [pltpu.VMEM((max(shapes[0][0], hidden_piece), max(hidden, shapes[0][1])), jnp.float32)]
        + [pltpu.SemaphoreType.DMA((chips, 5))] * 4,
        compiler_params=pltpu.CompilerParams(
            collective_id=1, has_side_effects=True, vmem_limit_bytes=60 * 2**20
        ),
        name="scatter_ring",
    )(*lefts, *rights, gain_terms, spread)


def dot(left, right):
    return jnp.dot(left, right, preferred_element_type=jnp.float32)


def dot_nt(left, right):
    return lax.dot_general(
        left, right, (((1,), (1,)), ((), ())), preferred_element_type=jnp.float32
    )


def dot_tn(left, right):
    return lax.dot_general(
        left, right, (((0,), (0,)), ((), ())), preferred_element_type=jnp.float32
    )


def turn_heads(values, tables, sign):
    cos_table, early_sine, late_sine = tables
    half = HEAD // 2
    span = cos_table.shape[1]
    turned = []
    for start in range(0, values.shape[1], span):
        part = values[:, start : start + span]
        turned.append(
            part * cos_table[...]
            + sign
            * (
                pltpu.roll(part, span - half, 1) * early_sine[...]
                + pltpu.roll(part, half, 1) * late_sine[...]
            )
        )
    return jnp.concatenate(turned, axis=1)


def head_rows(source, micro, rows, first, group):
    return jnp.concatenate(
        [
            source[micro * rows : (micro + 1) * rows, (first + g) * HEAD : (first + g + 1) * HEAD]
            for g in range(group)
        ],
        axis=0,
    )


def forward_kernel(
    model,
    layout,
    stream,
    gains,
    bias,
    cos_table,
    early_sine,
    late_sine,
    spread,
    w_qkv,
    w_out,
    w_gate,
    w_up,
    w_down,
    layer_out,
    normed,
    turned,
    values,
    mixed_wide,
    middle,
    normed_two,
    gate_pre,
    up_pre,
    activation,
    mixed,
):
    heads, kv_heads, micro_count, rows = layout
    group = heads // kv_heads

    @pl.when(pl.program_id(0) == 0)
    def _():
        residual = stream[...]
        scale = lax.rsqrt(jnp.sum(residual * residual, axis=1, keepdims=True) / model + EPSILON)
        normed[...] = (residual * scale * gains[0:1, :]).astype(jnp.bfloat16)
        products = dot(normed[...], w_qkv[...])
        split = (heads + kv_heads) * HEAD
        turned[...] = turn_heads(
            products[:, :split], (cos_table, early_sine, late_sine), 1.0
        ).astype(jnp.bfloat16)
        values[...] = products[:, split:].astype(jnp.bfloat16)
        for micro in range(micro_count):
            part = slice(micro * rows, (micro + 1) * rows)
            for kv in range(kv_heads):
                query = head_rows(turned, micro, rows, kv * group, group)
                key = turned[part, (heads + kv) * HEAD : (heads + kv + 1) * HEAD]
                value = values[part, kv * HEAD : (kv + 1) * HEAD]
                scores = dot_nt(query, key) * HEAD ** (-0.5)
                scores = scores + jnp.concatenate([bias[micro]] * group, axis=0)
                exponent = jnp.exp(scores - jnp.max(scores, axis=1, keepdims=True))
                total = jnp.sum(exponent, axis=1, keepdims=True)
                probability = (exponent / total).astype(jnp.bfloat16)
                attended = dot(probability, value).astype(jnp.bfloat16)
                for g in range(group):
                    head = kv * group + g
                    mixed[part, head * HEAD : (head + 1) * HEAD] = attended[
                        g * rows : (g + 1) * rows, :
                    ]
        mixed_wide[...] = dot(mixed[...], spread[...]).astype(jnp.bfloat16)
        halfway = residual + dot(mixed_wide[...], w_out[...])
        middle[...] = halfway
        scale_two = lax.rsqrt(jnp.sum(halfway * halfway, axis=1, keepdims=True) / model + EPSILON)
        normed_two[...] = (halfway * scale_two * gains[1:2, :]).astype(jnp.bfloat16)
        layer_out[...] = halfway

    gate = dot(normed_two[...], w_gate[...])
    up = dot(normed_two[...], w_up[...])
    gate_pre[...] = gate
    up_pre[...] = up
    active = (gate * jax.nn.sigmoid(gate) * up).astype(jnp.bfloat16)
    activation[...] = active
    layer_out[...] += dot(active, w_down[...])


def full(array):
    return pl.BlockSpec(array.shape, lambda i: (0,) * len(array.shape))


def shape_of(rows, width, dtype):
    return jax.ShapeDtypeStruct((rows, width), dtype)


def tile_width(hidden):
    for width in (512, 256, 128):
        if hidden % width == 0:
            return width
    return hidden


def forward_fast(model, layout, stream, gains, bias, tables, spread, matrices):
    w_qkv, w_out, w_gate, w_up, w_down = matrices
    heads, kv_heads, micro_count, rows = layout
    tokens, wide = stream.shape
    hidden = w_gate.shape[1]
    tile = tile_width(hidden)
    split = (heads + kv_heads) * HEAD
    low, high = jnp.bfloat16, jnp.float32
    out_shape = (
        shape_of(tokens, wide, high),
        shape_of(tokens, wide, low),
        shape_of(tokens, split, low),
        shape_of(tokens, w_qkv.shape[1] - split, low),
        shape_of(tokens, wide, low),
        shape_of(tokens, wide, high),
        shape_of(tokens, wide, low),
        shape_of(tokens, hidden, high),
        shape_of(tokens, hidden, high),
        shape_of(tokens, hidden, low),
    )
    columns = lambda height: pl.BlockSpec((height, tile), lambda i: (0, i))
    ins = (stream, gains, bias, *tables, spread, w_qkv, w_out)
    return pl.pallas_call(
        functools.partial(forward_kernel, model, layout),
        grid=(hidden // tile,),
        out_shape=out_shape,
        in_specs=[full(member) for member in ins]
        + [columns(wide), columns(wide), pl.BlockSpec((tile, wide), lambda i: (i, 0))],
        out_specs=tuple([full(member) for member in out_shape[:7]] + [columns(tokens)] * 3),
        scratch_shapes=[pltpu.VMEM((tokens, heads * HEAD), low)],
        compiler_params=pltpu.CompilerParams(vmem_limit_bytes=56 * 2**20),
        cost_estimate=pl.CostEstimate(
            flops=20 * 2**28, bytes_accessed=30 * 2**20, transcendentals=2**20
        ),
        name="forward_layer",
    )(*ins, w_gate, w_up, w_down)


def backward_kernel(
    model,
    layout,
    cotangent,
    stream,
    gains,
    bias,
    cos_table,
    early_sine,
    late_sine,
    spread,
    turned,
    values,
    middle,
    w_qkv,
    w_out,
    gate_pre,
    up_pre,
    w_gate,
    w_up,
    w_down,
    grad_input,
    grad_low,
    grad_gains,
    grad_branch,
    grad_qkv,
    grad_gate,
    grad_up,
    norm_grad,
    grad_mixed,
    grad_turned,
    grad_values,
):
    heads, kv_heads, micro_count, rows = layout
    group = heads // kv_heads
    step = pl.program_id(0)

    @pl.when(step == 0)
    def _():
        grad_low[...] = cotangent[...].astype(jnp.bfloat16)
        norm_grad[...] = jnp.zeros_like(norm_grad)

    gate = gate_pre[...]
    grad_act = dot_nt(grad_low[...], w_down[...])
    sigmoid = jax.nn.sigmoid(gate)
    grad_gate[...] = (
        grad_act * up_pre[...] * sigmoid * (1.0 + gate * (1.0 - sigmoid))
    ).astype(jnp.bfloat16)
    grad_up[...] = (grad_act * gate * sigmoid).astype(jnp.bfloat16)
    norm_grad[...] += dot_nt(grad_gate[...], w_gate[...]) + dot_nt(grad_up[...], w_up[...])

    @pl.when(step == pl.num_programs(0) - 1)
    def _():
        halfway = middle[...]
        scale_two = lax.rsqrt(jnp.sum(halfway * halfway, axis=1, keepdims=True) / model + EPSILON)
        centered = halfway * scale_two
        gradient = norm_grad[...]
        grad_gains[1:2, :] = jnp.sum(gradient * centered, axis=0, keepdims=True)
        scaled = gradient * gains[1:2, :]
        grad_middle = cotangent[...] + scale_two * (
            scaled - centered * (jnp.sum(scaled * centered, axis=1, keepdims=True) / model)
        )
        grad_input[...] = grad_middle
        grad_branch[...] = grad_middle.astype(jnp.bfloat16)
        grad_wide = dot_nt(grad_branch[...], w_out[...]).astype(jnp.bfloat16)
        grad_mixed[...] = dot_nt(grad_wide, spread[...]).astype(jnp.bfloat16)
        grad_values[...] = jnp.zeros_like(grad_values)
        for micro in range(micro_count):
            part = slice(micro * rows, (micro + 1) * rows)
            for kv in range(kv_heads):
                query = head_rows(turned, micro, rows, kv * group, group)
                key = turned[part, (heads + kv) * HEAD : (heads + kv + 1) * HEAD]
                value = values[part, kv * HEAD : (kv + 1) * HEAD]
                grad_head = head_rows(grad_mixed, micro, rows, kv * group, group)
                scores = dot_nt(query, key) * HEAD ** (-0.5)
                scores = scores + jnp.concatenate([bias[micro]] * group, axis=0)
                exponent = jnp.exp(scores - jnp.max(scores, axis=1, keepdims=True))
                total = jnp.sum(exponent, axis=1, keepdims=True)
                probability = exponent / total
                grad_value = dot_tn(probability.astype(jnp.bfloat16), grad_head)
                grad_prob = dot_nt(grad_head, value)
                inner = jnp.sum(probability * grad_prob, axis=1, keepdims=True)
                grad_scores = (probability * (grad_prob - inner)).astype(jnp.bfloat16)
                grad_query = dot(grad_scores, key) * HEAD ** (-0.5)
                grad_key = dot_tn(grad_scores, query) * HEAD ** (-0.5)
                for g in range(group):
                    head = kv * group + g
                    grad_turned[part, head * HEAD : (head + 1) * HEAD] = grad_query[
                        g * rows : (g + 1) * rows, :
                    ]
                grad_turned[part, (heads + kv) * HEAD : (heads + kv + 1) * HEAD] = grad_key
                grad_values[part, kv * HEAD : (kv + 1) * HEAD] = grad_value
        split = (heads + kv_heads) * HEAD
        grad_qkv[:, :split] = turn_heads(
            grad_turned[...], (cos_table, early_sine, late_sine), -1.0
        ).astype(jnp.bfloat16)
        grad_qkv[:, split:] = grad_values[...].astype(jnp.bfloat16)
        first_gradient = dot_nt(grad_qkv[...], w_qkv[...])
        residual = stream[...]
        scale = lax.rsqrt(jnp.sum(residual * residual, axis=1, keepdims=True) / model + EPSILON)
        first_centered = residual * scale
        grad_gains[0:1, :] = jnp.sum(first_gradient * first_centered, axis=0, keepdims=True)
        first_scaled = first_gradient * gains[0:1, :]
        grad_input[...] += scale * (
            first_scaled
            - first_centered
            * (jnp.sum(first_scaled * first_centered, axis=1, keepdims=True) / model)
        )


def backward_fast(model, layout, cotangent, kept, gains, bias, tables, spread, matrices):
    w_qkv, w_out, w_gate, w_up, w_down = matrices
    stream, _, turned, values, _, middle, _, gate_pre, up_pre, _ = kept
    heads, kv_heads, micro_count, rows = layout
    tokens, wide = stream.shape
    hidden = w_gate.shape[1]
    tile = tile_width(hidden)
    split = (heads + kv_heads) * HEAD
    low, high = jnp.bfloat16, jnp.float32
    out_shape = (
        shape_of(tokens, wide, high),
        shape_of(tokens, wide, low),
        shape_of(2, wide, high),
        shape_of(tokens, wide, low),
        shape_of(tokens, w_qkv.shape[1], low),
        shape_of(tokens, hidden, low),
        shape_of(tokens, hidden, low),
    )
    columns = lambda height: pl.BlockSpec((height, tile), lambda i: (0, i))
    ins = (cotangent, stream, gains, bias, *tables, spread, turned, values, middle, w_qkv, w_out)
    return pl.pallas_call(
        functools.partial(backward_kernel, model, layout),
        grid=(hidden // tile,),
        out_shape=out_shape,
        in_specs=[full(member) for member in ins]
        + [columns(tokens)] * 2
        + [columns(wide), columns(wide), pl.BlockSpec((tile, wide), lambda i: (i, 0))],
        out_specs=tuple([full(member) for member in out_shape[:5]] + [columns(tokens)] * 2),
        scratch_shapes=[
            pltpu.VMEM((tokens, wide), high),
            pltpu.VMEM((tokens, heads * HEAD), low),
            pltpu.VMEM((tokens, split), high),
            pltpu.VMEM((tokens, w_qkv.shape[1] - split), high),
        ],
        compiler_params=pltpu.CompilerParams(vmem_limit_bytes=56 * 2**20),
        cost_estimate=pl.CostEstimate(
            flops=24 * 2**28, bytes_accessed=36 * 2**20, transcendentals=2**20
        ),
        name="backward_layer",
    )(*ins, gate_pre, up_pre, w_gate, w_up, w_down)


def widen(array, members, room):
    width = array.shape[-1] // members
    cut = array.reshape(array.shape[:-1] + (members, width))
    cut = jnp.pad(cut, [(0, 0)] * (cut.ndim - 1) + [(0, room - width)])
    return cut.reshape(array.shape[:-1] + (members * room,))


def narrow(array, members, width):
    room = array.shape[-1] // members
    cut = array.reshape(array.shape[:-1] + (members, room))[..., :width]
    return cut.reshape(array.shape[:-1] + (members * width,))


def lifted(array, height, width):
    return jnp.pad(array, [(0, height - array.shape[0]), (0, width - array.shape[1])])


def rows_room(model, members):
    return -(-(model // members + 1) // 16) * 16


def on_device_fast(boundary, doc_lens, w_query, w_key, w_value, w_out, gains, w_gate, w_up, w_down):
    section = lax.axis_index("section")
    members = lax.axis_size("dp")
    _, micro_count, rows, model = boundary.shape
    tokens = micro_count * rows
    piece = model // members
    room = rows_room(model, members)
    wide = room * members
    kv_width = w_key.size // piece
    hidden = w_gate.size // piece
    heads, kv_heads = model // HEAD, kv_width // HEAD
    layout = (heads, kv_heads, micro_count, rows)
    split = model + kv_width
    qkv_wide = split + -(-kv_width // 128) * 128
    hidden_piece = hidden // members
    gain_piece = gains.size

    feature = jnp.arange(model, dtype=jnp.int32)
    spread = (
        (feature // piece * room + feature % piece)[:, None]
        == jnp.arange(wide, dtype=jnp.int32)[None, :]
    ).astype(jnp.bfloat16)

    def spread_out(array):
        return jnp.dot(array, spread, preferred_element_type=jnp.float32).astype(array.dtype)

    sizes = (piece, hidden_piece, model, kv_width, hidden)
    gain_row = lifted(gains, 1, wide).astype(jnp.float32)
    gathered = gather_all(
        (w_query, w_key, w_value, w_out, w_gate, w_up, w_down, gain_row, spread),
        sizes,
        members,
        ((room, qkv_wide), (room, wide), (room, hidden), (room, hidden), (hidden_piece, wide)),
    )
    gain_rows = gathered[1].reshape(members, room, wide)[:, piece, :gain_piece]
    gain_pair = widen(gain_rows.reshape(2, model), members, room).astype(jnp.float32)

    layouts = [doc_layout(doc_lens[micro, 0], rows) for micro in range(micro_count)]
    segments = jnp.stack([item[0] for item in layouts])
    positions = jnp.concatenate([item[1] for item in layouts])
    live = jnp.concatenate([item[2] for item in layouts]).astype(jnp.float32)
    slot_ids = jnp.arange(rows, dtype=jnp.int32)
    allowed = (slot_ids[None, :] <= slot_ids[:, None])[None] & (
        segments[:, :, None] == segments[:, None, :]
    )
    bias = jnp.where(allowed, 0.0, -1e30).astype(jnp.float32)
    cos_table, sine_table = rope_tables(positions)
    first_half = (jnp.arange(HEAD, dtype=jnp.int32) < HEAD // 2)[None, :]
    tables = tuple(
        jnp.tile(table, (1, 128 // HEAD))
        for table in (
            cos_table,
            jnp.where(first_half, -sine_table, 0.0),
            jnp.where(first_half, 0.0, sine_table),
        )
    )

    own = spread_out(boundary.reshape(tokens, model))
    stream_zero = own.astype(jnp.float32)
    shared = (gain_pair, bias, tables, spread, gathered)
    kept_zero = forward_fast(model, layout, stream_zero, *shared)
    relayed = passed_along(kept_zero[0].astype(jnp.bfloat16), "section", 1)
    stream_one = relayed.astype(jnp.float32)
    kept_one = forward_fast(model, layout, stream_one, *shared)

    cotangent = jnp.where(section == 1, stream_zero * live[:, None], 0.0)
    back_one = backward_fast(model, layout, cotangent, (stream_one,) + tuple(kept_one[1:]), *shared)
    returned = passed_along(back_one[0].astype(jnp.bfloat16), "section", -1).astype(jnp.float32)
    back_zero = backward_fast(
        model, layout, returned, (stream_zero,) + tuple(kept_zero[1:]), *shared
    )

    pick = lambda early, late: jnp.where(section == 0, early, late)
    results = narrow(pick(back_zero[0], kept_one[0]), members, piece)
    normed, mixed, normed_two, activation = (
        pick(kept_zero[at], kept_one[at]).T for at in (1, 4, 6, 9)
    )
    _, grad_low, grad_gains, grad_branch, grad_qkv, grad_gate, grad_up = (
        pick(early, late) for early, late in zip(back_zero, back_one)
    )
    gain_terms = narrow(grad_gains, members, piece).reshape(members, 1, gain_piece)
    gain_terms = jnp.pad(gain_terms, ((0, 0), (0, 0), (0, wide - gain_piece)))
    shares = scatter_all(
        (normed, mixed, normed_two, normed_two, activation),
        (grad_qkv, grad_branch, grad_gate, grad_up, grad_low),
        gain_terms,
        spread,
        sizes,
        members,
    )
    return (
        results.reshape(1, micro_count, rows, model),
        *shares[:4],
        shares[4][:, :gain_piece],
        *shares[5:],
    )


def rows_fit(mesh, model, hidden):
    members = mesh.shape["dp"]
    return (
        mesh.shape["section"] == 2
        and members >= 6
        and members % 4 == 0
        and model % members == 0
        and hidden % members == 0
        and (hidden // members) % 16 == 0
        and hidden % 128 == 0
        and model % 64 == 0
        and (model // members) % 2 == 0
        and (rows_room(model, members) * members) % 128 == 0
    )


def solution(mesh):
    placed = (
        P("section", None, "dp", None),
        P(None, "dp", None),
        P("section", "dp"),
        P("section", "dp"),
        P("section", "dp"),
        P("section", "dp"),
        P("section", "dp"),
        P("section", "dp"),
        P("section", "dp"),
        P("section", "dp"),
    )

    def chosen(*operands):
        model = operands[0].shape[3]
        hidden = operands[7].size * mesh.shape["dp"] // model
        return (on_device_fast if rows_fit(mesh, model, hidden) else on_device)(*operands)

    return jax.shard_map(
        chosen,
        mesh=mesh,
        in_specs=placed,
        out_specs=(
            P("section", None, "dp", None),
            P("section", "dp"),
            P("section", "dp"),
            P("section", "dp"),
            P("section", "dp"),
            P("section", "dp"),
            P("section", "dp"),
            P("section", "dp"),
            P("section", "dp"),
        ),
        check_vma=False,
    )
```

```python
import functools

import jax
import jax.numpy as jnp
from jax import lax
from jax.experimental import pallas as pl
from jax.experimental.pallas import tpu as pltpu
from jax.sharding import PartitionSpec as P

HEAD = 64


EPSILON = 1e-05
ROPE_BASE = 100000.0


def passed_along(x, axis, by):
    devices = lax.axis_size(axis)
    pairs = [(i, i + by) for i in range(devices) if 0 <= i + by < devices]
    return lax.ppermute(x, axis, pairs)


def as_sent(x):
    return jax.tree.map(lambda a: a.astype(jnp.bfloat16) if a.dtype == jnp.float32 else a, x)


def doc_layout(lengths, slot_count):
    doc_ends = jnp.cumsum(lengths, dtype=jnp.int32)
    doc_starts = doc_ends - lengths
    doc_count = lengths.shape[0]
    slot_ids = jnp.arange(slot_count, dtype=jnp.int32)
    segment = jnp.sum(
        (slot_ids[:, None] >= doc_ends[None, :]).astype(jnp.int32), axis=1, dtype=jnp.int32
    )
    start_table = jnp.concatenate([doc_starts, doc_ends[doc_count - 1 :]])
    picked = segment[:, None] == jnp.arange(doc_count + 1, dtype=jnp.int32)[None, :]
    first_slot = jnp.sum(jnp.where(picked, start_table[None, :], 0), axis=1, dtype=jnp.int32)
    return (segment, slot_ids - first_slot, segment < doc_count)


def rope_tables(position):
    half_width = HEAD // 2
    inverse_freq = ROPE_BASE ** (-(jnp.arange(half_width, dtype=jnp.float32) * (2.0 / HEAD)))
    angles = position.astype(jnp.float32)[:, None] * inverse_freq[None, :]
    cos_table = jnp.cos(angles)
    sine_table = jnp.sin(angles)
    return (
        jnp.concatenate([cos_table, cos_table], axis=1),
        jnp.concatenate([sine_table, sine_table], axis=1),
    )


def rotate(values, cos_table, sine_table):
    half_width = values.shape[-1] // 2
    turned = jnp.concatenate([-values[..., half_width:], values[..., :half_width]], axis=-1)
    return values * cos_table[:, None, :] + turned * sine_table[:, None, :]


def unrotate(values, cos_table, sine_table):
    half_width = values.shape[-1] // 2
    sined = values * sine_table[:, None, :]
    turned = jnp.concatenate([sined[..., half_width:], -sined[..., :half_width]], axis=-1)
    return values * cos_table[:, None, :] + turned


def unpack(gathered, model_width):
    kv_width = gathered[1].size // model_width
    hidden_width = gathered[5].size // model_width
    return (
        gathered[0].reshape(model_width, model_width),
        gathered[1].reshape(model_width, kv_width),
        gathered[2].reshape(model_width, kv_width),
        gathered[3].reshape(model_width, model_width),
        gathered[4].reshape(2 * model_width),
        gathered[5].reshape(model_width, hidden_width),
        gathered[6].reshape(model_width, hidden_width),
        gathered[7].reshape(hidden_width, model_width),
    )


def add_sources(received):
    return tuple((jnp.sum(member, axis=0, keepdims=True) for member in received))


def forward_layer(layer_input_rows, matrices, allowed, cos_table, sine_table):
    w_query, w_key, w_value, w_out, gain_pair, w_gate, w_up, w_down = matrices
    row_count, model_width = layer_input_rows.shape
    kv_count = w_key.shape[1] // HEAD
    group_size = w_query.shape[1] // w_key.shape[1]
    score_scale = HEAD ** (-0.5)
    gain_one = gain_pair[:model_width].astype(jnp.float32)
    gain_two = gain_pair[model_width:].astype(jnp.float32)
    residual = layer_input_rows.astype(jnp.float32)
    first_inverse_scale = lax.rsqrt(jnp.mean(residual * residual, axis=1, keepdims=True) + EPSILON)
    normed = (residual * first_inverse_scale * gain_one).astype(jnp.bfloat16)
    queries = rotate(
        jnp.dot(normed, w_query, preferred_element_type=jnp.float32).reshape(row_count, -1, HEAD),
        cos_table,
        sine_table,
    ).astype(jnp.bfloat16)
    keys_turned = rotate(
        jnp.dot(normed, w_key, preferred_element_type=jnp.float32).reshape(
            row_count, kv_count, HEAD
        ),
        cos_table,
        sine_table,
    ).astype(jnp.bfloat16)
    values_low = jnp.dot(normed, w_value, preferred_element_type=jnp.float32).astype(jnp.bfloat16)
    heads_query = queries.reshape(row_count, kv_count, group_size, HEAD).transpose(1, 0, 2, 3)
    heads_key = keys_turned.transpose(1, 0, 2)
    heads_value = values_low.reshape(row_count, kv_count, HEAD).transpose(1, 0, 2)

    def one_head(operands):
        head_query, head_key, head_value = operands
        scores = (
            jnp.einsum("qgd,td->gqt", head_query, head_key, preferred_element_type=jnp.float32)
            * score_scale
        )
        scores = jnp.where(allowed[None], scores, -1e30)
        row_top = jnp.max(scores, axis=2, keepdims=True)
        exponent = jnp.exp(scores - row_top)
        row_total = jnp.sum(exponent, axis=2, keepdims=True)
        probability = (exponent / row_total).astype(jnp.bfloat16)
        attended = jnp.einsum(
            "gqt,td->qgd", probability, head_value, preferred_element_type=jnp.float32
        )
        return (attended, (row_top + jnp.log(row_total))[..., 0])

    attended, log_total = lax.map(one_head, (heads_query, heads_key, heads_value))
    mixed_low = attended.transpose(1, 0, 2, 3).reshape(row_count, model_width).astype(jnp.bfloat16)
    midway_hidden = residual + jnp.dot(mixed_low, w_out, preferred_element_type=jnp.float32)
    second_inverse_scale = lax.rsqrt(
        jnp.mean(midway_hidden * midway_hidden, axis=1, keepdims=True) + EPSILON
    )
    normed_two = (midway_hidden * second_inverse_scale * gain_two).astype(jnp.bfloat16)
    gate_pre = jnp.dot(normed_two, w_gate, preferred_element_type=jnp.float32)
    up_pre = jnp.dot(normed_two, w_up, preferred_element_type=jnp.float32)
    activation = (jax.nn.silu(gate_pre) * up_pre).astype(jnp.bfloat16)
    layer_out = midway_hidden + jnp.dot(activation, w_down, preferred_element_type=jnp.float32)
    kept_values = (
        layer_input_rows,
        normed,
        queries,
        keys_turned,
        values_low,
        log_total,
        mixed_low,
        midway_hidden,
        first_inverse_scale,
        second_inverse_scale,
        normed_two,
        gate_pre,
        up_pre,
        activation,
    )
    return (layer_out, kept_values)


def backward_layer(kept_values, matrices, allowed, cos_table, sine_table, grad_output, piece_count):
    (
        layer_input_rows,
        normed,
        queries,
        keys_turned,
        values_low,
        log_total,
        mixed_low,
        midway_hidden,
        first_inverse_scale,
        second_inverse_scale,
        normed_two,
        gate_pre,
        up_pre,
        activation,
    ) = kept_values
    w_query, w_key, w_value, w_out, gain_pair, w_gate, w_up, w_down = matrices
    row_count, model_width = layer_input_rows.shape
    kv_count = w_key.shape[1] // HEAD
    group_size = w_query.shape[1] // w_key.shape[1]
    score_scale = HEAD ** (-0.5)
    gain_one = gain_pair[:model_width].astype(jnp.float32)
    gain_two = gain_pair[model_width:].astype(jnp.float32)
    grad_low = grad_output.astype(jnp.bfloat16)
    grad_wdown = jnp.einsum("nf,nd->fd", activation, grad_low, preferred_element_type=jnp.float32)
    grad_act = jnp.einsum("nd,fd->nf", grad_low, w_down, preferred_element_type=jnp.float32)
    sigmoid_gate = jax.nn.sigmoid(gate_pre)
    grad_gate_pre = (
        grad_act * up_pre * sigmoid_gate * (1.0 + gate_pre * (1.0 - sigmoid_gate))
    ).astype(jnp.bfloat16)
    grad_up_pre = (grad_act * gate_pre * sigmoid_gate).astype(jnp.bfloat16)
    grad_wgate = jnp.einsum(
        "nd,nf->df", normed_two, grad_gate_pre, preferred_element_type=jnp.float32
    )
    grad_wup = jnp.einsum("nd,nf->df", normed_two, grad_up_pre, preferred_element_type=jnp.float32)
    second_norm_gradient = jnp.einsum(
        "nf,df->nd", grad_gate_pre, w_gate, preferred_element_type=jnp.float32
    ) + jnp.einsum("nf,df->nd", grad_up_pre, w_up, preferred_element_type=jnp.float32)
    second_centered_input = midway_hidden * second_inverse_scale
    second_normalized_rows = second_norm_gradient * gain_two
    second_gain_gradient = jnp.sum(second_norm_gradient * second_centered_input, axis=0)
    grad_middle = grad_output + second_inverse_scale * (
        second_normalized_rows
        - second_centered_input
        * jnp.mean(second_normalized_rows * second_centered_input, axis=1, keepdims=True)
    )
    grad_branch = grad_middle.astype(jnp.bfloat16)
    grad_wout = jnp.einsum("nd,ne->de", mixed_low, grad_branch, preferred_element_type=jnp.float32)
    grad_mixed = jnp.einsum(
        "ne,de->nd", grad_branch, w_out, preferred_element_type=jnp.float32
    ).astype(jnp.bfloat16)
    heads_query = queries.reshape(row_count, kv_count, group_size, HEAD).transpose(1, 0, 2, 3)
    heads_key = keys_turned.transpose(1, 0, 2)
    heads_value = values_low.reshape(row_count, kv_count, HEAD).transpose(1, 0, 2)
    heads_grad = grad_mixed.reshape(row_count, kv_count, group_size, HEAD).transpose(1, 0, 2, 3)

    def one_back(operands):
        head_query, head_key, head_value, head_lse, head_grad = operands
        scores = (
            jnp.einsum("qgd,td->gqt", head_query, head_key, preferred_element_type=jnp.float32)
            * score_scale
        )
        scores = jnp.where(allowed[None], scores, -1e30)
        probability = jnp.exp(scores - head_lse[..., None])
        grad_vhead = jnp.einsum(
            "gqt,qgd->td",
            probability.astype(jnp.bfloat16),
            head_grad,
            preferred_element_type=jnp.float32,
        )
        grad_prob = jnp.einsum(
            "qgd,td->gqt", head_grad, head_value, preferred_element_type=jnp.float32
        )
        grad_scores = (
            probability * (grad_prob - jnp.sum(probability * grad_prob, axis=2, keepdims=True))
        ).astype(jnp.bfloat16)
        grad_qhead = (
            jnp.einsum("gqt,td->qgd", grad_scores, head_key, preferred_element_type=jnp.float32)
            * score_scale
        )
        grad_khead = (
            jnp.einsum("gqt,qgd->td", grad_scores, head_query, preferred_element_type=jnp.float32)
            * score_scale
        )
        return (grad_qhead, grad_khead, grad_vhead)

    grad_qheads, grad_kheads, grad_vheads = lax.map(
        one_back, (heads_query, heads_key, heads_value, log_total, heads_grad)
    )
    grad_queries = (
        unrotate(
            grad_qheads.transpose(1, 0, 2, 3).reshape(row_count, -1, HEAD), cos_table, sine_table
        )
        .reshape(row_count, -1)
        .astype(jnp.bfloat16)
    )
    grad_keys = (
        unrotate(grad_kheads.transpose(1, 0, 2), cos_table, sine_table)
        .reshape(row_count, -1)
        .astype(jnp.bfloat16)
    )
    grad_values = grad_vheads.transpose(1, 0, 2).reshape(row_count, -1).astype(jnp.bfloat16)
    grad_wquery = jnp.einsum("nd,ne->de", normed, grad_queries, preferred_element_type=jnp.float32)
    grad_wkey = jnp.einsum("nd,ne->de", normed, grad_keys, preferred_element_type=jnp.float32)
    grad_wvalue = jnp.einsum("nd,ne->de", normed, grad_values, preferred_element_type=jnp.float32)
    first_norm_gradient = (
        jnp.einsum("ne,de->nd", grad_queries, w_query, preferred_element_type=jnp.float32)
        + jnp.einsum("ne,de->nd", grad_keys, w_key, preferred_element_type=jnp.float32)
        + jnp.einsum("ne,de->nd", grad_values, w_value, preferred_element_type=jnp.float32)
    )
    first_centered_input = layer_input_rows.astype(jnp.float32) * first_inverse_scale
    first_normalized_rows = first_norm_gradient * gain_one
    first_gain_gradient = jnp.sum(first_norm_gradient * first_centered_input, axis=0)
    grad_input = grad_middle + first_inverse_scale * (
        first_normalized_rows
        - first_centered_input
        * jnp.mean(first_normalized_rows * first_centered_input, axis=1, keepdims=True)
    )
    grad_terms = (
        grad_wquery,
        grad_wkey,
        grad_wvalue,
        grad_wout,
        jnp.concatenate([first_gain_gradient, second_gain_gradient]),
        grad_wgate,
        grad_wup,
        grad_wdown,
    )
    return (grad_input, tuple((member.reshape(piece_count, -1) for member in grad_terms)))


def on_device(boundary, doc_lens, w_query, w_key, w_value, w_out, gains, w_gate, w_up, w_down):
    sections = lax.axis_size("section")
    section_index = lax.axis_index("section")
    dp_count = lax.axis_size("dp")
    micro_count = boundary.shape[1]
    row_count = boundary.shape[2]
    model_width = boundary.shape[3]
    round_total = micro_count + sections - 1
    shards = (w_query, w_key, w_value, w_out, gains, w_gate, w_up, w_down)
    layouts = [
        doc_layout(doc_lens[micro_number, 0], row_count) for micro_number in range(micro_count)
    ]
    segments = jnp.stack([layout_item[0] for layout_item in layouts])
    positions = jnp.stack([layout_item[1] for layout_item in layouts])
    live_rows = jnp.stack([layout_item[2] for layout_item in layouts]).astype(jnp.float32)
    slot_ids = jnp.arange(row_count, dtype=jnp.int32)
    causal = slot_ids[None, :] <= slot_ids[:, None]

    def layout_for(micro_slot):
        segment = lax.dynamic_index_in_dim(segments, micro_slot, 0, keepdims=False)
        position = lax.dynamic_index_in_dim(positions, micro_slot, 0, keepdims=False)
        allowed = causal & (segment[:, None] == segment[None, :])
        cos_table, sine_table = rope_tables(position)
        return (allowed, cos_table, sine_table)

    matrices = unpack(
        (
            lax.all_gather(shards[0], "dp", axis=0, tiled=True),
            lax.all_gather(shards[1], "dp", axis=0, tiled=True),
            lax.all_gather(shards[2], "dp", axis=0, tiled=True),
            lax.all_gather(shards[3], "dp", axis=0, tiled=True),
            lax.all_gather(shards[4], "dp", axis=0, tiled=True),
            lax.all_gather(shards[5], "dp", axis=0, tiled=True),
            lax.all_gather(shards[6], "dp", axis=0, tiled=True),
            lax.all_gather(shards[7], "dp", axis=0, tiled=True),
        ),
        model_width,
    )
    own_inputs = boundary[0]
    results = jnp.zeros((micro_count, row_count, model_width), jnp.float32)
    outgoing = jnp.zeros((row_count, model_width), jnp.bfloat16)
    kept_rounds = []
    for round_index in range(round_total):
        if round_index > 0:
            incoming = passed_along(outgoing, "section", 1)
        else:
            incoming = jnp.zeros((row_count, model_width), jnp.bfloat16)
        micro_index = round_index - section_index
        is_valid = (micro_index >= 0) & (micro_index < micro_count)
        micro_slot = jnp.clip(micro_index, 0, micro_count - 1)
        layer_input_rows = jnp.where(
            section_index == 0,
            lax.dynamic_index_in_dim(own_inputs, micro_slot, 0, keepdims=False),
            incoming,
        )
        allowed, cos_table, sine_table = layout_for(micro_slot)
        layer_out, kept_values = forward_layer(
            layer_input_rows, matrices, allowed, cos_table, sine_table
        )
        kept_rounds.append(kept_values)
        finished = is_valid & (section_index == sections - 1)
        results = jnp.where(
            finished, lax.dynamic_update_index_in_dim(results, layer_out, micro_slot, 0), results
        )
        outgoing = layer_out.astype(jnp.bfloat16)
    stacked = jax.tree.map(lambda *members: jnp.stack(members), *kept_rounds)
    matrices_back = unpack(
        (
            lax.all_gather(shards[0], "dp", axis=0, tiled=True),
            lax.all_gather(shards[1], "dp", axis=0, tiled=True),
            lax.all_gather(shards[2], "dp", axis=0, tiled=True),
            lax.all_gather(shards[3], "dp", axis=0, tiled=True),
            lax.all_gather(shards[4], "dp", axis=0, tiled=True),
            lax.all_gather(shards[5], "dp", axis=0, tiled=True),
            lax.all_gather(shards[6], "dp", axis=0, tiled=True),
            lax.all_gather(shards[7], "dp", axis=0, tiled=True),
        ),
        model_width,
    )
    cotangent = boundary[sections - 1]
    totals = tuple(
        (jnp.zeros((dp_count, shard_piece.shape[1]), jnp.float32) for shard_piece in shards)
    )
    shares = tuple((jnp.zeros(shard_piece.shape, jnp.float32) for shard_piece in shards))
    back_outgoing = jnp.zeros((row_count, model_width), jnp.bfloat16)
    for round_index in range(round_total):
        if round_index > 0:
            arriving = passed_along(back_outgoing, "section", -1)
        else:
            arriving = jnp.zeros((row_count, model_width), jnp.bfloat16)
        micro_index = micro_count - 1 - round_index + (sections - 1 - section_index)
        is_valid = (micro_index >= 0) & (micro_index < micro_count)
        micro_slot = jnp.clip(micro_index, 0, micro_count - 1)
        kept_slot = jnp.clip(micro_index + section_index, 0, round_total - 1)
        kept_values = jax.tree.map(
            lambda member: lax.dynamic_index_in_dim(member, kept_slot, 0, keepdims=False), stacked
        )
        live_now = lax.dynamic_index_in_dim(live_rows, micro_slot, 0, keepdims=False)
        own_grad = (
            lax.dynamic_index_in_dim(cotangent, micro_slot, 0, keepdims=False).astype(jnp.float32)
            * live_now[:, None]
        )
        grad_output = jnp.where(
            section_index == sections - 1, own_grad, arriving.astype(jnp.float32)
        )
        grad_output = grad_output * is_valid.astype(jnp.float32)
        allowed, cos_table, sine_table = layout_for(micro_slot)
        grad_input, grad_terms = backward_layer(
            kept_values, matrices_back, allowed, cos_table, sine_table, grad_output, dp_count
        )
        totals = tuple(
            (left_term + right_term for left_term, right_term in zip(totals, grad_terms))
        )
        results = jnp.where(
            is_valid & (section_index == 0),
            lax.dynamic_update_index_in_dim(results, grad_input, micro_slot, 0),
            results,
        )
        back_outgoing = grad_input.astype(jnp.bfloat16)
    shares = add_sources(
        jax.tree.map(
            lambda part, own: part.astype(own.dtype),
            lax.all_to_all(as_sent(totals), "dp", split_axis=0, concat_axis=0, tiled=True),
            totals,
        )
    )
    return (
        results[None],
        shares[0],
        shares[1],
        shares[2],
        shares[3],
        shares[4],
        shares[5],
        shares[6],
        shares[7],
    )


def ring_place(chips):
    depth = chips // 2

    def place_of(chip):
        side = chip % 2
        level = chip // 2
        return level * (1 - side) + (chips - 1 - level) * side

    def chip_at(place):
        side = place // depth
        level = place * (1 - side) + (chips - 1 - place) * side
        return level * 2 + side

    return place_of, chip_at


def ring_setup(chips):
    place_of, chip_at = ring_place(chips)
    member = lax.axis_index("dp")
    core = member % 2
    place = place_of(member // 2)
    turn = 1 - 2 * core

    def at(offset, on_core):
        return chip_at((place + offset + 2 * chips) % chips) * 2 + on_core

    following = at(turn, core)
    preceding = at(-turn, core)
    sibling = member + turn
    barrier = pltpu.get_barrier_semaphore()
    for other in (following, preceding, sibling):
        pl.semaphore_signal(
            barrier, inc=1, device_id={"dp": other}, device_id_type=pl.DeviceIdType.MESH
        )
    pl.semaphore_wait(barrier, 3)
    return member, core, turn, at, following, sibling


def unit_of(width):
    return 1 if width % 128 == 0 else 2


def flat_part(line, width):
    span = unit_of(width) * width
    return pl.ds(pl.multiple_of(line * span, 128), span)


def rows_from(flat, stage, count, width, lane):
    unit = unit_of(width)

    def body(line):
        taken = flat[0:1, flat_part(line, width)].astype(jnp.float32)
        for u in range(unit):
            stage[pl.ds(line * unit + u, 1), lane : lane + width] = taken[
                :, u * width : (u + 1) * width
            ]

    pl.loop(0, count // unit)(body)


def rows_into(flat, stage, count, width, lane):
    unit = unit_of(width)

    def body(line):
        taken = [stage[pl.ds(line * unit + u, 1), lane : lane + width] for u in range(unit)]
        flat[0:1, flat_part(line, width)] = jnp.concatenate(taken, axis=1)

    pl.loop(0, count // unit)(body)


SEND_ORDER = (2, 3, 4, 0, 1)


def gather_kernel(
    chips,
    sizes,
    w_query,
    w_key,
    w_value,
    w_out,
    w_gate,
    w_up,
    w_down,
    gain_row,
    spread,
    *refs,
):
    piece, hidden_piece, model, kv_width, hidden = sizes
    wholes = refs[:5]
    pieces = refs[5:10]
    stage, keep_sem, ring_send, ring_recv, side_send, side_recv = refs[10:]
    heights = [whole.shape[0] // (2 * chips) for whole in wholes]
    room, wide = pieces[1].shape
    member, core, turn, at, following, sibling = ring_setup(chips)

    def rows(index, owner):
        height = heights[index]
        return wholes[index].at[pl.ds(pl.multiple_of(owner * height, 16), height), :]

    def ring_copy(index, source, owner, step):
        return pltpu.make_async_remote_copy(
            src_ref=source,
            dst_ref=rows(index, owner),
            send_sem=ring_send.at[step, index],
            recv_sem=ring_recv.at[step, index],
            device_id={"dp": following},
            device_id_type=pl.DeviceIdType.MESH,
        )

    def side_copy(index, source, owner, step):
        return pltpu.make_async_remote_copy(
            src_ref=source,
            dst_ref=rows(index, owner),
            send_sem=side_send.at[step, index],
            recv_sem=side_recv.at[step, index],
            device_id={"dp": sibling},
            device_id_type=pl.DeviceIdType.MESH,
        )

    def keep_copy(index):
        return pltpu.make_async_copy(pieces[index], rows(index, member), keep_sem.at[index])

    def build(index):
        if index == 0:
            stage[:room, : pieces[0].shape[1]] = jnp.zeros(pieces[0].shape, jnp.float32)
            rows_from(w_query, stage, piece, model, 0)
            rows_from(w_key, stage, piece, kv_width, model)
            rows_from(w_value, stage, piece, kv_width, model + kv_width)
            pieces[0][...] = stage[:room, : pieces[0].shape[1]].astype(jnp.bfloat16)
        elif index == 1:
            stage[:room, :model] = jnp.zeros((room, model), jnp.float32)
            rows_from(w_out, stage, piece, model, 0)
            spaced = dot(stage[:room, :model].astype(jnp.bfloat16), spread[...])
            line = lax.broadcasted_iota(jnp.int32, (room, wide), 0)
            spaced = spaced + jnp.where(line == piece, gain_row[...], 0.0)
            pieces[1][...] = spaced.astype(jnp.bfloat16)
        elif index == 4:
            rows_from(w_down, stage, hidden_piece, model, 0)
            pieces[4][...] = dot(
                stage[:hidden_piece, :model].astype(jnp.bfloat16), spread[...]
            ).astype(jnp.bfloat16)
        else:
            stage[:room, :hidden] = jnp.zeros((room, hidden), jnp.float32)
            rows_from(w_gate if index == 2 else w_up, stage, piece, hidden, 0)
            pieces[index][...] = stage[:room, :hidden].astype(jnp.bfloat16)

    for index in SEND_ORDER:
        build(index)
        ring_copy(index, pieces[index], member, 0).start()
        side_copy(index, pieces[index], member, 0).start()
        keep_copy(index).start()
    for step in range(1, chips):
        owner = at(-turn * step, core)
        for index in SEND_ORDER:
            ring_copy(index, rows(index, owner), owner, step - 1).wait_recv()
            if step < chips - 1:
                ring_copy(index, rows(index, owner), owner, step).start()
            side_copy(index, rows(index, owner), owner, step).start()
    for index in SEND_ORDER:
        keep_copy(index).wait()
    for step in range(chips):
        owner = at(-turn * step, core)
        theirs = at(turn * step, 1 - core)
        for index in SEND_ORDER:
            if step < chips - 1:
                ring_copy(index, rows(index, owner), owner, step).wait_send()
            side_copy(index, rows(index, owner), owner, step).wait_send()
            side_copy(index, rows(index, theirs), theirs, step).wait_recv()


def gather_all(operands, sizes, members, shapes):
    chips = members // 2
    piece, hidden_piece, model, kv_width, hidden = sizes
    vmem = pl.BlockSpec(memory_space=pltpu.VMEM)
    return pl.pallas_call(
        functools.partial(gather_kernel, chips, sizes),
        out_shape=tuple(
            jax.ShapeDtypeStruct((members * height, width), jnp.bfloat16)
            for height, width in shapes
        ),
        in_specs=[vmem] * len(operands),
        out_specs=tuple([pl.BlockSpec(memory_space=pl.ANY)] * 5),
        scratch_shapes=[pltpu.VMEM(shape, jnp.bfloat16) for shape in shapes]
        + [pltpu.VMEM((max(shapes[0][0], hidden_piece), max(hidden, shapes[0][1])), jnp.float32)]
        + [pltpu.SemaphoreType.DMA((5,))]
        + [pltpu.SemaphoreType.DMA((chips, 5))] * 4,
        compiler_params=pltpu.CompilerParams(
            collective_id=0, has_side_effects=True, vmem_limit_bytes=56 * 2**20
        ),
        name="gather_ring",
    )(*operands)


LEFT_OF = (0, 1, 2, 2, 3)


def scatter_kernel(chips, sizes, micro_count, *refs):
    piece = sizes[0]
    fetched = 9
    choices = 2 * micro_count
    sources = [refs[slot * choices : (slot + 1) * choices] for slot in range(fetched)]
    refs = refs[fetched * choices :]
    gain_terms = refs[0]
    totals = refs[1:6]
    loaded, lefts = refs[6:15], refs[15:19]
    owns, outs, sides, rings = refs[19:24], refs[24:29], refs[29:34], refs[34:39]
    load_sem, ring_send, ring_recv, side_send, side_recv = refs[39:]
    rights = loaded[4:]
    heights = [own.shape[1] for own in owns]
    section = lax.axis_index("section")
    member, core, turn, at, following, sibling = ring_setup(chips)

    def load(slot, micro, late):
        rows = sources[slot][0].shape[0]
        return pltpu.make_async_copy(
            sources[slot][late * micro_count + micro],
            loaded[slot].at[pl.ds(micro * rows, rows), :],
            load_sem.at[slot, micro],
        )

    def start_load(slot):
        for micro in range(micro_count):

            @pl.when(section == 0)
            def _():
                load(slot, micro, 0).start()

            @pl.when(section != 0)
            def _():
                load(slot, micro, 1).start()

    def wait_load(slot):
        for micro in range(micro_count):
            load(slot, micro, 0).wait()

    def term(index, owner):
        height = heights[index]
        part = lefts[LEFT_OF[index]][pl.ds(pl.multiple_of(owner * height, 16), height), :]
        value = dot(part, rights[index][...])
        if index == 1:
            line = lax.broadcasted_iota(jnp.int32, value.shape, 0)
            value = value + jnp.where(line == piece, gain_terms[owner], 0.0)
        return value.astype(jnp.bfloat16)

    def side_copy(index, step):
        return pltpu.make_async_remote_copy(
            src_ref=outs[index].at[step % 2],
            dst_ref=sides[index].at[step],
            send_sem=side_send.at[step, index],
            recv_sem=side_recv.at[step, index],
            device_id={"dp": sibling},
            device_id_type=pl.DeviceIdType.MESH,
        )

    def ring_copy(index, step):
        return pltpu.make_async_remote_copy(
            src_ref=owns[index].at[step],
            dst_ref=rings[index].at[step],
            send_sem=ring_send.at[step, index],
            recv_sem=ring_recv.at[step, index],
            device_id={"dp": following},
            device_id_type=pl.DeviceIdType.MESH,
        )

    def prepare(index, step):
        theirs = at(turn * (step + 1), 1 - core)
        mine = at(-turn * (step + 1), core)
        if step > 1:
            side_copy(index, step - 2).wait_send()
        outs[index][step % 2] = term(index, theirs)
        side_copy(index, step).start()
        owns[index][step] = term(index, mine)

    def advance(index, step):
        side_copy(index, step).wait_recv()
        if step > 0:
            ring_copy(index, step - 1).wait_recv()

        def add(block):
            part = pl.ds(pl.multiple_of(block * 16, 16), 16)
            total = owns[index][step, part, :].astype(jnp.float32) + sides[index][
                step, part, :
            ].astype(jnp.float32)
            if step > 0:
                total = total + rings[index][step - 1, part, :].astype(jnp.float32)
            if step < chips - 1:
                owns[index][step, part, :] = total.astype(jnp.bfloat16)
            else:
                totals[index][part, :] = total

        pl.loop(0, heights[index] // 16)(add)
        if step < chips - 1:
            ring_copy(index, step).start()

    ready = []
    for index in SEND_ORDER:
        if LEFT_OF[index] not in ready:
            start_load(LEFT_OF[index])
            ready.append(LEFT_OF[index])
        start_load(4 + index)
    ready = []
    waiting = None
    for index in SEND_ORDER:
        left = LEFT_OF[index]
        if left not in ready:
            wait_load(left)
            lefts[left][...] = loaded[left][...].T
            ready.append(left)
        wait_load(4 + index)
        prepare(index, 0)
        if waiting is not None:
            advance(waiting, 0)
        waiting = index
    advance(waiting, 0)
    for step in range(1, chips):
        for index in SEND_ORDER:
            prepare(index, step)
        for index in SEND_ORDER:
            advance(index, step)
    for step in range(chips):
        for index in SEND_ORDER:
            if step >= chips - 2:
                side_copy(index, step).wait_send()
            if step < chips - 1:
                ring_copy(index, step).wait_send()


def scatter_all(sources, gain_terms, sizes, members):
    chips = members // 2
    micro_count = len(sources[0]) // 2
    wholes = [(micro_count * group[0].shape[0], group[0].shape[1]) for group in sources]
    shapes = [
        (wholes[LEFT_OF[index]][1] // members, wholes[4 + index][1]) for index in range(5)
    ]
    stacks = lambda depth: [pltpu.VMEM((depth, *shape), jnp.bfloat16) for shape in shapes]
    vmem = pl.BlockSpec(memory_space=pltpu.VMEM)
    flat_sources = [member for group in sources for member in group]
    return pl.pallas_call(
        functools.partial(scatter_kernel, chips, sizes, micro_count),
        out_shape=tuple(jax.ShapeDtypeStruct(shape, jnp.float32) for shape in shapes),
        in_specs=[pl.BlockSpec(memory_space=pl.ANY)] * len(flat_sources) + [vmem],
        out_specs=tuple([vmem] * 5),
        scratch_shapes=[pltpu.VMEM(whole, jnp.bfloat16) for whole in wholes]
        + [pltpu.VMEM(whole[::-1], jnp.bfloat16) for whole in wholes[:4]]
        + stacks(chips)
        + stacks(2)
        + stacks(chips)
        + stacks(chips - 1)
        + [pltpu.SemaphoreType.DMA((9, micro_count))]
        + [pltpu.SemaphoreType.DMA((chips, 5))] * 4,
        compiler_params=pltpu.CompilerParams(
            collective_id=1, has_side_effects=True, vmem_limit_bytes=60 * 2**20
        ),
        name="scatter_ring",
    )(*flat_sources, gain_terms)


def flatten_kernel(sizes, *refs):
    piece, hidden_piece, model, kv_width, hidden = sizes
    totals, spread = refs[:5], refs[5]
    out_query, out_key, out_value, out_out, out_gains, out_gate, out_up, out_down = refs[6:14]
    stage = refs[14]
    rows_into(out_gate, totals[2], piece, hidden, 0)
    rows_into(out_up, totals[3], piece, hidden, 0)
    rows_into(out_query, totals[0], piece, model, 0)
    rows_into(out_key, totals[0], piece, kv_width, model)
    rows_into(out_value, totals[0], piece, kv_width, model + kv_width)
    out_gains[...] = totals[1][piece : piece + 1, : out_gains.shape[1]]
    for index in (1, 4):
        total = totals[index][...]
        upper = total.astype(jnp.bfloat16)
        lower = (total - upper.astype(jnp.float32)).astype(jnp.bfloat16)
        stage[: total.shape[0], :] = dot_nt(upper, spread[...]) + dot_nt(lower, spread[...])
        if index == 1:
            rows_into(out_out, stage, piece, model, 0)
        else:
            rows_into(out_down, stage, hidden_piece, model, 0)


def flatten_all(totals, spread, sizes):
    piece, hidden_piece, model, kv_width, hidden = sizes
    lengths = (
        piece * model,
        piece * kv_width,
        piece * kv_width,
        piece * model,
        -(-2 * piece // 128) * 128,
        piece * hidden,
        piece * hidden,
        hidden_piece * model,
    )
    vmem = pl.BlockSpec(memory_space=pltpu.VMEM)
    return pl.pallas_call(
        functools.partial(flatten_kernel, sizes),
        out_shape=tuple(jax.ShapeDtypeStruct((1, length), jnp.float32) for length in lengths),
        in_specs=[vmem] * 6,
        out_specs=tuple([vmem] * 8),
        scratch_shapes=[pltpu.VMEM((max(totals[1].shape[0], hidden_piece), model), jnp.float32)],
        compiler_params=pltpu.CompilerParams(vmem_limit_bytes=40 * 2**20),
        name="flatten_pieces",
    )(*totals, spread)


def dot(left, right):
    return jnp.dot(left, right, preferred_element_type=jnp.float32)


def dot_nt(left, right):
    return lax.dot_general(
        left, right, (((1,), (1,)), ((), ())), preferred_element_type=jnp.float32
    )


def dot_tn(left, right):
    return lax.dot_general(
        left, right, (((0,), (0,)), ((), ())), preferred_element_type=jnp.float32
    )


def turn_heads(values, tables, sign):
    cos_table, early_sine, late_sine = tables
    half = HEAD // 2
    span = cos_table.shape[1]
    turned = []
    for start in range(0, values.shape[1], span):
        part = values[:, start : start + span]
        turned.append(
            part * cos_table[...]
            + sign
            * (
                pltpu.roll(part, span - half, 1) * early_sine[...]
                + pltpu.roll(part, half, 1) * late_sine[...]
            )
        )
    return jnp.concatenate(turned, axis=1)


def head_rows(source, micro, rows, first, group):
    return jnp.concatenate(
        [
            source[micro * rows : (micro + 1) * rows, (first + g) * HEAD : (first + g + 1) * HEAD]
            for g in range(group)
        ],
        axis=0,
    )


def forward_kernel(
    model,
    layout,
    stream,
    gains,
    bias,
    cos_table,
    early_sine,
    late_sine,
    spread,
    w_qkv,
    w_out,
    w_gate,
    w_up,
    w_down,
    layer_out,
    layer_low,
    normed,
    turned,
    values,
    mixed_wide,
    middle,
    normed_two,
    gate_pre,
    up_pre,
    activation,
    mixed,
):
    heads, kv_heads, micro_count, rows = layout
    group = heads // kv_heads

    @pl.when(pl.program_id(0) == 0)
    def _():
        residual = stream[...].astype(jnp.float32)
        scale = lax.rsqrt(jnp.sum(residual * residual, axis=1, keepdims=True) / model + EPSILON)
        normed[...] = (residual * scale * gains[0:1, :]).astype(jnp.bfloat16)
        products = dot(normed[...], w_qkv[...])
        split = (heads + kv_heads) * HEAD
        turned[...] = turn_heads(
            products[:, :split], (cos_table, early_sine, late_sine), 1.0
        ).astype(jnp.bfloat16)
        values[...] = products[:, split:].astype(jnp.bfloat16)
        for micro in range(micro_count):
            part = slice(micro * rows, (micro + 1) * rows)
            for kv in range(kv_heads):
                query = head_rows(turned, micro, rows, kv * group, group)
                key = turned[part, (heads + kv) * HEAD : (heads + kv + 1) * HEAD]
                value = values[part, kv * HEAD : (kv + 1) * HEAD]
                scores = dot_nt(query, key) * HEAD ** (-0.5)
                scores = scores + jnp.concatenate([bias[micro]] * group, axis=0)
                exponent = jnp.exp(scores - jnp.max(scores, axis=1, keepdims=True))
                total = jnp.sum(exponent, axis=1, keepdims=True)
                probability = (exponent / total).astype(jnp.bfloat16)
                attended = dot(probability, value).astype(jnp.bfloat16)
                for g in range(group):
                    head = kv * group + g
                    mixed[part, head * HEAD : (head + 1) * HEAD] = attended[
                        g * rows : (g + 1) * rows, :
                    ]
        mixed_wide[...] = dot(mixed[...], spread[...]).astype(jnp.bfloat16)
        halfway = residual + dot(mixed_wide[...], w_out[...])
        middle[...] = halfway
        scale_two = lax.rsqrt(jnp.sum(halfway * halfway, axis=1, keepdims=True) / model + EPSILON)
        normed_two[...] = (halfway * scale_two * gains[1:2, :]).astype(jnp.bfloat16)
        layer_out[...] = halfway

    gate = dot(normed_two[...], w_gate[...])
    up = dot(normed_two[...], w_up[...])
    gate_pre[...] = gate
    up_pre[...] = up
    active = (gate * jax.nn.sigmoid(gate) * up).astype(jnp.bfloat16)
    activation[...] = active
    layer_out[...] += dot(active, w_down[...])

    @pl.when(pl.program_id(0) == pl.num_programs(0) - 1)
    def _():
        layer_low[...] = layer_out[...].astype(jnp.bfloat16)


def full(array):
    return pl.BlockSpec(array.shape, lambda i: (0,) * len(array.shape))


def shape_of(rows, width, dtype):
    return jax.ShapeDtypeStruct((rows, width), dtype)


def tile_width(hidden):
    for width in (512, 256, 128):
        if hidden % width == 0:
            return width
    return hidden


def forward_fast(model, layout, stream, gains, bias, tables, spread, matrices):
    w_qkv, w_out, w_gate, w_up, w_down = matrices
    heads, kv_heads, micro_count, rows = layout
    tokens, wide = stream.shape
    hidden = w_gate.shape[1]
    tile = tile_width(hidden)
    split = (heads + kv_heads) * HEAD
    low, high = jnp.bfloat16, jnp.float32
    out_shape = (
        shape_of(tokens, wide, high),
        shape_of(tokens, wide, low),
        shape_of(tokens, wide, low),
        shape_of(tokens, split, low),
        shape_of(tokens, w_qkv.shape[1] - split, low),
        shape_of(tokens, wide, low),
        shape_of(tokens, wide, high),
        shape_of(tokens, wide, low),
        shape_of(tokens, hidden, high),
        shape_of(tokens, hidden, high),
        shape_of(tokens, hidden, low),
    )
    columns = lambda height: pl.BlockSpec((height, tile), lambda i: (0, i))
    ins = (stream, gains, bias, *tables, spread, w_qkv, w_out)
    return pl.pallas_call(
        functools.partial(forward_kernel, model, layout),
        grid=(hidden // tile,),
        out_shape=out_shape,
        in_specs=[full(member) for member in ins]
        + [columns(wide), columns(wide), pl.BlockSpec((tile, wide), lambda i: (i, 0))],
        out_specs=tuple([full(member) for member in out_shape[:8]] + [columns(tokens)] * 3),
        scratch_shapes=[pltpu.VMEM((tokens, heads * HEAD), low)],
        compiler_params=pltpu.CompilerParams(vmem_limit_bytes=56 * 2**20),
        cost_estimate=pl.CostEstimate(
            flops=10 * 2**28, bytes_accessed=28 * 2**20, transcendentals=2**20
        ),
        name="forward_layer",
    )(*ins, w_gate, w_up, w_down)


def backward_kernel(
    model,
    layout,
    cotangent,
    stream,
    gains,
    bias,
    cos_table,
    early_sine,
    late_sine,
    spread,
    turned,
    values,
    middle,
    w_qkv,
    w_out,
    gate_pre,
    up_pre,
    w_gate,
    w_up,
    w_down,
    grad_input,
    input_low,
    grad_gains,
    grad_branch,
    grad_qkv,
    grad_gate,
    grad_up,
    norm_grad,
    grad_mixed,
    grad_turned,
    grad_values,
):
    heads, kv_heads, micro_count, rows = layout
    group = heads // kv_heads
    step = pl.program_id(0)

    @pl.when(step == 0)
    def _():
        norm_grad[...] = jnp.zeros_like(norm_grad)

    gate = gate_pre[...]
    grad_act = dot_nt(cotangent[...], w_down[...])
    sigmoid = jax.nn.sigmoid(gate)
    grad_gate[...] = (
        grad_act * up_pre[...] * sigmoid * (1.0 + gate * (1.0 - sigmoid))
    ).astype(jnp.bfloat16)
    grad_up[...] = (grad_act * gate * sigmoid).astype(jnp.bfloat16)
    norm_grad[...] += dot_nt(grad_gate[...], w_gate[...]) + dot_nt(grad_up[...], w_up[...])

    @pl.when(step == pl.num_programs(0) - 1)
    def _():
        halfway = middle[...]
        scale_two = lax.rsqrt(jnp.sum(halfway * halfway, axis=1, keepdims=True) / model + EPSILON)
        centered = halfway * scale_two
        gradient = norm_grad[...]
        grad_gains[1:2, :] = jnp.sum(gradient * centered, axis=0, keepdims=True)
        scaled = gradient * gains[1:2, :]
        grad_middle = cotangent[...].astype(jnp.float32) + scale_two * (
            scaled - centered * (jnp.sum(scaled * centered, axis=1, keepdims=True) / model)
        )
        grad_input[...] = grad_middle
        grad_branch[...] = grad_middle.astype(jnp.bfloat16)
        grad_wide = dot_nt(grad_branch[...], w_out[...]).astype(jnp.bfloat16)
        grad_mixed[...] = dot_nt(grad_wide, spread[...]).astype(jnp.bfloat16)
        grad_values[...] = jnp.zeros_like(grad_values)
        for micro in range(micro_count):
            part = slice(micro * rows, (micro + 1) * rows)
            for kv in range(kv_heads):
                query = head_rows(turned, micro, rows, kv * group, group)
                key = turned[part, (heads + kv) * HEAD : (heads + kv + 1) * HEAD]
                value = values[part, kv * HEAD : (kv + 1) * HEAD]
                grad_head = head_rows(grad_mixed, micro, rows, kv * group, group)
                scores = dot_nt(query, key) * HEAD ** (-0.5)
                scores = scores + jnp.concatenate([bias[micro]] * group, axis=0)
                exponent = jnp.exp(scores - jnp.max(scores, axis=1, keepdims=True))
                total = jnp.sum(exponent, axis=1, keepdims=True)
                probability = exponent / total
                grad_value = dot_tn(probability.astype(jnp.bfloat16), grad_head)
                grad_prob = dot_nt(grad_head, value)
                inner = jnp.sum(probability * grad_prob, axis=1, keepdims=True)
                grad_scores = (probability * (grad_prob - inner)).astype(jnp.bfloat16)
                grad_query = dot(grad_scores, key) * HEAD ** (-0.5)
                grad_key = dot_tn(grad_scores, query) * HEAD ** (-0.5)
                for g in range(group):
                    head = kv * group + g
                    grad_turned[part, head * HEAD : (head + 1) * HEAD] = grad_query[
                        g * rows : (g + 1) * rows, :
                    ]
                grad_turned[part, (heads + kv) * HEAD : (heads + kv + 1) * HEAD] = grad_key
                grad_values[part, kv * HEAD : (kv + 1) * HEAD] = grad_value
        split = (heads + kv_heads) * HEAD
        grad_qkv[:, :split] = turn_heads(
            grad_turned[...], (cos_table, early_sine, late_sine), -1.0
        ).astype(jnp.bfloat16)
        grad_qkv[:, split:] = grad_values[...].astype(jnp.bfloat16)
        first_gradient = dot_nt(grad_qkv[...], w_qkv[...])
        residual = stream[...].astype(jnp.float32)
        scale = lax.rsqrt(jnp.sum(residual * residual, axis=1, keepdims=True) / model + EPSILON)
        first_centered = residual * scale
        grad_gains[0:1, :] = jnp.sum(first_gradient * first_centered, axis=0, keepdims=True)
        first_scaled = first_gradient * gains[0:1, :]
        grad_input[...] += scale * (
            first_scaled
            - first_centered
            * (jnp.sum(first_scaled * first_centered, axis=1, keepdims=True) / model)
        )
        input_low[...] = grad_input[...].astype(jnp.bfloat16)


def backward_fast(model, layout, cotangent, kept, gains, bias, tables, spread, matrices):
    w_qkv, w_out, w_gate, w_up, w_down = matrices
    stream, _, _, turned, values, _, middle, _, gate_pre, up_pre, _ = kept
    heads, kv_heads, micro_count, rows = layout
    tokens, wide = stream.shape
    hidden = w_gate.shape[1]
    tile = tile_width(hidden)
    split = (heads + kv_heads) * HEAD
    low, high = jnp.bfloat16, jnp.float32
    out_shape = (
        shape_of(tokens, wide, high),
        shape_of(tokens, wide, low),
        shape_of(2, wide, high),
        shape_of(tokens, wide, low),
        shape_of(tokens, w_qkv.shape[1], low),
        shape_of(tokens, hidden, low),
        shape_of(tokens, hidden, low),
    )
    columns = lambda height: pl.BlockSpec((height, tile), lambda i: (0, i))
    ins = (cotangent, stream, gains, bias, *tables, spread, turned, values, middle, w_qkv, w_out)
    return pl.pallas_call(
        functools.partial(backward_kernel, model, layout),
        grid=(hidden // tile,),
        out_shape=out_shape,
        in_specs=[full(member) for member in ins]
        + [columns(tokens)] * 2
        + [columns(wide), columns(wide), pl.BlockSpec((tile, wide), lambda i: (i, 0))],
        out_specs=tuple([full(member) for member in out_shape[:5]] + [columns(tokens)] * 2),
        scratch_shapes=[
            pltpu.VMEM((tokens, wide), high),
            pltpu.VMEM((tokens, heads * HEAD), low),
            pltpu.VMEM((tokens, split), high),
            pltpu.VMEM((tokens, w_qkv.shape[1] - split), high),
        ],
        compiler_params=pltpu.CompilerParams(vmem_limit_bytes=56 * 2**20),
        cost_estimate=pl.CostEstimate(
            flops=12 * 2**28, bytes_accessed=30 * 2**20, transcendentals=2**20
        ),
        name="backward_layer",
    )(*ins, gate_pre, up_pre, w_gate, w_up, w_down)


def widen(array, members, room):
    width = array.shape[-1] // members
    cut = array.reshape(array.shape[:-1] + (members, width))
    cut = jnp.pad(cut, [(0, 0)] * (cut.ndim - 1) + [(0, room - width)])
    return cut.reshape(array.shape[:-1] + (members * room,))


def narrow(array, members, width):
    room = array.shape[-1] // members
    cut = array.reshape(array.shape[:-1] + (members, room))[..., :width]
    return cut.reshape(array.shape[:-1] + (members * width,))


def lifted(array, height, width):
    return jnp.pad(array, [(0, height - array.shape[0]), (0, width - array.shape[1])])


def rows_room(model, members):
    return -(-(model // members + 1) // 16) * 16


def on_device_fast(boundary, doc_lens, w_query, w_key, w_value, w_out, gains, w_gate, w_up, w_down):
    section = lax.axis_index("section")
    members = lax.axis_size("dp")
    _, micro_count, rows, model = boundary.shape
    tokens = micro_count * rows
    piece = model // members
    room = rows_room(model, members)
    wide = room * members
    kv_width = w_key.size // piece
    hidden = w_gate.size // piece
    heads, kv_heads = model // HEAD, kv_width // HEAD
    layout = (heads, kv_heads, micro_count, rows)
    split = model + kv_width
    qkv_wide = split + -(-kv_width // 128) * 128
    hidden_piece = hidden // members
    gain_piece = gains.size

    feature = jnp.arange(model, dtype=jnp.int32)
    spread = (
        (feature // piece * room + feature % piece)[:, None]
        == jnp.arange(wide, dtype=jnp.int32)[None, :]
    ).astype(jnp.bfloat16)

    def spread_out(array):
        return jnp.dot(array, spread, preferred_element_type=jnp.float32).astype(array.dtype)

    sizes = (piece, hidden_piece, model, kv_width, hidden)
    gain_row = lifted(gains, 1, wide).astype(jnp.float32)
    gathered = gather_all(
        (w_query, w_key, w_value, w_out, w_gate, w_up, w_down, gain_row, spread),
        sizes,
        members,
        ((room, qkv_wide), (room, wide), (room, hidden), (room, hidden), (hidden_piece, wide)),
    )
    gain_rows = gathered[1].reshape(members, room, wide)[:, piece, :gain_piece]
    gain_pair = widen(gain_rows.reshape(2, model), members, room).astype(jnp.float32)

    layouts = [doc_layout(doc_lens[micro, 0], rows) for micro in range(micro_count)]
    segments = jnp.stack([item[0] for item in layouts])
    positions = jnp.concatenate([item[1] for item in layouts])
    live = jnp.concatenate([item[2] for item in layouts]).astype(jnp.float32)
    slot_ids = jnp.arange(rows, dtype=jnp.int32)
    allowed = (slot_ids[None, :] <= slot_ids[:, None])[None] & (
        segments[:, :, None] == segments[:, None, :]
    )
    bias = jnp.where(allowed, 0.0, -1e30).astype(jnp.float32)
    cos_table, sine_table = rope_tables(positions)
    first_half = (jnp.arange(HEAD, dtype=jnp.int32) < HEAD // 2)[None, :]
    tables = tuple(
        jnp.tile(table, (1, 128 // HEAD))
        for table in (
            cos_table,
            jnp.where(first_half, -sine_table, 0.0),
            jnp.where(first_half, 0.0, sine_table),
        )
    )

    own = spread_out(boundary.reshape(tokens, model))
    dimmed = jnp.where(section == 1, own * live[:, None].astype(jnp.bfloat16), 0.0)
    alone = (heads, kv_heads, 1, rows)
    micros = range(micro_count)
    part = lambda array, micro: array[micro * rows : (micro + 1) * rows]
    shared = [
        (gain_pair, bias[m : m + 1], tuple(part(t, m) for t in tables), spread, gathered)
        for m in micros
    ]
    streams_zero = [part(own, m) for m in micros]
    kept_zero = [forward_fast(model, alone, streams_zero[m], *shared[m]) for m in micros]
    streams_one = [passed_along(kept[1], "section", 1) for kept in kept_zero]
    kept_one = [forward_fast(model, alone, streams_one[m], *shared[m]) for m in micros]
    starts_one = [part(dimmed, m).astype(jnp.bfloat16) for m in micros]
    back_one = [
        backward_fast(model, alone, starts_one[m], (streams_one[m], *kept_one[m][1:]), *shared[m])
        for m in micros
    ]
    starts_zero = [passed_along(back[1], "section", -1) for back in back_one]
    back_zero = [
        backward_fast(
            model, alone, starts_zero[m], (streams_zero[m], *kept_zero[m][1:]), *shared[m]
        )
        for m in micros
    ]

    pick = lambda early, late: jnp.where(section == 0, early, late)
    results = jnp.stack([pick(back_zero[m][0], kept_one[m][0]) for m in micros])
    results = narrow(results, members, piece)
    sources = [[*kept_zero, *kept_one], [*back_zero, *back_one], [*starts_zero, *starts_one]]
    sources = (
        [[kept[at] for kept in sources[0]] for at in (2, 5, 7, 10)]
        + [[back[at] for back in sources[1]] for at in (4, 3, 5, 6)]
        + [sources[2]]
    )
    grad_gains = pick(sum(back[2] for back in back_zero), sum(back[2] for back in back_one))
    gain_terms = narrow(grad_gains, members, piece).reshape(members, 1, gain_piece)
    gain_terms = jnp.pad(gain_terms, ((0, 0), (0, 0), (0, wide - gain_piece)))
    totals = scatter_all(sources, gain_terms, sizes, members)
    shares = flatten_all(totals, spread, sizes)
    return (
        results[None],
        *shares[:4],
        shares[4][:, :gain_piece],
        *shares[5:],
    )


def rows_fit(mesh, model, hidden):
    members = mesh.shape["dp"]
    return (
        mesh.shape["section"] == 2
        and members >= 6
        and members % 4 == 0
        and model % members == 0
        and hidden % members == 0
        and (hidden // members) % 16 == 0
        and hidden % 128 == 0
        and model % 64 == 0
        and (model // members) % 2 == 0
        and (rows_room(model, members) * members) % 128 == 0
    )


def solution(mesh):
    placed = (
        P("section", None, "dp", None),
        P(None, "dp", None),
        P("section", "dp"),
        P("section", "dp"),
        P("section", "dp"),
        P("section", "dp"),
        P("section", "dp"),
        P("section", "dp"),
        P("section", "dp"),
        P("section", "dp"),
    )

    def chosen(*operands):
        model = operands[0].shape[3]
        hidden = operands[7].size * mesh.shape["dp"] // model
        return (on_device_fast if rows_fit(mesh, model, hidden) else on_device)(*operands)

    return jax.shard_map(
        chosen,
        mesh=mesh,
        in_specs=placed,
        out_specs=(
            P("section", None, "dp", None),
            P("section", "dp"),
            P("section", "dp"),
            P("section", "dp"),
            P("section", "dp"),
            P("section", "dp"),
            P("section", "dp"),
            P("section", "dp"),
            P("section", "dp"),
        ),
        check_vma=False,
    )
```

```python
import functools

import jax
import jax.numpy as jnp
from jax import lax
from jax.experimental import pallas as pl
from jax.experimental.pallas import tpu as pltpu
from jax.sharding import PartitionSpec as P

HEAD = 64


EPSILON = 1e-05
ROPE_BASE = 100000.0


def passed_along(x, axis, by):
    devices = lax.axis_size(axis)
    pairs = [(i, i + by) for i in range(devices) if 0 <= i + by < devices]
    return lax.ppermute(x, axis, pairs)


def as_sent(x):
    return jax.tree.map(lambda a: a.astype(jnp.bfloat16) if a.dtype == jnp.float32 else a, x)


def doc_layout(lengths, slot_count):
    doc_ends = jnp.cumsum(lengths, dtype=jnp.int32)
    doc_starts = doc_ends - lengths
    doc_count = lengths.shape[0]
    slot_ids = jnp.arange(slot_count, dtype=jnp.int32)
    segment = jnp.sum(
        (slot_ids[:, None] >= doc_ends[None, :]).astype(jnp.int32), axis=1, dtype=jnp.int32
    )
    start_table = jnp.concatenate([doc_starts, doc_ends[doc_count - 1 :]])
    picked = segment[:, None] == jnp.arange(doc_count + 1, dtype=jnp.int32)[None, :]
    first_slot = jnp.sum(jnp.where(picked, start_table[None, :], 0), axis=1, dtype=jnp.int32)
    return (segment, slot_ids - first_slot, segment < doc_count)


def rope_tables(position):
    half_width = HEAD // 2
    inverse_freq = ROPE_BASE ** (-(jnp.arange(half_width, dtype=jnp.float32) * (2.0 / HEAD)))
    angles = position.astype(jnp.float32)[:, None] * inverse_freq[None, :]
    cos_table = jnp.cos(angles)
    sine_table = jnp.sin(angles)
    return (
        jnp.concatenate([cos_table, cos_table], axis=1),
        jnp.concatenate([sine_table, sine_table], axis=1),
    )


def rotate(values, cos_table, sine_table):
    half_width = values.shape[-1] // 2
    turned = jnp.concatenate([-values[..., half_width:], values[..., :half_width]], axis=-1)
    return values * cos_table[:, None, :] + turned * sine_table[:, None, :]


def unrotate(values, cos_table, sine_table):
    half_width = values.shape[-1] // 2
    sined = values * sine_table[:, None, :]
    turned = jnp.concatenate([sined[..., half_width:], -sined[..., :half_width]], axis=-1)
    return values * cos_table[:, None, :] + turned


def unpack(gathered, model_width):
    kv_width = gathered[1].size // model_width
    hidden_width = gathered[5].size // model_width
    return (
        gathered[0].reshape(model_width, model_width),
        gathered[1].reshape(model_width, kv_width),
        gathered[2].reshape(model_width, kv_width),
        gathered[3].reshape(model_width, model_width),
        gathered[4].reshape(2 * model_width),
        gathered[5].reshape(model_width, hidden_width),
        gathered[6].reshape(model_width, hidden_width),
        gathered[7].reshape(hidden_width, model_width),
    )


def add_sources(received):
    return tuple((jnp.sum(member, axis=0, keepdims=True) for member in received))


def forward_layer(layer_input_rows, matrices, allowed, cos_table, sine_table):
    w_query, w_key, w_value, w_out, gain_pair, w_gate, w_up, w_down = matrices
    row_count, model_width = layer_input_rows.shape
    kv_count = w_key.shape[1] // HEAD
    group_size = w_query.shape[1] // w_key.shape[1]
    score_scale = HEAD ** (-0.5)
    gain_one = gain_pair[:model_width].astype(jnp.float32)
    gain_two = gain_pair[model_width:].astype(jnp.float32)
    residual = layer_input_rows.astype(jnp.float32)
    first_inverse_scale = lax.rsqrt(jnp.mean(residual * residual, axis=1, keepdims=True) + EPSILON)
    normed = (residual * first_inverse_scale * gain_one).astype(jnp.bfloat16)
    queries = rotate(
        jnp.dot(normed, w_query, preferred_element_type=jnp.float32).reshape(row_count, -1, HEAD),
        cos_table,
        sine_table,
    ).astype(jnp.bfloat16)
    keys_turned = rotate(
        jnp.dot(normed, w_key, preferred_element_type=jnp.float32).reshape(
            row_count, kv_count, HEAD
        ),
        cos_table,
        sine_table,
    ).astype(jnp.bfloat16)
    values_low = jnp.dot(normed, w_value, preferred_element_type=jnp.float32).astype(jnp.bfloat16)
    heads_query = queries.reshape(row_count, kv_count, group_size, HEAD).transpose(1, 0, 2, 3)
    heads_key = keys_turned.transpose(1, 0, 2)
    heads_value = values_low.reshape(row_count, kv_count, HEAD).transpose(1, 0, 2)

    def one_head(operands):
        head_query, head_key, head_value = operands
        scores = (
            jnp.einsum("qgd,td->gqt", head_query, head_key, preferred_element_type=jnp.float32)
            * score_scale
        )
        scores = jnp.where(allowed[None], scores, -1e30)
        row_top = jnp.max(scores, axis=2, keepdims=True)
        exponent = jnp.exp(scores - row_top)
        row_total = jnp.sum(exponent, axis=2, keepdims=True)
        probability = (exponent / row_total).astype(jnp.bfloat16)
        attended = jnp.einsum(
            "gqt,td->qgd", probability, head_value, preferred_element_type=jnp.float32
        )
        return (attended, (row_top + jnp.log(row_total))[..., 0])

    attended, log_total = lax.map(one_head, (heads_query, heads_key, heads_value))
    mixed_low = attended.transpose(1, 0, 2, 3).reshape(row_count, model_width).astype(jnp.bfloat16)
    midway_hidden = residual + jnp.dot(mixed_low, w_out, preferred_element_type=jnp.float32)
    second_inverse_scale = lax.rsqrt(
        jnp.mean(midway_hidden * midway_hidden, axis=1, keepdims=True) + EPSILON
    )
    normed_two = (midway_hidden * second_inverse_scale * gain_two).astype(jnp.bfloat16)
    gate_pre = jnp.dot(normed_two, w_gate, preferred_element_type=jnp.float32)
    up_pre = jnp.dot(normed_two, w_up, preferred_element_type=jnp.float32)
    activation = (jax.nn.silu(gate_pre) * up_pre).astype(jnp.bfloat16)
    layer_out = midway_hidden + jnp.dot(activation, w_down, preferred_element_type=jnp.float32)
    kept_values = (
        layer_input_rows,
        normed,
        queries,
        keys_turned,
        values_low,
        log_total,
        mixed_low,
        midway_hidden,
        first_inverse_scale,
        second_inverse_scale,
        normed_two,
        gate_pre,
        up_pre,
        activation,
    )
    return (layer_out, kept_values)


def backward_layer(kept_values, matrices, allowed, cos_table, sine_table, grad_output, piece_count):
    (
        layer_input_rows,
        normed,
        queries,
        keys_turned,
        values_low,
        log_total,
        mixed_low,
        midway_hidden,
        first_inverse_scale,
        second_inverse_scale,
        normed_two,
        gate_pre,
        up_pre,
        activation,
    ) = kept_values
    w_query, w_key, w_value, w_out, gain_pair, w_gate, w_up, w_down = matrices
    row_count, model_width = layer_input_rows.shape
    kv_count = w_key.shape[1] // HEAD
    group_size = w_query.shape[1] // w_key.shape[1]
    score_scale = HEAD ** (-0.5)
    gain_one = gain_pair[:model_width].astype(jnp.float32)
    gain_two = gain_pair[model_width:].astype(jnp.float32)
    grad_low = grad_output.astype(jnp.bfloat16)
    grad_wdown = jnp.einsum("nf,nd->fd", activation, grad_low, preferred_element_type=jnp.float32)
    grad_act = jnp.einsum("nd,fd->nf", grad_low, w_down, preferred_element_type=jnp.float32)
    sigmoid_gate = jax.nn.sigmoid(gate_pre)
    grad_gate_pre = (
        grad_act * up_pre * sigmoid_gate * (1.0 + gate_pre * (1.0 - sigmoid_gate))
    ).astype(jnp.bfloat16)
    grad_up_pre = (grad_act * gate_pre * sigmoid_gate).astype(jnp.bfloat16)
    grad_wgate = jnp.einsum(
        "nd,nf->df", normed_two, grad_gate_pre, preferred_element_type=jnp.float32
    )
    grad_wup = jnp.einsum("nd,nf->df", normed_two, grad_up_pre, preferred_element_type=jnp.float32)
    second_norm_gradient = jnp.einsum(
        "nf,df->nd", grad_gate_pre, w_gate, preferred_element_type=jnp.float32
    ) + jnp.einsum("nf,df->nd", grad_up_pre, w_up, preferred_element_type=jnp.float32)
    second_centered_input = midway_hidden * second_inverse_scale
    second_normalized_rows = second_norm_gradient * gain_two
    second_gain_gradient = jnp.sum(second_norm_gradient * second_centered_input, axis=0)
    grad_middle = grad_output + second_inverse_scale * (
        second_normalized_rows
        - second_centered_input
        * jnp.mean(second_normalized_rows * second_centered_input, axis=1, keepdims=True)
    )
    grad_branch = grad_middle.astype(jnp.bfloat16)
    grad_wout = jnp.einsum("nd,ne->de", mixed_low, grad_branch, preferred_element_type=jnp.float32)
    grad_mixed = jnp.einsum(
        "ne,de->nd", grad_branch, w_out, preferred_element_type=jnp.float32
    ).astype(jnp.bfloat16)
    heads_query = queries.reshape(row_count, kv_count, group_size, HEAD).transpose(1, 0, 2, 3)
    heads_key = keys_turned.transpose(1, 0, 2)
    heads_value = values_low.reshape(row_count, kv_count, HEAD).transpose(1, 0, 2)
    heads_grad = grad_mixed.reshape(row_count, kv_count, group_size, HEAD).transpose(1, 0, 2, 3)

    def one_back(operands):
        head_query, head_key, head_value, head_lse, head_grad = operands
        scores = (
            jnp.einsum("qgd,td->gqt", head_query, head_key, preferred_element_type=jnp.float32)
            * score_scale
        )
        scores = jnp.where(allowed[None], scores, -1e30)
        probability = jnp.exp(scores - head_lse[..., None])
        grad_vhead = jnp.einsum(
            "gqt,qgd->td",
            probability.astype(jnp.bfloat16),
            head_grad,
            preferred_element_type=jnp.float32,
        )
        grad_prob = jnp.einsum(
            "qgd,td->gqt", head_grad, head_value, preferred_element_type=jnp.float32
        )
        grad_scores = (
            probability * (grad_prob - jnp.sum(probability * grad_prob, axis=2, keepdims=True))
        ).astype(jnp.bfloat16)
        grad_qhead = (
            jnp.einsum("gqt,td->qgd", grad_scores, head_key, preferred_element_type=jnp.float32)
            * score_scale
        )
        grad_khead = (
            jnp.einsum("gqt,qgd->td", grad_scores, head_query, preferred_element_type=jnp.float32)
            * score_scale
        )
        return (grad_qhead, grad_khead, grad_vhead)

    grad_qheads, grad_kheads, grad_vheads = lax.map(
        one_back, (heads_query, heads_key, heads_value, log_total, heads_grad)
    )
    grad_queries = (
        unrotate(
            grad_qheads.transpose(1, 0, 2, 3).reshape(row_count, -1, HEAD), cos_table, sine_table
        )
        .reshape(row_count, -1)
        .astype(jnp.bfloat16)
    )
    grad_keys = (
        unrotate(grad_kheads.transpose(1, 0, 2), cos_table, sine_table)
        .reshape(row_count, -1)
        .astype(jnp.bfloat16)
    )
    grad_values = grad_vheads.transpose(1, 0, 2).reshape(row_count, -1).astype(jnp.bfloat16)
    grad_wquery = jnp.einsum("nd,ne->de", normed, grad_queries, preferred_element_type=jnp.float32)
    grad_wkey = jnp.einsum("nd,ne->de", normed, grad_keys, preferred_element_type=jnp.float32)
    grad_wvalue = jnp.einsum("nd,ne->de", normed, grad_values, preferred_element_type=jnp.float32)
    first_norm_gradient = (
        jnp.einsum("ne,de->nd", grad_queries, w_query, preferred_element_type=jnp.float32)
        + jnp.einsum("ne,de->nd", grad_keys, w_key, preferred_element_type=jnp.float32)
        + jnp.einsum("ne,de->nd", grad_values, w_value, preferred_element_type=jnp.float32)
    )
    first_centered_input = layer_input_rows.astype(jnp.float32) * first_inverse_scale
    first_normalized_rows = first_norm_gradient * gain_one
    first_gain_gradient = jnp.sum(first_norm_gradient * first_centered_input, axis=0)
    grad_input = grad_middle + first_inverse_scale * (
        first_normalized_rows
        - first_centered_input
        * jnp.mean(first_normalized_rows * first_centered_input, axis=1, keepdims=True)
    )
    grad_terms = (
        grad_wquery,
        grad_wkey,
        grad_wvalue,
        grad_wout,
        jnp.concatenate([first_gain_gradient, second_gain_gradient]),
        grad_wgate,
        grad_wup,
        grad_wdown,
    )
    return (grad_input, tuple((member.reshape(piece_count, -1) for member in grad_terms)))


def on_device(boundary, doc_lens, w_query, w_key, w_value, w_out, gains, w_gate, w_up, w_down):
    sections = lax.axis_size("section")
    section_index = lax.axis_index("section")
    dp_count = lax.axis_size("dp")
    micro_count = boundary.shape[1]
    row_count = boundary.shape[2]
    model_width = boundary.shape[3]
    round_total = micro_count + sections - 1
    shards = (w_query, w_key, w_value, w_out, gains, w_gate, w_up, w_down)
    layouts = [
        doc_layout(doc_lens[micro_number, 0], row_count) for micro_number in range(micro_count)
    ]
    segments = jnp.stack([layout_item[0] for layout_item in layouts])
    positions = jnp.stack([layout_item[1] for layout_item in layouts])
    live_rows = jnp.stack([layout_item[2] for layout_item in layouts]).astype(jnp.float32)
    slot_ids = jnp.arange(row_count, dtype=jnp.int32)
    causal = slot_ids[None, :] <= slot_ids[:, None]

    def layout_for(micro_slot):
        segment = lax.dynamic_index_in_dim(segments, micro_slot, 0, keepdims=False)
        position = lax.dynamic_index_in_dim(positions, micro_slot, 0, keepdims=False)
        allowed = causal & (segment[:, None] == segment[None, :])
        cos_table, sine_table = rope_tables(position)
        return (allowed, cos_table, sine_table)

    matrices = unpack(
        (
            lax.all_gather(shards[0], "dp", axis=0, tiled=True),
            lax.all_gather(shards[1], "dp", axis=0, tiled=True),
            lax.all_gather(shards[2], "dp", axis=0, tiled=True),
            lax.all_gather(shards[3], "dp", axis=0, tiled=True),
            lax.all_gather(shards[4], "dp", axis=0, tiled=True),
            lax.all_gather(shards[5], "dp", axis=0, tiled=True),
            lax.all_gather(shards[6], "dp", axis=0, tiled=True),
            lax.all_gather(shards[7], "dp", axis=0, tiled=True),
        ),
        model_width,
    )
    own_inputs = boundary[0]
    results = jnp.zeros((micro_count, row_count, model_width), jnp.float32)
    outgoing = jnp.zeros((row_count, model_width), jnp.bfloat16)
    kept_rounds = []
    for round_index in range(round_total):
        if round_index > 0:
            incoming = passed_along(outgoing, "section", 1)
        else:
            incoming = jnp.zeros((row_count, model_width), jnp.bfloat16)
        micro_index = round_index - section_index
        is_valid = (micro_index >= 0) & (micro_index < micro_count)
        micro_slot = jnp.clip(micro_index, 0, micro_count - 1)
        layer_input_rows = jnp.where(
            section_index == 0,
            lax.dynamic_index_in_dim(own_inputs, micro_slot, 0, keepdims=False),
            incoming,
        )
        allowed, cos_table, sine_table = layout_for(micro_slot)
        layer_out, kept_values = forward_layer(
            layer_input_rows, matrices, allowed, cos_table, sine_table
        )
        kept_rounds.append(kept_values)
        finished = is_valid & (section_index == sections - 1)
        results = jnp.where(
            finished, lax.dynamic_update_index_in_dim(results, layer_out, micro_slot, 0), results
        )
        outgoing = layer_out.astype(jnp.bfloat16)
    stacked = jax.tree.map(lambda *members: jnp.stack(members), *kept_rounds)
    matrices_back = unpack(
        (
            lax.all_gather(shards[0], "dp", axis=0, tiled=True),
            lax.all_gather(shards[1], "dp", axis=0, tiled=True),
            lax.all_gather(shards[2], "dp", axis=0, tiled=True),
            lax.all_gather(shards[3], "dp", axis=0, tiled=True),
            lax.all_gather(shards[4], "dp", axis=0, tiled=True),
            lax.all_gather(shards[5], "dp", axis=0, tiled=True),
            lax.all_gather(shards[6], "dp", axis=0, tiled=True),
            lax.all_gather(shards[7], "dp", axis=0, tiled=True),
        ),
        model_width,
    )
    cotangent = boundary[sections - 1]
    totals = tuple(
        (jnp.zeros((dp_count, shard_piece.shape[1]), jnp.float32) for shard_piece in shards)
    )
    shares = tuple((jnp.zeros(shard_piece.shape, jnp.float32) for shard_piece in shards))
    back_outgoing = jnp.zeros((row_count, model_width), jnp.bfloat16)
    for round_index in range(round_total):
        if round_index > 0:
            arriving = passed_along(back_outgoing, "section", -1)
        else:
            arriving = jnp.zeros((row_count, model_width), jnp.bfloat16)
        micro_index = micro_count - 1 - round_index + (sections - 1 - section_index)
        is_valid = (micro_index >= 0) & (micro_index < micro_count)
        micro_slot = jnp.clip(micro_index, 0, micro_count - 1)
        kept_slot = jnp.clip(micro_index + section_index, 0, round_total - 1)
        kept_values = jax.tree.map(
            lambda member: lax.dynamic_index_in_dim(member, kept_slot, 0, keepdims=False), stacked
        )
        live_now = lax.dynamic_index_in_dim(live_rows, micro_slot, 0, keepdims=False)
        own_grad = (
            lax.dynamic_index_in_dim(cotangent, micro_slot, 0, keepdims=False).astype(jnp.float32)
            * live_now[:, None]
        )
        grad_output = jnp.where(
            section_index == sections - 1, own_grad, arriving.astype(jnp.float32)
        )
        grad_output = grad_output * is_valid.astype(jnp.float32)
        allowed, cos_table, sine_table = layout_for(micro_slot)
        grad_input, grad_terms = backward_layer(
            kept_values, matrices_back, allowed, cos_table, sine_table, grad_output, dp_count
        )
        totals = tuple(
            (left_term + right_term for left_term, right_term in zip(totals, grad_terms))
        )
        results = jnp.where(
            is_valid & (section_index == 0),
            lax.dynamic_update_index_in_dim(results, grad_input, micro_slot, 0),
            results,
        )
        back_outgoing = grad_input.astype(jnp.bfloat16)
    shares = add_sources(
        jax.tree.map(
            lambda part, own: part.astype(own.dtype),
            lax.all_to_all(as_sent(totals), "dp", split_axis=0, concat_axis=0, tiled=True),
            totals,
        )
    )
    return (
        results[None],
        shares[0],
        shares[1],
        shares[2],
        shares[3],
        shares[4],
        shares[5],
        shares[6],
        shares[7],
    )


def ring_place(chips):
    depth = chips // 2

    def place_of(chip):
        side = chip % 2
        level = chip // 2
        return level * (1 - side) + (chips - 1 - level) * side

    def chip_at(place):
        side = place // depth
        level = place * (1 - side) + (chips - 1 - place) * side
        return level * 2 + side

    return place_of, chip_at


def ring_setup(chips):
    place_of, chip_at = ring_place(chips)
    member = lax.axis_index("dp")
    core = member % 2
    place = place_of(member // 2)
    turn = 1 - 2 * core

    def at(offset, on_core):
        return chip_at((place + offset + 2 * chips) % chips) * 2 + on_core

    following = at(turn, core)
    preceding = at(-turn, core)
    sibling = member + turn
    barrier = pltpu.get_barrier_semaphore()
    for other in (following, preceding, sibling):
        pl.semaphore_signal(
            barrier, inc=1, device_id={"dp": other}, device_id_type=pl.DeviceIdType.MESH
        )
    pl.semaphore_wait(barrier, 3)
    return member, core, turn, at, following, sibling


def unit_of(width):
    return 1 if width % 128 == 0 else 2


def flat_part(line, width):
    span = unit_of(width) * width
    return pl.ds(pl.multiple_of(line * span, 128), span)


def rows_from(flat, stage, count, width, lane):
    unit = unit_of(width)

    def body(line):
        taken = flat[0:1, flat_part(line, width)].astype(jnp.float32)
        for u in range(unit):
            stage[pl.ds(line * unit + u, 1), lane : lane + width] = taken[
                :, u * width : (u + 1) * width
            ]

    pl.loop(0, count // unit)(body)


SEND_ORDER = (2, 3, 4, 0, 1)


def gather_kernel(
    chips,
    sizes,
    w_query,
    w_key,
    w_value,
    w_out,
    w_gate,
    w_up,
    w_down,
    gain_row,
    spread,
    *refs,
):
    piece, hidden_piece, model, kv_width, hidden = sizes
    wholes = refs[:5]
    pieces = refs[5:10]
    stage, keep_sem, ring_send, ring_recv, side_send, side_recv = refs[10:]
    heights = [whole.shape[0] // (2 * chips) for whole in wholes]
    room, wide = pieces[1].shape
    member, core, turn, at, following, sibling = ring_setup(chips)

    def rows(index, owner):
        height = heights[index]
        return wholes[index].at[pl.ds(pl.multiple_of(owner * height, 16), height), :]

    def ring_copy(index, source, owner, step):
        return pltpu.make_async_remote_copy(
            src_ref=source,
            dst_ref=rows(index, owner),
            send_sem=ring_send.at[step, index],
            recv_sem=ring_recv.at[step, index],
            device_id={"dp": following},
            device_id_type=pl.DeviceIdType.MESH,
        )

    def side_copy(index, source, owner, step):
        return pltpu.make_async_remote_copy(
            src_ref=source,
            dst_ref=rows(index, owner),
            send_sem=side_send.at[step, index],
            recv_sem=side_recv.at[step, index],
            device_id={"dp": sibling},
            device_id_type=pl.DeviceIdType.MESH,
        )

    def keep_copy(index):
        return pltpu.make_async_copy(pieces[index], rows(index, member), keep_sem.at[index])

    def build(index):
        if index == 0:
            stage[:room, : pieces[0].shape[1]] = jnp.zeros(pieces[0].shape, jnp.float32)
            rows_from(w_query, stage, piece, model, 0)
            rows_from(w_key, stage, piece, kv_width, model)
            rows_from(w_value, stage, piece, kv_width, model + kv_width)
            pieces[0][...] = stage[:room, : pieces[0].shape[1]].astype(jnp.bfloat16)
        elif index == 1:
            stage[:room, :model] = jnp.zeros((room, model), jnp.float32)
            rows_from(w_out, stage, piece, model, 0)
            spaced = dot(stage[:room, :model].astype(jnp.bfloat16), spread[...])
            line = lax.broadcasted_iota(jnp.int32, (room, wide), 0)
            spaced = spaced + jnp.where(line == piece, gain_row[...], 0.0)
            pieces[1][...] = spaced.astype(jnp.bfloat16)
        elif index == 4:
            rows_from(w_down, stage, hidden_piece, model, 0)
            pieces[4][...] = dot(
                stage[:hidden_piece, :model].astype(jnp.bfloat16), spread[...]
            ).astype(jnp.bfloat16)
        else:
            stage[:room, :hidden] = jnp.zeros((room, hidden), jnp.float32)
            rows_from(w_gate if index == 2 else w_up, stage, piece, hidden, 0)
            pieces[index][...] = stage[:room, :hidden].astype(jnp.bfloat16)

    for index in SEND_ORDER:
        build(index)
        ring_copy(index, pieces[index], member, 0).start()
        side_copy(index, pieces[index], member, 0).start()
        keep_copy(index).start()
    for step in range(1, chips):
        owner = at(-turn * step, core)
        for index in SEND_ORDER:
            ring_copy(index, rows(index, owner), owner, step - 1).wait_recv()
            if step < chips - 1:
                ring_copy(index, rows(index, owner), owner, step).start()
            side_copy(index, rows(index, owner), owner, step).start()
    for index in SEND_ORDER:
        keep_copy(index).wait()
    for step in range(chips):
        owner = at(-turn * step, core)
        theirs = at(turn * step, 1 - core)
        for index in SEND_ORDER:
            if step < chips - 1:
                ring_copy(index, rows(index, owner), owner, step).wait_send()
            side_copy(index, rows(index, owner), owner, step).wait_send()
            side_copy(index, rows(index, theirs), theirs, step).wait_recv()


def gather_all(operands, sizes, members, shapes):
    chips = members // 2
    piece, hidden_piece, model, kv_width, hidden = sizes
    vmem = pl.BlockSpec(memory_space=pltpu.VMEM)
    return pl.pallas_call(
        functools.partial(gather_kernel, chips, sizes),
        out_shape=tuple(
            jax.ShapeDtypeStruct((members * height, width), jnp.bfloat16)
            for height, width in shapes
        ),
        in_specs=[vmem] * len(operands),
        out_specs=tuple([pl.BlockSpec(memory_space=pl.ANY)] * 5),
        scratch_shapes=[pltpu.VMEM(shape, jnp.bfloat16) for shape in shapes]
        + [pltpu.VMEM((max(shapes[0][0], hidden_piece), max(hidden, shapes[0][1])), jnp.float32)]
        + [pltpu.SemaphoreType.DMA((5,))]
        + [pltpu.SemaphoreType.DMA((chips, 5))] * 4,
        compiler_params=pltpu.CompilerParams(
            collective_id=0, has_side_effects=True, vmem_limit_bytes=56 * 2**20
        ),
        name="gather_ring",
    )(*operands)


LEFT_OF = (0, 1, 2, 2, 3)


def scatter_kernel(chips, sizes, micro_count, *refs):
    piece = sizes[0]
    fetched = 9
    choices = 2 * micro_count
    sources = [refs[slot * choices : (slot + 1) * choices] for slot in range(fetched)]
    refs = refs[fetched * choices :]
    gain_terms = refs[0]
    totals = refs[1:6]
    loaded, lefts = refs[6:15], refs[15:19]
    owns, outs, sides, rings = refs[19:24], refs[24:29], refs[29:34], refs[34:39]
    load_sem, ring_send, ring_recv, side_send, side_recv = refs[39:]
    rights = loaded[4:]
    heights = [own.shape[1] for own in owns]
    section = lax.axis_index("section")
    member, core, turn, at, following, sibling = ring_setup(chips)

    def load(slot, micro, late):
        rows = sources[slot][0].shape[0]
        return pltpu.make_async_copy(
            sources[slot][late * micro_count + micro],
            loaded[slot].at[pl.ds(micro * rows, rows), :],
            load_sem.at[slot, micro],
        )

    def start_load(slot):
        for micro in range(micro_count):

            @pl.when(section == 0)
            def _():
                load(slot, micro, 0).start()

            @pl.when(section != 0)
            def _():
                load(slot, micro, 1).start()

    def wait_load(slot):
        for micro in range(micro_count):
            load(slot, micro, 0).wait()

    def term(index, owner):
        height = heights[index]
        part = lefts[LEFT_OF[index]][pl.ds(pl.multiple_of(owner * height, 16), height), :]
        value = dot(part, rights[index][...])
        if index == 1:
            line = lax.broadcasted_iota(jnp.int32, value.shape, 0)
            value = value + jnp.where(line == piece, gain_terms[owner], 0.0)
        return value.astype(jnp.bfloat16)

    def side_copy(index, step):
        return pltpu.make_async_remote_copy(
            src_ref=outs[index].at[step % 2],
            dst_ref=sides[index].at[step],
            send_sem=side_send.at[step, index],
            recv_sem=side_recv.at[step, index],
            device_id={"dp": sibling},
            device_id_type=pl.DeviceIdType.MESH,
        )

    def ring_copy(index, step):
        return pltpu.make_async_remote_copy(
            src_ref=owns[index].at[step],
            dst_ref=rings[index].at[step],
            send_sem=ring_send.at[step, index],
            recv_sem=ring_recv.at[step, index],
            device_id={"dp": following},
            device_id_type=pl.DeviceIdType.MESH,
        )

    def prepare(index, step):
        theirs = at(turn * (step + 1), 1 - core)
        mine = at(-turn * (step + 1), core)
        if step > 1:
            side_copy(index, step - 2).wait_send()
        outs[index][step % 2] = term(index, theirs)
        side_copy(index, step).start()
        owns[index][step] = term(index, mine)

    def advance(index, step):
        side_copy(index, step).wait_recv()
        if step > 0:
            ring_copy(index, step - 1).wait_recv()

        def add(block):
            part = pl.ds(pl.multiple_of(block * 16, 16), 16)
            total = owns[index][step, part, :].astype(jnp.float32) + sides[index][
                step, part, :
            ].astype(jnp.float32)
            if step > 0:
                total = total + rings[index][step - 1, part, :].astype(jnp.float32)
            if step < chips - 1:
                owns[index][step, part, :] = total.astype(jnp.bfloat16)
            else:
                totals[index][part, :] = total

        pl.loop(0, heights[index] // 16)(add)
        if step < chips - 1:
            ring_copy(index, step).start()

    ready = []
    for index in SEND_ORDER:
        if LEFT_OF[index] not in ready:
            start_load(LEFT_OF[index])
            ready.append(LEFT_OF[index])
        start_load(4 + index)
    ready = []
    waiting = None
    for index in SEND_ORDER:
        left = LEFT_OF[index]
        if left not in ready:
            wait_load(left)
            lefts[left][...] = loaded[left][...].T
            ready.append(left)
        wait_load(4 + index)
        prepare(index, 0)
        if waiting is not None:
            advance(waiting, 0)
        waiting = index
    advance(waiting, 0)
    for step in range(1, chips):
        for index in SEND_ORDER:
            prepare(index, step)
        for index in SEND_ORDER:
            advance(index, step)
    for step in range(chips):
        for index in SEND_ORDER:
            if step >= chips - 2:
                side_copy(index, step).wait_send()
            if step < chips - 1:
                ring_copy(index, step).wait_send()


def scatter_all(sources, gain_terms, sizes, members):
    chips = members // 2
    micro_count = len(sources[0]) // 2
    wholes = [(micro_count * group[0].shape[0], group[0].shape[1]) for group in sources]
    shapes = [
        (wholes[LEFT_OF[index]][1] // members, wholes[4 + index][1]) for index in range(5)
    ]
    stacks = lambda depth: [pltpu.VMEM((depth, *shape), jnp.bfloat16) for shape in shapes]
    vmem = pl.BlockSpec(memory_space=pltpu.VMEM)
    flat_sources = [member for group in sources for member in group]
    return pl.pallas_call(
        functools.partial(scatter_kernel, chips, sizes, micro_count),
        out_shape=tuple(jax.ShapeDtypeStruct(shape, jnp.float32) for shape in shapes),
        in_specs=[pl.BlockSpec(memory_space=pl.ANY)] * len(flat_sources) + [vmem],
        out_specs=tuple([vmem] * 5),
        scratch_shapes=[pltpu.VMEM(whole, jnp.bfloat16) for whole in wholes]
        + [pltpu.VMEM(whole[::-1], jnp.bfloat16) for whole in wholes[:4]]
        + stacks(chips)
        + stacks(2)
        + stacks(chips)
        + stacks(chips - 1)
        + [pltpu.SemaphoreType.DMA((9, micro_count))]
        + [pltpu.SemaphoreType.DMA((chips, 5))] * 4,
        compiler_params=pltpu.CompilerParams(
            collective_id=1, has_side_effects=True, vmem_limit_bytes=60 * 2**20
        ),
        name="scatter_ring",
    )(*flat_sources, gain_terms)


def dot(left, right):
    return jnp.dot(left, right, preferred_element_type=jnp.float32)


def dot_nt(left, right):
    return lax.dot_general(
        left, right, (((1,), (1,)), ((), ())), preferred_element_type=jnp.float32
    )


def dot_tn(left, right):
    return lax.dot_general(
        left, right, (((0,), (0,)), ((), ())), preferred_element_type=jnp.float32
    )


def turn_heads(values, tables, sign):
    cos_table, early_sine, late_sine = tables
    half = HEAD // 2
    span = cos_table.shape[1]
    turned = []
    for start in range(0, values.shape[1], span):
        part = values[:, start : start + span]
        turned.append(
            part * cos_table[...]
            + sign
            * (
                pltpu.roll(part, span - half, 1) * early_sine[...]
                + pltpu.roll(part, half, 1) * late_sine[...]
            )
        )
    return jnp.concatenate(turned, axis=1)


def head_rows(source, micro, rows, first, group):
    return jnp.concatenate(
        [
            source[micro * rows : (micro + 1) * rows, (first + g) * HEAD : (first + g + 1) * HEAD]
            for g in range(group)
        ],
        axis=0,
    )


def forward_kernel(
    model,
    layout,
    stream,
    gains,
    bias,
    cos_table,
    early_sine,
    late_sine,
    spread,
    w_qkv,
    w_out,
    w_gate,
    w_up,
    w_down,
    layer_out,
    layer_low,
    normed,
    turned,
    values,
    mixed_wide,
    middle,
    normed_two,
    gate_pre,
    up_pre,
    activation,
    mixed,
):
    heads, kv_heads, micro_count, rows = layout
    group = heads // kv_heads

    @pl.when(pl.program_id(0) == 0)
    def _():
        residual = stream[...].astype(jnp.float32)
        scale = lax.rsqrt(jnp.sum(residual * residual, axis=1, keepdims=True) / model + EPSILON)
        normed[...] = (residual * scale * gains[0:1, :]).astype(jnp.bfloat16)
        products = dot(normed[...], w_qkv[...])
        split = (heads + kv_heads) * HEAD
        turned[...] = turn_heads(
            products[:, :split], (cos_table, early_sine, late_sine), 1.0
        ).astype(jnp.bfloat16)
        values[...] = products[:, split:].astype(jnp.bfloat16)
        for micro in range(micro_count):
            part = slice(micro * rows, (micro + 1) * rows)
            for kv in range(kv_heads):
                query = head_rows(turned, micro, rows, kv * group, group)
                key = turned[part, (heads + kv) * HEAD : (heads + kv + 1) * HEAD]
                value = values[part, kv * HEAD : (kv + 1) * HEAD]
                scores = dot_nt(query, key) * HEAD ** (-0.5)
                scores = scores + jnp.concatenate([bias[micro]] * group, axis=0)
                exponent = jnp.exp(scores - jnp.max(scores, axis=1, keepdims=True))
                total = jnp.sum(exponent, axis=1, keepdims=True)
                probability = (exponent / total).astype(jnp.bfloat16)
                attended = dot(probability, value).astype(jnp.bfloat16)
                for g in range(group):
                    head = kv * group + g
                    mixed[part, head * HEAD : (head + 1) * HEAD] = attended[
                        g * rows : (g + 1) * rows, :
                    ]
        mixed_wide[...] = dot(mixed[...], spread[...]).astype(jnp.bfloat16)
        halfway = residual + dot(mixed_wide[...], w_out[...])
        middle[...] = halfway
        scale_two = lax.rsqrt(jnp.sum(halfway * halfway, axis=1, keepdims=True) / model + EPSILON)
        normed_two[...] = (halfway * scale_two * gains[1:2, :]).astype(jnp.bfloat16)
        layer_out[...] = halfway

    gate = dot(normed_two[...], w_gate[...])
    up = dot(normed_two[...], w_up[...])
    gate_pre[...] = gate
    up_pre[...] = up
    active = (gate * jax.nn.sigmoid(gate) * up).astype(jnp.bfloat16)
    activation[...] = active
    layer_out[...] += dot(active, w_down[...])

    @pl.when(pl.program_id(0) == pl.num_programs(0) - 1)
    def _():
        layer_low[...] = layer_out[...].astype(jnp.bfloat16)


def full(array):
    return pl.BlockSpec(array.shape, lambda i: (0,) * len(array.shape))


def shape_of(rows, width, dtype):
    return jax.ShapeDtypeStruct((rows, width), dtype)


def tile_width(hidden):
    for width in (512, 256, 128):
        if hidden % width == 0:
            return width
    return hidden


def forward_fast(model, layout, stream, gains, bias, tables, spread, matrices):
    w_qkv, w_out, w_gate, w_up, w_down = matrices
    heads, kv_heads, micro_count, rows = layout
    tokens, wide = stream.shape
    hidden = w_gate.shape[1]
    tile = tile_width(hidden)
    split = (heads + kv_heads) * HEAD
    low, high = jnp.bfloat16, jnp.float32
    out_shape = (
        shape_of(tokens, wide, high),
        shape_of(tokens, wide, low),
        shape_of(tokens, wide, low),
        shape_of(tokens, split, low),
        shape_of(tokens, w_qkv.shape[1] - split, low),
        shape_of(tokens, wide, low),
        shape_of(tokens, wide, high),
        shape_of(tokens, wide, low),
        shape_of(tokens, hidden, high),
        shape_of(tokens, hidden, high),
        shape_of(tokens, hidden, low),
    )
    columns = lambda height: pl.BlockSpec((height, tile), lambda i: (0, i))
    ins = (stream, gains, bias, *tables, spread, w_qkv, w_out)
    return pl.pallas_call(
        functools.partial(forward_kernel, model, layout),
        grid=(hidden // tile,),
        out_shape=out_shape,
        in_specs=[full(member) for member in ins]
        + [columns(wide), columns(wide), pl.BlockSpec((tile, wide), lambda i: (i, 0))],
        out_specs=tuple([full(member) for member in out_shape[:8]] + [columns(tokens)] * 3),
        scratch_shapes=[pltpu.VMEM((tokens, heads * HEAD), low)],
        compiler_params=pltpu.CompilerParams(vmem_limit_bytes=56 * 2**20),
        cost_estimate=pl.CostEstimate(
            flops=20 * 2**28, bytes_accessed=30 * 2**20, transcendentals=2**20
        ),
        name="forward_layer",
    )(*ins, w_gate, w_up, w_down)


def backward_kernel(
    model,
    layout,
    cotangent,
    stream,
    gains,
    bias,
    cos_table,
    early_sine,
    late_sine,
    spread,
    turned,
    values,
    middle,
    w_qkv,
    w_out,
    gate_pre,
    up_pre,
    w_gate,
    w_up,
    w_down,
    grad_input,
    input_low,
    grad_gains,
    grad_branch,
    grad_qkv,
    grad_gate,
    grad_up,
    norm_grad,
    grad_mixed,
    grad_turned,
    grad_values,
):
    heads, kv_heads, micro_count, rows = layout
    group = heads // kv_heads
    step = pl.program_id(0)

    @pl.when(step == 0)
    def _():
        norm_grad[...] = jnp.zeros_like(norm_grad)

    gate = gate_pre[...]
    grad_act = dot_nt(cotangent[...], w_down[...])
    sigmoid = jax.nn.sigmoid(gate)
    grad_gate[...] = (
        grad_act * up_pre[...] * sigmoid * (1.0 + gate * (1.0 - sigmoid))
    ).astype(jnp.bfloat16)
    grad_up[...] = (grad_act * gate * sigmoid).astype(jnp.bfloat16)
    norm_grad[...] += dot_nt(grad_gate[...], w_gate[...]) + dot_nt(grad_up[...], w_up[...])

    @pl.when(step == pl.num_programs(0) - 1)
    def _():
        halfway = middle[...]
        scale_two = lax.rsqrt(jnp.sum(halfway * halfway, axis=1, keepdims=True) / model + EPSILON)
        centered = halfway * scale_two
        gradient = norm_grad[...]
        grad_gains[1:2, :] = jnp.sum(gradient * centered, axis=0, keepdims=True)
        scaled = gradient * gains[1:2, :]
        grad_middle = cotangent[...].astype(jnp.float32) + scale_two * (
            scaled - centered * (jnp.sum(scaled * centered, axis=1, keepdims=True) / model)
        )
        grad_input[...] = grad_middle
        grad_branch[...] = grad_middle.astype(jnp.bfloat16)
        grad_wide = dot_nt(grad_branch[...], w_out[...]).astype(jnp.bfloat16)
        grad_mixed[...] = dot_nt(grad_wide, spread[...]).astype(jnp.bfloat16)
        grad_values[...] = jnp.zeros_like(grad_values)
        for micro in range(micro_count):
            part = slice(micro * rows, (micro + 1) * rows)
            for kv in range(kv_heads):
                query = head_rows(turned, micro, rows, kv * group, group)
                key = turned[part, (heads + kv) * HEAD : (heads + kv + 1) * HEAD]
                value = values[part, kv * HEAD : (kv + 1) * HEAD]
                grad_head = head_rows(grad_mixed, micro, rows, kv * group, group)
                scores = dot_nt(query, key) * HEAD ** (-0.5)
                scores = scores + jnp.concatenate([bias[micro]] * group, axis=0)
                exponent = jnp.exp(scores - jnp.max(scores, axis=1, keepdims=True))
                total = jnp.sum(exponent, axis=1, keepdims=True)
                probability = exponent / total
                grad_value = dot_tn(probability.astype(jnp.bfloat16), grad_head)
                grad_prob = dot_nt(grad_head, value)
                inner = jnp.sum(probability * grad_prob, axis=1, keepdims=True)
                grad_scores = (probability * (grad_prob - inner)).astype(jnp.bfloat16)
                grad_query = dot(grad_scores, key) * HEAD ** (-0.5)
                grad_key = dot_tn(grad_scores, query) * HEAD ** (-0.5)
                for g in range(group):
                    head = kv * group + g
                    grad_turned[part, head * HEAD : (head + 1) * HEAD] = grad_query[
                        g * rows : (g + 1) * rows, :
                    ]
                grad_turned[part, (heads + kv) * HEAD : (heads + kv + 1) * HEAD] = grad_key
                grad_values[part, kv * HEAD : (kv + 1) * HEAD] = grad_value
        split = (heads + kv_heads) * HEAD
        grad_qkv[:, :split] = turn_heads(
            grad_turned[...], (cos_table, early_sine, late_sine), -1.0
        ).astype(jnp.bfloat16)
        grad_qkv[:, split:] = grad_values[...].astype(jnp.bfloat16)
        first_gradient = dot_nt(grad_qkv[...], w_qkv[...])
        residual = stream[...].astype(jnp.float32)
        scale = lax.rsqrt(jnp.sum(residual * residual, axis=1, keepdims=True) / model + EPSILON)
        first_centered = residual * scale
        grad_gains[0:1, :] = jnp.sum(first_gradient * first_centered, axis=0, keepdims=True)
        first_scaled = first_gradient * gains[0:1, :]
        grad_input[...] += scale * (
            first_scaled
            - first_centered
            * (jnp.sum(first_scaled * first_centered, axis=1, keepdims=True) / model)
        )
        input_low[...] = grad_input[...].astype(jnp.bfloat16)


def backward_fast(model, layout, cotangent, kept, gains, bias, tables, spread, matrices):
    w_qkv, w_out, w_gate, w_up, w_down = matrices
    stream, _, _, turned, values, _, middle, _, gate_pre, up_pre, _ = kept
    heads, kv_heads, micro_count, rows = layout
    tokens, wide = stream.shape
    hidden = w_gate.shape[1]
    tile = tile_width(hidden)
    split = (heads + kv_heads) * HEAD
    low, high = jnp.bfloat16, jnp.float32
    out_shape = (
        shape_of(tokens, wide, high),
        shape_of(tokens, wide, low),
        shape_of(2, wide, high),
        shape_of(tokens, wide, low),
        shape_of(tokens, w_qkv.shape[1], low),
        shape_of(tokens, hidden, low),
        shape_of(tokens, hidden, low),
    )
    columns = lambda height: pl.BlockSpec((height, tile), lambda i: (0, i))
    ins = (cotangent, stream, gains, bias, *tables, spread, turned, values, middle, w_qkv, w_out)
    return pl.pallas_call(
        functools.partial(backward_kernel, model, layout),
        grid=(hidden // tile,),
        out_shape=out_shape,
        in_specs=[full(member) for member in ins]
        + [columns(tokens)] * 2
        + [columns(wide), columns(wide), pl.BlockSpec((tile, wide), lambda i: (i, 0))],
        out_specs=tuple([full(member) for member in out_shape[:5]] + [columns(tokens)] * 2),
        scratch_shapes=[
            pltpu.VMEM((tokens, wide), high),
            pltpu.VMEM((tokens, heads * HEAD), low),
            pltpu.VMEM((tokens, split), high),
            pltpu.VMEM((tokens, w_qkv.shape[1] - split), high),
        ],
        compiler_params=pltpu.CompilerParams(vmem_limit_bytes=56 * 2**20),
        cost_estimate=pl.CostEstimate(
            flops=24 * 2**28, bytes_accessed=36 * 2**20, transcendentals=2**20
        ),
        name="backward_layer",
    )(*ins, gate_pre, up_pre, w_gate, w_up, w_down)


def widen(array, members, room):
    width = array.shape[-1] // members
    cut = array.reshape(array.shape[:-1] + (members, width))
    cut = jnp.pad(cut, [(0, 0)] * (cut.ndim - 1) + [(0, room - width)])
    return cut.reshape(array.shape[:-1] + (members * room,))


def narrow(array, members, width):
    room = array.shape[-1] // members
    cut = array.reshape(array.shape[:-1] + (members, room))[..., :width]
    return cut.reshape(array.shape[:-1] + (members * width,))


def lifted(array, height, width):
    return jnp.pad(array, [(0, height - array.shape[0]), (0, width - array.shape[1])])


def rows_room(model, members):
    return -(-(model // members + 1) // 16) * 16


def on_device_fast(boundary, doc_lens, w_query, w_key, w_value, w_out, gains, w_gate, w_up, w_down):
    section = lax.axis_index("section")
    members = lax.axis_size("dp")
    _, micro_count, rows, model = boundary.shape
    tokens = micro_count * rows
    piece = model // members
    room = rows_room(model, members)
    wide = room * members
    kv_width = w_key.size // piece
    hidden = w_gate.size // piece
    heads, kv_heads = model // HEAD, kv_width // HEAD
    layout = (heads, kv_heads, micro_count, rows)
    split = model + kv_width
    qkv_wide = split + -(-kv_width // 128) * 128
    hidden_piece = hidden // members
    gain_piece = gains.size

    feature = jnp.arange(model, dtype=jnp.int32)
    spread = (
        (feature // piece * room + feature % piece)[:, None]
        == jnp.arange(wide, dtype=jnp.int32)[None, :]
    ).astype(jnp.bfloat16)

    def spread_out(array):
        return jnp.dot(array, spread, preferred_element_type=jnp.float32).astype(array.dtype)

    sizes = (piece, hidden_piece, model, kv_width, hidden)
    gain_row = lifted(gains, 1, wide).astype(jnp.float32)
    gathered = gather_all(
        (w_query, w_key, w_value, w_out, w_gate, w_up, w_down, gain_row, spread),
        sizes,
        members,
        ((room, qkv_wide), (room, wide), (room, hidden), (room, hidden), (hidden_piece, wide)),
    )
    gain_rows = gathered[1].reshape(members, room, wide)[:, piece, :gain_piece]
    gain_pair = widen(gain_rows.reshape(2, model), members, room).astype(jnp.float32)

    layouts = [doc_layout(doc_lens[micro, 0], rows) for micro in range(micro_count)]
    segments = jnp.stack([item[0] for item in layouts])
    positions = jnp.concatenate([item[1] for item in layouts])
    live = jnp.concatenate([item[2] for item in layouts]).astype(jnp.float32)
    slot_ids = jnp.arange(rows, dtype=jnp.int32)
    allowed = (slot_ids[None, :] <= slot_ids[:, None])[None] & (
        segments[:, :, None] == segments[:, None, :]
    )
    bias = jnp.where(allowed, 0.0, -1e30).astype(jnp.float32)
    cos_table, sine_table = rope_tables(positions)
    first_half = (jnp.arange(HEAD, dtype=jnp.int32) < HEAD // 2)[None, :]
    tables = tuple(
        jnp.tile(table, (1, 128 // HEAD))
        for table in (
            cos_table,
            jnp.where(first_half, -sine_table, 0.0),
            jnp.where(first_half, 0.0, sine_table),
        )
    )

    own = spread_out(boundary.reshape(tokens, model))
    dimmed = jnp.where(section == 1, own * live[:, None].astype(jnp.bfloat16), 0.0)
    shared = (gain_pair, bias, tables, spread, gathered)
    kept_zero = forward_fast(model, layout, own, *shared)
    stream_one = passed_along(kept_zero[1], "section", 1)
    kept_one = forward_fast(model, layout, stream_one, *shared)
    start_one = dimmed.astype(jnp.bfloat16)
    back_one = backward_fast(model, layout, start_one, (stream_one, *kept_one[1:]), *shared)
    start_zero = passed_along(back_one[1], "section", -1)
    back_zero = backward_fast(model, layout, start_zero, (own, *kept_zero[1:]), *shared)

    pick = lambda early, late: jnp.where(section == 0, early, late)
    results = narrow(pick(back_zero[0], kept_one[0]), members, piece)
    sources = (
        [(kept_zero[at], kept_one[at]) for at in (2, 5, 7, 10)]
        + [(back_zero[at], back_one[at]) for at in (4, 3, 5, 6)]
        + [(start_zero, start_one)]
    )
    gain_terms = narrow(pick(back_zero[2], back_one[2]), members, piece)
    gain_terms = gain_terms.reshape(members, 1, gain_piece)
    gain_terms = jnp.pad(gain_terms, ((0, 0), (0, 0), (0, wide - gain_piece)))
    share_qkv, share_out, share_gate, share_up, share_down = scatter_all(
        sources, gain_terms, sizes, members
    )
    flat = lambda array: array.reshape(1, -1)
    return (
        results.reshape(1, micro_count, rows, model),
        flat(share_qkv[:piece, :model]),
        flat(share_qkv[:piece, model:split]),
        flat(share_qkv[:piece, split : split + kv_width]),
        flat(narrow(share_out[:piece], members, piece)),
        flat(share_out[piece : piece + 1, :gain_piece]),
        flat(share_gate[:piece]),
        flat(share_up[:piece]),
        flat(narrow(share_down, members, piece)),
    )


def rows_fit(mesh, model, hidden):
    members = mesh.shape["dp"]
    return (
        mesh.shape["section"] == 2
        and members >= 6
        and members % 4 == 0
        and model % members == 0
        and hidden % members == 0
        and (hidden // members) % 16 == 0
        and hidden % 128 == 0
        and model % 64 == 0
        and (model // members) % 2 == 0
        and (rows_room(model, members) * members) % 128 == 0
    )


def solution(mesh):
    placed = (
        P("section", None, "dp", None),
        P(None, "dp", None),
        P("section", "dp"),
        P("section", "dp"),
        P("section", "dp"),
        P("section", "dp"),
        P("section", "dp"),
        P("section", "dp"),
        P("section", "dp"),
        P("section", "dp"),
    )

    def chosen(*operands):
        model = operands[0].shape[3]
        hidden = operands[7].size * mesh.shape["dp"] // model
        return (on_device_fast if rows_fit(mesh, model, hidden) else on_device)(*operands)

    return jax.shard_map(
        chosen,
        mesh=mesh,
        in_specs=placed,
        out_specs=(
            P("section", None, "dp", None),
            P("section", "dp"),
            P("section", "dp"),
            P("section", "dp"),
            P("section", "dp"),
            P("section", "dp"),
            P("section", "dp"),
            P("section", "dp"),
            P("section", "dp"),
        ),
        check_vma=False,
    )
```
